512 devices in a mesh: gx: 32 (over z, core), gy: 16 (over y, x).
Axes of the slice: x: 4, y: 4, z: 16, core: 2. Of those that a mesh axis runs over, the one named last changes fastest.
Arguments:
- nodes: bfloat16 [524288, 128], P(('gx', 'gy')), may hold values from -6 to 6
- edge_feat: bfloat16 [2097152, 128], P(('gx', 'gy')), may hold values from -6 to 6
- senders: int32 [2097152], P(('gx', 'gy')), may hold values from 0 to 1535
- receivers: int32 [2097152], P(('gx', 'gy')), may hold values from 0 to 1023
- send_lists: int32 [512, 4, 128], P(('gx', 'gy')), may hold values from 0 to 1023
- owner: int32 [524288], P(('gx', 'gy')), may hold values from 0 to 1023
- edge_live: int32 [512], P(('gx', 'gy')), may hold values from 1 to 4096, 1310720 in all
- cotangent: bfloat16 [524288, 128], P(('gx', 'gy')), may hold values from -6 to 6
- w_edge: bfloat16 [4, 128, 128], replicated, may hold values from -0.5 to 0.5
- w_node: bfloat16 [3, 128, 128], replicated, may hold values from -0.5 to 0.5
- w_coarse: bfloat16 [2, 128, 128], replicated, may hold values from -0.5 to 0.5
- biases: float32 [3, 128], replicated, may hold values from -3 to 3
Outputs:
- node_out: bfloat16 [524288, 128], P(('gx', 'gy'))
- d_nodes: bfloat16 [524288, 128], P(('gx', 'gy'))
- d_edges: bfloat16 [2097152, 128], P(('gx', 'gy'))
- weight_grads: float32 [9, 128, 128], replicated
- bias_grads: float32 [3, 128], replicated
The draws below stay inside these ranges and needn't reach their ends.
Inputs may be any that keep to these rules, and one draw needn't show every extreme that they name: `senders`: a row of the partition's own 1024 cells or of its 512 halo rows. `receivers`: a cell of the partition. `send_lists`: cells of the sending partition. `owner`: a coarse cell of the cell's grid row. `edge_live`: some partition has all 4096 slots live.
All inputs are finite; a program needn't handle non-finite values. No bound on the sum of `edge_live` on one device may be relied on, other than what follows from the above.
Results may differ from the reference program's by a relative error of at most 0.014.
Values may be sent and summed in bfloat16 or wider, within the bound.
A program may use at most 64 MiB of HBM per device.

```python
import math
import jax
import jax.numpy as jnp
import numpy as np
from jax import lax

WIDTH = 128
CELL_DEV = 1024
EDGE_DEV = 4096
HALO_ROWS = 128
COARSE_ROW = 1024
CELLS = 524288
EDGES = 2097152
N_GX = 32
N_GY = 16
DEVICES = 512


def plant(array, rng, smallest, largest):
    dims = array.shape
    place = [jax.random.randint(jax.random.fold_in(rng, axis), (), 0, dims[axis]) for axis in range(len(dims))]
    array = array.at[tuple(place)].set(smallest)
    longest = dims.index(max(dims))
    place[longest] = (place[longest] + 1) % dims[longest]
    return array.at[tuple(place)].set(largest)


def shard_levels(stream_key, extent, split, least, largest):
    level, own = 1.0, jax.random.fold_in(stream_key, 6)
    for axis_at, parts in split:
        steps = jnp.exp(jax.random.uniform(jax.random.fold_in(own, axis_at), (parts,), jnp.float32, least / len(split), largest / len(split)))
        level = level * jnp.repeat(steps, extent[axis_at] // parts).reshape([-1 if axis == axis_at else 1 for axis in range(len(extent))])
    return level


def length_profile(amount, total, most, slope):
    portions = [(1 << 20) // math.isqrt(grade ** slope) + 1 for grade in range(2, amount + 1)]
    surplus, given = total - most - (amount - 1), [1] * (amount - 1)
    while surplus > 0:
        candidates = [i for i in range(amount - 1) if given[i] < most]
        whole, left = sum([portions[i] for i in candidates]), surplus
        for i in candidates:
            more = min(most - given[i], max(1, left * portions[i] // whole), surplus)
            given[i] = given[i] + more
            surplus = surplus - more
    return np.array([most] + given)


def uneven(own_key, amount, total, reach, slope):
    if amount == 2:
        one = jax.random.randint(own_key, (), max(1, total - reach), min(reach, total - 1) + 1)
        return jnp.stack([one, total - one])
    tallies = jnp.asarray(length_profile(amount, total, reach, slope), jnp.int32)
    twos = (amount - 1) // 2
    source_of, receiver = tallies[1:1 + 2 * twos:2], tallies[2:2 + 2 * twos:2]
    room = jnp.minimum(source_of - 1, reach - receiver)
    shifted = jax.random.randint(jax.random.fold_in(own_key, 1), (twos,), 0, 1 << 20) % (room + 1)
    tallies = tallies.at[1:1 + 2 * twos:2].set(source_of - shifted).at[2:2 + 2 * twos:2].set(receiver + shifted)
    return tallies[jax.random.permutation(jax.random.fold_in(own_key, 2), amount)]


def bell_draw(own_key, shape, spread, limit, pieces=(), kind=jnp.bfloat16):
    drawn = jax.random.normal(own_key, shape, jnp.float32) * spread
    if len(pieces) > 0:
        drawn = shard_levels(own_key, shape, pieces, -0.22, 0.18) * drawn
    return jnp.clip(drawn, min=-limit, max=limit).astype(kind)


def setup_inputs(seed: int = 0) -> dict:
    arg_keys = jax.random.split(jax.random.key(seed), 13)
    nodes = bell_draw(arg_keys[0], (CELLS, WIDTH), 1.0, 6.0, ((0, 512),))
    edge_feat = bell_draw(arg_keys[1], (EDGES, WIDTH), 1.0, 6.0, ((0, 512),))
    senders = plant(jax.random.randint(arg_keys[2], (EDGES,), 0, CELL_DEV + 4 * HALO_ROWS), jax.random.fold_in(arg_keys[2], 1), 0, (CELL_DEV + 4 * HALO_ROWS) - 1).astype(jnp.int32)
    receivers = plant(jax.random.randint(arg_keys[3], (EDGES,), 0, CELL_DEV), jax.random.fold_in(arg_keys[3], 1), 0, CELL_DEV - 1).astype(jnp.int32)
    send_lists = plant(jax.random.randint(arg_keys[4], (DEVICES, 4, HALO_ROWS), 0, CELL_DEV), jax.random.fold_in(arg_keys[4], 1), 0, CELL_DEV - 1).astype(jnp.int32)
    owner = plant(jax.random.randint(arg_keys[5], (CELLS,), 0, COARSE_ROW), jax.random.fold_in(arg_keys[5], 1), 0, COARSE_ROW - 1).astype(jnp.int32)
    edge_live = uneven(arg_keys[6], DEVICES, DEVICES * EDGE_DEV * 5 // 8, EDGE_DEV, 2).astype(jnp.int32)
    cotangent = bell_draw(arg_keys[7], (CELLS, WIDTH), 1.0, 6.0, ((0, 512),))
    w_edge = bell_draw(arg_keys[8], (4, WIDTH, WIDTH), WIDTH ** -0.5, 0.5)
    w_node = bell_draw(arg_keys[9], (3, WIDTH, WIDTH), WIDTH ** -0.5, 0.5)
    w_coarse = bell_draw(arg_keys[10], (2, WIDTH, WIDTH), WIDTH ** -0.5, 0.5)
    biases = bell_draw(arg_keys[11], (3, WIDTH), 0.5, 3.0, (), jnp.float32)
    return dict(nodes=nodes, edge_feat=edge_feat, senders=senders, receivers=receivers, send_lists=send_lists, owner=owner, edge_live=edge_live, cotangent=cotangent, w_edge=w_edge, w_node=w_node, w_coarse=w_coarse, biases=biases)


def matmul(left, right):
    return jnp.dot(left, right, preferred_element_type=jnp.float32)


def left_t(left, right):
    return lax.dot_general(left, right, (((0,), (0,)), ((), ())), preferred_element_type=jnp.float32)


def right_t(left, right):
    return lax.dot_general(left, right, (((1,), (1,)), ((), ())), preferred_element_type=jnp.float32)


def silu_slope(value):
    sigma = jax.nn.sigmoid(value)
    return sigma * (1.0 + value * (1.0 - sigma))


def edge_front(extended, edge_feat, senders, receivers, live, w_edge, biases):
    send_rows = extended[senders]
    recv_rows = extended[receivers]
    pre_edge = matmul(send_rows, w_edge[0]) + matmul(recv_rows, w_edge[1]) + matmul(edge_feat, w_edge[2]) + biases[0]
    edge_hidden = jax.nn.silu(pre_edge).astype(jnp.bfloat16)
    message = matmul(edge_hidden, w_edge[3]) * live[:, None]
    return send_rows, recv_rows, pre_edge, edge_hidden, message


def node_front(nodes, message, receivers, w_node, biases):
    aggregated = jax.ops.segment_sum(message, receivers, num_segments=nodes.shape[0])
    agg_bf = aggregated.astype(jnp.bfloat16)
    pre_node = matmul(nodes, w_node[0]) + matmul(agg_bf, w_node[1]) + biases[1]
    node_hidden = jax.nn.silu(pre_node).astype(jnp.bfloat16)
    fine_state = nodes.astype(jnp.float32) + matmul(node_hidden, w_node[2])
    return agg_bf, pre_node, node_hidden, fine_state


def coarse_front(coarse_in, w_coarse, biases):
    coarse_bf = coarse_in.astype(jnp.bfloat16)
    pre_coarse = matmul(coarse_bf, w_coarse[0]) + biases[2]
    coarse_hidden = jax.nn.silu(pre_coarse).astype(jnp.bfloat16)
    coarse_out = matmul(coarse_hidden, w_coarse[1]).astype(jnp.bfloat16)
    return coarse_bf, pre_coarse, coarse_hidden, coarse_out


def coarse_back(pre_coarse, d_coarse_out, w_coarse):
    d_pre = right_t(d_coarse_out.astype(jnp.bfloat16), w_coarse[1]) * silu_slope(pre_coarse)
    d_coarse_in = right_t(d_pre.astype(jnp.bfloat16), w_coarse[0]).astype(jnp.bfloat16)
    return d_pre, d_coarse_in


def coarse_grads(coarse_bf, coarse_hidden, d_coarse_out, d_pre):
    first = left_t(coarse_bf, d_pre.astype(jnp.bfloat16))
    second = left_t(coarse_hidden, d_coarse_out.astype(jnp.bfloat16))
    return jnp.stack([first, second]), jnp.sum(d_pre, axis=0)


def node_back(nodes, agg_bf, pre_node, node_hidden, d_fine, w_node):
    d_fine_bf = d_fine.astype(jnp.bfloat16)
    d_pre = right_t(d_fine_bf, w_node[2]) * silu_slope(pre_node)
    d_pre_bf = d_pre.astype(jnp.bfloat16)
    d_part = d_fine + right_t(d_pre_bf, w_node[0])
    d_agg = right_t(d_pre_bf, w_node[1])
    grads = jnp.stack([left_t(nodes, d_pre_bf), left_t(agg_bf, d_pre_bf), left_t(node_hidden, d_fine_bf)])
    return d_part, d_agg, grads, jnp.sum(d_pre, axis=0)


def edge_back(send_rows, recv_rows, pre_edge, edge_hidden, edge_feat, senders, receivers, live, d_agg, w_edge, ext_count):
    d_message = (d_agg[receivers] * live[:, None]).astype(jnp.bfloat16)
    d_pre = right_t(d_message, w_edge[3]) * silu_slope(pre_edge)
    d_pre_bf = d_pre.astype(jnp.bfloat16)
    d_edges = right_t(d_pre_bf, w_edge[2]).astype(jnp.bfloat16)
    d_ext = jax.ops.segment_sum(right_t(d_pre_bf, w_edge[0]), senders, num_segments=ext_count)
    d_ext = d_ext + jax.ops.segment_sum(right_t(d_pre_bf, w_edge[1]), receivers, num_segments=ext_count)
    grads = jnp.stack([left_t(send_rows, d_pre_bf), left_t(recv_rows, d_pre_bf), left_t(edge_feat, d_pre_bf), left_t(edge_hidden, d_message)])
    return d_edges, d_ext, grads, jnp.sum(d_pre, axis=0)


def halo_table(picked):
    blank_row = jnp.zeros_like(picked[:1, :, 0])
    blank_col = jnp.zeros_like(picked[:, :1, 0])
    from_lower = jnp.concatenate([blank_row, picked[:-1, :, 1]], axis=0)
    from_upper = jnp.concatenate([picked[1:, :, 0], blank_row], axis=0)
    from_left = jnp.concatenate([blank_col, picked[:, :-1, 3]], axis=1)
    from_right = jnp.concatenate([picked[:, 1:, 2], blank_col], axis=1)
    return jnp.stack([from_lower, from_upper, from_left, from_right], axis=2)


def reference(nodes, edge_feat, senders, receivers, send_lists, owner, edge_live, cotangent, w_edge, w_node, w_coarse, biases):
    ext_count = CELL_DEV + 4 * HALO_ROWS
    node_dev = nodes.reshape(DEVICES, CELL_DEV, WIDTH)
    picked = jax.vmap(lambda table, rows: table[rows])(node_dev, send_lists)
    picked = picked.reshape(N_GX, N_GY, 4, HALO_ROWS, WIDTH)
    halo = halo_table(picked).reshape(DEVICES, 4 * HALO_ROWS, WIDTH)
    ext_dev = jnp.concatenate([node_dev, halo], axis=1)
    feat_dev = edge_feat.reshape(DEVICES, EDGE_DEV, WIDTH)
    send_dev = senders.reshape(DEVICES, EDGE_DEV)
    recv_dev = receivers.reshape(DEVICES, EDGE_DEV)
    live_dev = (jnp.arange(EDGE_DEV, dtype=jnp.int32)[None, :] < edge_live[:, None]).astype(jnp.float32)

    def forward_device(pack):
        extended, node_part, feat, send_idx, recv_idx, live = pack
        message = edge_front(extended, feat, send_idx, recv_idx, live, w_edge, biases)[4]
        return node_front(node_part, message, recv_idx, w_node, biases)[3]

    fine = lax.map(forward_device, (ext_dev, node_dev, feat_dev, send_dev, recv_dev, live_dev))
    row_of = (jnp.arange(DEVICES, dtype=jnp.int32) // N_GY) * COARSE_ROW
    global_owner = (owner.reshape(DEVICES, CELL_DEV) + row_of[:, None]).astype(jnp.int32)
    flat_owner = global_owner.reshape(-1)
    coarse_in = 0.0625 * jax.ops.segment_sum(fine.reshape(-1, WIDTH), flat_owner, num_segments=N_GX * COARSE_ROW)
    coarse_bf, pre_coarse, coarse_hidden, coarse_out = coarse_front(coarse_in, w_coarse, biases)
    node_out = (fine + coarse_out[global_owner].astype(jnp.float32)).astype(jnp.bfloat16).reshape(CELLS, WIDTH)

    grad_dev = cotangent.astype(jnp.float32).reshape(DEVICES, CELL_DEV, WIDTH)
    d_coarse_out = jax.ops.segment_sum(grad_dev.reshape(-1, WIDTH), flat_owner, num_segments=N_GX * COARSE_ROW)
    d_pre_coarse, d_coarse_in = coarse_back(pre_coarse, d_coarse_out, w_coarse)
    coarse_w, coarse_b = coarse_grads(coarse_bf, coarse_hidden, d_coarse_out, d_pre_coarse)
    d_fine = grad_dev + 0.0625 * d_coarse_in[global_owner].astype(jnp.float32)

    def backward_device(pack):
        extended, node_part, feat, send_idx, recv_idx, live, d_fine_part = pack
        send_rows, recv_rows, pre_edge, edge_hidden, message = edge_front(extended, feat, send_idx, recv_idx, live, w_edge, biases)
        agg_bf, pre_node, node_hidden, fine_state = node_front(node_part, message, recv_idx, w_node, biases)
        d_part, d_agg, node_w, node_b = node_back(node_part, agg_bf, pre_node, node_hidden, d_fine_part, w_node)
        d_edges, d_ext, edge_w, edge_b = edge_back(send_rows, recv_rows, pre_edge, edge_hidden, feat, send_idx, recv_idx, live, d_agg, w_edge, ext_count)
        return d_edges, d_part + d_ext[:CELL_DEV], d_ext[CELL_DEV:], edge_w, node_w, edge_b, node_b

    d_edges, d_part, d_halo, edge_w, node_w, edge_b, node_b = lax.map(backward_device, (ext_dev, node_dev, feat_dev, send_dev, recv_dev, live_dev, d_fine))
    back = halo_table(d_halo.reshape(N_GX, N_GY, 4, HALO_ROWS, WIDTH)).reshape(DEVICES, 4 * HALO_ROWS, WIDTH)
    returned = jax.vmap(lambda values, rows: jax.ops.segment_sum(values, rows, num_segments=CELL_DEV))(back, send_lists.reshape(DEVICES, 4 * HALO_ROWS))
    d_nodes = (d_part + returned).astype(jnp.bfloat16).reshape(CELLS, WIDTH)
    weight_grads = jnp.concatenate([jnp.sum(edge_w, axis=0), jnp.sum(node_w, axis=0), coarse_w], axis=0)
    bias_grads = jnp.stack([jnp.sum(edge_b, axis=0), jnp.sum(node_b, axis=0), coarse_b])
    return node_out, d_nodes, d_edges.reshape(EDGES, WIDTH), weight_grads, bias_grads
```

```python
import functools

import jax
import jax.numpy as jnp
from jax import lax
from jax.experimental import pallas as pl
from jax.experimental.pallas import tpu as pltpu
from jax.sharding import PartitionSpec as P

F32, BF16, I32 = jnp.float32, jnp.bfloat16, jnp.int32
W = 128
BLOCK = 256
MESH = pl.DeviceIdType.MESH


def dot(left, right):
    return jnp.dot(left, right, preferred_element_type=F32)


def right_t(left, right):
    return lax.dot_general(left, right, (((1,), (1,)), ((), ())), preferred_element_type=F32)


def sigmoid(value):
    return 0.5 * jnp.tanh(0.5 * value) + 0.5


def slope(value, sigma):
    return sigma * (1.0 + value * (1.0 - sigma))


def lane_row(ref, first, count):
    return jnp.concatenate([ref[pl.ds(first + q, 1), :] for q in range(count)], axis=1)


def kernel(
    dims,
    nodes,
    feat,
    snd,
    rcv,
    slist,
    owner,
    live,
    cot,
    w_edge,
    w_node,
    w_coarse,
    bias,
    node_out,
    d_nodes,
    d_edges,
    grads,
    bias_grads,
    iota,
    ext_t,
    table_t,
    hot_list,
    own_t,
    own_n,
    pick,
    halo,
    slopes,
    h_acc,
    sr_acc,
    we_acc,
    fine,
    node_slope,
    d_part,
    hb,
    agg,
    hid,
    cot_src,
    cot_in,
    fine_src,
    fine_in,
    coarse_all,
    back_src,
    back_in,
    bias_rows,
    a_src,
    a_in,
    a_mine,
    a_pair,
    a_z,
    a_fin,
    a_all,
    b_flat,
    b_src,
    b_in,
    b_mine,
    b_pair,
    b_z,
    b_fin,
    b_all,
    halo_sem,
    back_sem,
    cot_sem,
    fine_sem,
    coarse_sem,
    a_rs_sem,
    a_pair_sem,
    a_z_sem,
    a_ag_sem,
    b_rs_sem,
    b_pair_sem,
    b_z_sem,
    b_ag_sem,
):
    nx, ny, cells, edges, tile = dims
    nz = nx // 2
    ext = cells + 4 * W
    owned = cells // ny
    i, j = lax.axis_index("gx"), lax.axis_index("gy")
    core, z = lax.rem(i, 2), lax.div(i, 2)
    up, down = lax.rem(i + nx - 1, nx), lax.rem(i + 1, nx)
    left, right = lax.rem(j + ny - 1, ny), lax.rem(j + 1, ny)
    partner = i + 1 - 2 * core

    barrier = pltpu.get_barrier_semaphore()

    def greet(gx, gy):
        pl.semaphore_signal(barrier, inc=1, device_id=(gx, gy), device_id_type=MESH)

    greet(up, j)
    greet(down, j)

    def greet_row(d, c):
        greet(i, lax.rem(j + d, ny))
        return c

    def greet_column(d, c):
        greet(lax.rem(i + 2 * d, nx), j)
        return c

    lax.fori_loop(1, ny, greet_row, 0)
    lax.fori_loop(1, nz, greet_column, 0)

    def row_copy(src, dst, sems, slot, target):
        return pltpu.make_async_remote_copy(
            src_ref=src,
            dst_ref=dst.at[slot],
            send_sem=sems.at[0, target],
            recv_sem=sems.at[1, slot],
            device_id=(i, target),
            device_id_type=MESH,
        )

    def scatter_start(src, dst, sems):
        dst[j] = src[j]

        def step(d, c):
            t = lax.rem(j + d, ny)
            row_copy(src.at[t], dst, sems, j, t).start()
            return c

        lax.fori_loop(1, ny, step, 0)

    def gather_start(buf, sems):
        def step(d, c):
            t = lax.rem(j + d, ny)
            row_copy(buf.at[j], buf, sems, j, t).start()
            return c

        lax.fori_loop(1, ny, step, 0)

    def row_arrive(buf, sems):
        def step(d, c):
            t = lax.rem(j + d, ny)
            row_copy(buf.at[t], buf, sems, t, t).wait_recv()
            return c

        lax.fori_loop(1, ny, step, 0)

    def row_sent(src, dst, sems):
        def step(d, c):
            t = lax.rem(j + d, ny)
            row_copy(src.at[j], dst, sems, j, t).wait_send()
            return c

        lax.fori_loop(1, ny, step, 0)

    def z_copy(buf, sems, slot, target):
        return pltpu.make_async_remote_copy(
            src_ref=buf.at[slot],
            dst_ref=buf.at[slot],
            send_sem=sems.at[0, target],
            recv_sem=sems.at[1, slot],
            device_id=(2 * target + core, j),
            device_id_type=MESH,
        )

    def z_each(action):
        def step(d, c):
            action(lax.rem(z + d, nz))
            return c

        lax.fori_loop(1, nz, step, 0)

    def pair_copy(src, dst, sems, which):
        return pltpu.make_async_remote_copy(
            src_ref=src,
            dst_ref=dst,
            send_sem=sems.at[0, which],
            recv_sem=sems.at[1, which],
            device_id=(partner, j),
            device_id_type=MESH,
        )

    def slots_sum(ref):
        def step(k, total):
            return total + ref[k].astype(F32)

        return lax.fori_loop(1, ref.shape[0], step, ref[0].astype(F32))

    def reduce_stages(src, into, mine, pair, zbuf, fin, everything, sems):
        rs_sem, pair_sem, z_sem, ag_sem = sems
        half = mine.shape[0] // 2
        here = pl.ds(pl.multiple_of(core * half, 8), half)
        there = pl.ds(pl.multiple_of((1 - core) * half, 8), half)
        first = pair_copy(mine.at[there], pair, pair_sem, 0)
        second = pair_copy(fin.at[here], fin.at[here], pair_sem, 1)
        second_in = pair_copy(fin.at[there], fin.at[there], pair_sem, 1)

        def start():
            scatter_start(src, into, rs_sem)

        def to_pair():
            row_arrive(into, rs_sem)
            mine[...] = slots_sum(into)
            first.start()

        def to_column():
            first.wait_recv()
            zbuf[z] = mine[here, :] + pair[...]
            z_each(lambda t: z_copy(zbuf, z_sem, z, t).start())

        def from_column():
            z_each(lambda t: z_copy(zbuf, z_sem, t, t).wait_recv())
            fin[here, :] = slots_sum(zbuf)
            second.start()

        def to_row():
            second_in.wait_recv()
            everything[j] = fin[...]
            gather_start(everything, ag_sem)

        def finish():
            row_arrive(everything, ag_sem)
            row_sent(src, into, rs_sem)
            first.wait_send()
            second.wait_send()
            z_each(lambda t: z_copy(zbuf, z_sem, z, t).wait_send())
            row_sent(everything, everything, ag_sem)

        return start, to_pair, to_column, from_column, to_row, finish

    a_stage = reduce_stages(
        a_src, a_in, a_mine, a_pair, a_z, a_fin, a_all, (a_rs_sem, a_pair_sem, a_z_sem, a_ag_sem)
    )
    b_stage = reduce_stages(
        b_src, b_in, b_mine, b_pair, b_z, b_fin, b_all, (b_rs_sem, b_pair_sem, b_z_sem, b_ag_sem)
    )

    def halo_copies(src, dst, sems):
        targets = ((up, j), (down, j), (i, left), (i, right))
        return [
            pltpu.make_async_remote_copy(
                src_ref=src.at[k],
                dst_ref=dst.at[k ^ 1],
                send_sem=sems.at[0, k],
                recv_sem=sems.at[1, k ^ 1],
                device_id=targets[k],
                device_id_type=MESH,
            )
            for k in range(4)
        ]

    present = (i > 0, i < nx - 1, j > 0, j < ny - 1)

    def hot(row, count):
        parts = []
        for a in range(count // BLOCK):
            inside = jnp.where(lax.shift_right_arithmetic(row, 8) == a, row & 255, -1)
            inside = inside.astype(F32).astype(BF16)
            same = iota[:, : row.shape[1]] == inside
            parts.append(jnp.where(same, jnp.ones((), BF16), jnp.zeros((), BF16)))
        return jnp.concatenate(parts, axis=0)

    eye = (
        lax.broadcasted_iota(I32, (W, W), 0) == lax.broadcasted_iota(I32, (W, W), 1)
    ).astype(F32).astype(BF16)

    def turned(block):
        return right_t(eye, block).astype(BF16)

    iota[...] = lax.broadcasted_iota(I32, iota.shape, 0).astype(F32).astype(BF16)
    ext_t[:, :cells] = turned(nodes[...])
    hot_list[...] = hot(lane_row(slist, 0, 4), cells)
    picked = dot(ext_t[:, :cells], hot_list[...]).astype(BF16)
    for k in range(4):
        pick[k] = picked[:, k * W : (k + 1) * W]

    pl.semaphore_wait(barrier, 2 + ny - 1 + nz - 1)
    halo_out = halo_copies(pick, halo, halo_sem)
    for copy in halo_out:
        copy.start()

    own_row = lane_row(owner, 0, cells // W)
    own_t[...] = hot(own_row, cells)
    cot_src[...] = dot(own_t[...], cot[...]).astype(BF16).reshape(ny, owned, W)
    scatter_start(cot_src, cot_in, cot_sem)

    ws_t, wr_t, we_t = [turned(w_edge[k]) for k in range(3)]
    b_col = jnp.broadcast_to(bias[0:1, :], (W, W)).T
    table_t[:, ext:] = dot(wr_t, ext_t[:, :cells]).astype(BF16)
    for copy in halo_out:
        copy.wait_recv()
    for k in range(4):
        ext_t[:, cells + k * W : cells + (k + 1) * W] = jnp.where(
            present[k], halo[k].astype(F32), 0.0
        ).astype(BF16)
    table_t[:, :ext] = (
        dot(ws_t, ext_t[...]) + jnp.concatenate([b_col] * (ext // W), axis=1)
    ).astype(BF16)

    h_acc[...] = jnp.zeros_like(h_acc)
    per = tile // W
    alive = live[0]

    def hot_senders(t):
        return hot(lane_row(snd, t * per, per), ext)

    def hot_receivers(t):
        place = t * tile + lax.broadcasted_iota(I32, (1, tile), 1)
        return hot(jnp.where(place < alive, lane_row(rcv, t * per, per), -1), cells)

    def feat_tile(t):
        return feat[pl.ds(pl.multiple_of(t * tile, tile), tile), :]

    def forward(t, c):
        mark_r = hot_receivers(t)
        pre = (
            dot(table_t[:, :ext], hot_senders(t))
            + dot(table_t[:, ext:], mark_r)
            + right_t(we_t, feat_tile(t))
        )
        sigma = sigmoid(pre)
        slopes[t] = slope(pre, sigma)
        h_acc[...] += right_t(mark_r, (pre * sigma).astype(BF16))
        return c

    lax.fori_loop(0, edges // tile, forward, 0)

    hb[...] = h_acc[...].astype(BF16)
    agg[...] = dot(hb[...], w_edge[3]).astype(BF16)
    pre_node = dot(nodes[...], w_node[0]) + dot(agg[...], w_node[1]) + bias[1:2, :]
    sigma = sigmoid(pre_node)
    node_slope[...] = slope(pre_node, sigma)
    hid[...] = (pre_node * sigma).astype(BF16)
    fine[...] = nodes[...].astype(F32) + dot(hid[...], w_node[2])
    fine_src[...] = dot(own_t[...], fine[...].astype(BF16)).astype(BF16).reshape(ny, owned, W)
    scatter_start(fine_src, fine_in, fine_sem)

    for q in range(cells // W):
        column = jnp.broadcast_to(owner[q : q + 1, :].astype(F32), (W, W)).T
        lanes = lax.broadcasted_iota(I32, (W, W), 1).astype(F32)
        own_n[q * W : (q + 1) * W, :] = jnp.concatenate(
            [
                jnp.where(column == lanes + float(k * W), 1.0, 0.0).astype(BF16)
                for k in range(cells // W)
            ],
            axis=1,
        )
    agg_t, hid_t, hb_t = turned(agg[...]), turned(hid[...]), turned(hb[...])

    row_arrive(cot_in, cot_sem)
    d_coarse = slots_sum(cot_in).astype(BF16)
    d_hidden = right_t(d_coarse, w_coarse[1])
    row_arrive(fine_in, fine_sem)
    coarse_bf = (0.0625 * slots_sum(fine_in)).astype(BF16)
    pre_coarse = dot(coarse_bf, w_coarse[0]) + bias[2:3, :]
    sigma = sigmoid(pre_coarse)
    coarse_hid = (pre_coarse * sigma).astype(BF16)
    d_pre_c = d_hidden * slope(pre_coarse, sigma)
    d_pre_c_bf = d_pre_c.astype(BF16)
    coarse_all[j] = jnp.concatenate(
        [dot(coarse_hid, w_coarse[1]).astype(BF16), right_t(d_pre_c_bf, w_coarse[0]).astype(BF16)],
        axis=1,
    )
    gather_start(coarse_all, coarse_sem)
    grad_rows = a_src.shape[1]
    g_v1 = dot(turned(coarse_bf), d_pre_c_bf)
    g_v2 = dot(turned(coarse_hid), d_coarse)
    bias_rows[...] = jnp.zeros_like(bias_rows)
    bias_rows[2:3, :] = jnp.sum(d_pre_c, axis=0, keepdims=True)
    row_arrive(coarse_all, coarse_sem)

    picked = dot(own_n[...], coarse_all[...].reshape(cells, 2 * W))
    node_out[...] = (fine[...] + picked[:, :W]).astype(BF16)
    d_fine = cot[...].astype(F32) + 0.0625 * picked[:, W:]
    d_fine_bf = d_fine.astype(BF16)
    d_pre_n = right_t(d_fine_bf, w_node[2]) * node_slope[...]
    d_pre_n_bf = d_pre_n.astype(BF16)
    bias_rows[1:2, :] = jnp.sum(d_pre_n, axis=0, keepdims=True)
    d_part[...] = d_fine + right_t(d_pre_n_bf, w_node[0])
    d_agg = right_t(d_pre_n_bf, w_node[1]).astype(BF16)
    table_t[:, ext:] = right_t(w_edge[3], d_agg).astype(BF16)
    a_src[...] = jnp.concatenate(
        [
            dot(hb_t, d_agg),
            dot(ext_t[:, :cells], d_pre_n_bf),
            dot(agg_t, d_pre_n_bf),
            dot(hid_t, d_fine_bf),
            g_v1,
            g_v2,
        ],
        axis=0,
    ).reshape(ny, grad_rows, W)
    a_stage[0]()

    sr_acc[...] = jnp.zeros_like(sr_acc)
    we_acc[...] = jnp.zeros_like(we_acc)

    def backward(t, c):
        mark_r = hot_receivers(t)
        d_pre = (dot(table_t[:, ext:], mark_r) * slopes[t]).astype(BF16)
        sr_acc[:ext, :] += right_t(hot_senders(t), d_pre)
        sr_acc[ext:, :] += right_t(mark_r, d_pre)
        we_acc[...] += dot(d_pre, feat_tile(t))
        d_edges[pl.ds(pl.multiple_of(t * tile, tile), tile), :] = (
            dot(w_edge[2], d_pre).T.astype(BF16)
        )
        return c

    tiles = edges // tile
    cuts = [tiles * k // 4 for k in range(5)]
    for k in range(4):
        lax.fori_loop(cuts[k], cuts[k + 1], backward, 0)
        a_stage[k + 1]()

    s_bf = sr_acc[:ext, :].astype(BF16)
    r_bf = sr_acc[ext:, :].astype(BF16)
    back_src[...] = right_t(s_bf[cells:, :], w_edge[0]).astype(BF16).reshape(4, W, W)
    back_out = halo_copies(back_src, back_in, back_sem)
    for copy in back_out:
        copy.start()
    bias_rows[0:1, :] = jnp.sum(sr_acc[ext:, :], axis=0, keepdims=True)
    b_flat[...] = jnp.concatenate(
        [dot(ext_t[...], s_bf), dot(ext_t[:, :cells], r_bf), we_acc[...].T], axis=0
    )
    share = b_flat.shape[0] // ny
    for k in range(ny):
        b_src[k, :share, :] = b_flat[k * share : (k + 1) * share, :]
        b_src[k, share:, :] = bias_rows[...]
    b_stage[0]()
    local = d_part[...] + right_t(s_bf[:cells, :], w_edge[0]) + right_t(r_bf, w_edge[1])
    for copy in back_out:
        copy.wait_recv()
    returned = jnp.concatenate(
        [jnp.where(present[k], back_in[k].astype(F32), 0.0) for k in range(4)], axis=0
    ).astype(BF16)
    d_nodes[...] = (local + dot(hot_list[...], returned)).astype(BF16)
    for stage in b_stage[1:5]:
        stage()
    a_stage[5]()
    grads[3 * W :, :] = a_all[...].reshape(6 * W, W)
    row_sent(cot_src, cot_in, cot_sem)
    row_sent(fine_src, fine_in, fine_sem)
    row_sent(coarse_all, coarse_all, coarse_sem)
    for copy in halo_out + back_out:
        copy.wait_send()
    b_stage[5]()
    for k in range(ny):
        grads[k * share : (k + 1) * share, :] = b_all[k, :share, :]
    bias_grads[...] = b_fin[share:, :]


def body(
    dims,
    nodes,
    edge_feat,
    senders,
    receivers,
    send_lists,
    owner,
    edge_live,
    cotangent,
    w_edge,
    w_node,
    w_coarse,
    biases,
):
    nx, ny, cells, edges, tile = dims
    nz = nx // 2
    ext = cells + 4 * W
    owned = cells // ny
    a_rows, b_rows = 6 * W // ny, 3 * W // ny + 8
    vmem = pl.BlockSpec(memory_space=pltpu.VMEM)
    smem = pl.BlockSpec(memory_space=pltpu.SMEM)

    def exchange(rows):
        return [
            pltpu.VMEM((ny, rows, W), F32),
            pltpu.VMEM((ny, rows, W), F32),
            pltpu.VMEM((rows, W), F32),
            pltpu.VMEM((rows // 2, W), F32),
            pltpu.VMEM((nz, rows // 2, W), F32),
            pltpu.VMEM((rows, W), F32),
            pltpu.VMEM((ny, rows, W), F32),
        ]

    b_exchange = exchange(b_rows)
    sems = [4, 4, ny, ny, ny] + [ny, 2, nz, ny] * 2
    outs = pl.pallas_call(
        functools.partial(kernel, dims),
        out_shape=(
            jax.ShapeDtypeStruct((cells, W), BF16),
            jax.ShapeDtypeStruct((cells, W), BF16),
            jax.ShapeDtypeStruct((edges, W), BF16),
            jax.ShapeDtypeStruct((9 * W, W), F32),
            jax.ShapeDtypeStruct((8, W), F32),
        ),
        in_specs=[vmem] * 6 + [smem] + [vmem] * 5,
        out_specs=(vmem,) * 5,
        scratch_shapes=[
            pltpu.VMEM((BLOCK, max(cells, tile)), BF16),
            pltpu.VMEM((W, ext), BF16),
            pltpu.VMEM((W, ext + cells), BF16),
            pltpu.VMEM((cells, 4 * W), BF16),
            pltpu.VMEM((cells, cells), BF16),
            pltpu.VMEM((cells, cells), BF16),
            pltpu.VMEM((4, W, W), BF16),
            pltpu.VMEM((4, W, W), BF16),
            pltpu.VMEM((edges // tile, W, tile), F32),
            pltpu.VMEM((cells, W), F32),
            pltpu.VMEM((ext + cells, W), F32),
            pltpu.VMEM((W, W), F32),
            pltpu.VMEM((cells, W), F32),
            pltpu.VMEM((cells, W), F32),
            pltpu.VMEM((cells, W), F32),
            pltpu.VMEM((cells, W), BF16),
            pltpu.VMEM((cells, W), BF16),
            pltpu.VMEM((cells, W), BF16),
            pltpu.VMEM((ny, owned, W), BF16),
            pltpu.VMEM((ny, owned, W), BF16),
            pltpu.VMEM((ny, owned, W), BF16),
            pltpu.VMEM((ny, owned, W), BF16),
            pltpu.VMEM((ny, owned, 2 * W), BF16),
            pltpu.VMEM((4, W, W), BF16),
            pltpu.VMEM((4, W, W), BF16),
            pltpu.VMEM((8, W), F32),
            *exchange(a_rows),
            pltpu.VMEM((3 * W, W), F32),
            *b_exchange,
        ]
        + [pltpu.SemaphoreType.DMA((2, count)) for count in sems],
        compiler_params=pltpu.CompilerParams(
            collective_id=0, has_side_effects=True, vmem_limit_bytes=48 * 1024 * 1024
        ),
        cost_estimate=pl.CostEstimate(
            flops=2 * edges * W * (2 * ext + 4 * cells + 4 * W),
            bytes_accessed=2 * W * (2 * edges + 4 * cells),
            transcendentals=edges * W,
        ),
        name="mesh_step",
    )(
        nodes,
        edge_feat,
        senders.reshape(edges // W, W),
        receivers.reshape(edges // W, W),
        send_lists.reshape(4, W),
        owner.reshape(cells // W, W),
        edge_live,
        cotangent,
        w_edge,
        w_node,
        w_coarse,
        biases,
    )
    node_out, d_nodes, d_edges, grads, bias_grads = outs
    return node_out, d_nodes, d_edges, grads.reshape(9, W, W), bias_grads[:3]


def solution(mesh, cells=1024, edges=4096, tile=512):
    both = ("gx", "gy")
    dims = (mesh.shape["gx"], mesh.shape["gy"], cells, edges, tile)
    in_specs = (
        P(both, None),
        P(both, None),
        P(both),
        P(both),
        P(both, None, None),
        P(both),
        P(both),
        P(both, None),
        P(),
        P(),
        P(),
        P(),
    )
    out_specs = (P(both, None), P(both, None), P(both, None), P(), P())
    return jax.shard_map(
        functools.partial(body, dims),
        mesh=mesh,
        in_specs=in_specs,
        out_specs=out_specs,
        check_vma=False,
    )
```

```python
import functools
from types import SimpleNamespace

import jax
import jax.numpy as jnp
from jax import lax
from jax.experimental import pallas as pl
from jax.experimental.pallas import tpu as pltpu
from jax.sharding import PartitionSpec as P

F32, BF16, I32 = jnp.float32, jnp.bfloat16, jnp.int32
W = 128
BLOCK = 256
MESH = pl.DeviceIdType.MESH


def dot(left, right):
    return jnp.dot(left, right, preferred_element_type=F32)


def right_t(left, right):
    return lax.dot_general(left, right, (((1,), (1,)), ((), ())), preferred_element_type=F32)


def sigmoid(value):
    return 0.5 * jnp.tanh(0.5 * value) + 0.5


def slope(value, sigma):
    return sigma * (1.0 + value * (1.0 - sigma))


def lane_row(ref, first, count):
    return jnp.concatenate([ref[pl.ds(first + q, 1), :] for q in range(count)], axis=1)


INPUTS = (
    "nodes", "feat", "snd", "rcv", "slist", "owner", "cot", "w_edge", "w_node", "w_coarse", "bias"
)
ORDER = (
    "slist", "nodes", "owner", "cot", "snd", "rcv", "w_edge", "bias", "feat", "w_node", "w_coarse"
)
OUTPUTS = ("node_out", "d_nodes", "d_edges", "grads", "bias_grads")


def kernel(dims, names, *refs):
    r = SimpleNamespace(**dict(zip(names, refs)))
    nx, ny, cells, edges, tile = dims
    nz = nx // 2
    ng = 2 * ny
    ext = cells + 4 * W
    owned = cells // ny
    tiles = edges // tile
    i, j = lax.axis_index("gx"), lax.axis_index("gy")
    core, z = lax.rem(i, 2), lax.div(i, 2)
    g = core * ny + j
    up, down = lax.rem(i + nx - 1, nx), lax.rem(i + 1, nx)
    left, right = lax.rem(j + ny - 1, ny), lax.rem(j + 1, ny)
    across = lax.rem(i + nx - 1 + 2 * core, nx)

    barrier = pltpu.get_barrier_semaphore()

    def greet(gx, gy):
        pl.semaphore_signal(barrier, inc=1, device_id=(gx, gy), device_id_type=MESH)

    def each(count, me, action):
        def step(d, c):
            action(lax.rem(me + d, count))
            return c

        lax.fori_loop(1, count, step, 0)

    greet(across, j)
    loads = {
        name: pltpu.make_async_copy(
            getattr(r, name + "_in"), getattr(r, name), r.load_sem.at[k]
        )
        for k, name in enumerate(ORDER)
    }
    for name in ORDER:
        loads[name].start()
    each(ng, g, lambda t: greet(2 * z + lax.div(t, ny), lax.rem(t, ny)))
    each(nz, z, lambda t: greet(2 * t + core, j))

    def exchange(count, me, place):
        def copy(src, dst, sems, slot, target):
            return pltpu.make_async_remote_copy(
                src_ref=src,
                dst_ref=dst.at[slot],
                send_sem=sems.at[0, target],
                recv_sem=sems.at[1, slot],
                device_id=place(target),
                device_id_type=MESH,
            )

        def scatter(src, dst, sems):
            dst[me] = src[me]
            each(count, me, lambda t: copy(src.at[t], dst, sems, me, t).start())

        def gather(buf, sems):
            each(count, me, lambda t: copy(buf.at[me], buf, sems, me, t).start())

        def arrive(buf, sems):
            each(count, me, lambda t: copy(buf.at[t], buf, sems, t, t).wait_recv())

        def sent(buf, sems):
            each(count, me, lambda t: copy(buf.at[me], buf, sems, me, t).wait_send())

        return SimpleNamespace(scatter=scatter, gather=gather, arrive=arrive, sent=sent)

    row = exchange(ny, j, lambda t: (i, t))
    column = exchange(nz, z, lambda t: (2 * t + core, j))
    layer = exchange(ng, g, lambda t: (2 * z + lax.div(t, ny), lax.rem(t, ny)))

    def slots_sum(ref):
        return jnp.sum(ref[...].astype(F32), axis=0)

    def reduce_stages(src, into, zbuf, everything, sums, sems):
        rs_sem, z_sem, ag_sem = sems

        def start():
            layer.scatter(src, into, rs_sem)

        def to_column():
            layer.arrive(into, rs_sem)
            zbuf[z] = slots_sum(into).astype(BF16)
            column.gather(zbuf, z_sem)

        def to_layer():
            column.arrive(zbuf, z_sem)
            sums[...] = slots_sum(zbuf)
            everything[g] = sums[...].astype(BF16)
            layer.gather(everything, ag_sem)

        def finish():
            layer.arrive(everything, ag_sem)

        def sent():
            layer.sent(into, rs_sem)
            column.sent(zbuf, z_sem)
            layer.sent(everything, ag_sem)

        return SimpleNamespace(
            start=start, to_column=to_column, to_layer=to_layer, finish=finish, sent=sent
        )

    a_stage = reduce_stages(
        r.a_src, r.a_in, r.a_z, r.a_all, r.a_sum, (r.a_rs_sem, r.a_z_sem, r.a_ag_sem)
    )
    b_stage = reduce_stages(
        r.b_src, r.b_in, r.b_z, r.b_all, r.b_sum, (r.b_rs_sem, r.b_z_sem, r.b_ag_sem)
    )

    def halo_copies(src, dst, sems):
        targets = ((up, j), (down, j), (i, left), (i, right))
        return [
            pltpu.make_async_remote_copy(
                src_ref=src.at[k],
                dst_ref=dst.at[k ^ 1],
                send_sem=sems.at[0, k],
                recv_sem=sems.at[1, k ^ 1],
                device_id=targets[k],
                device_id_type=MESH,
            )
            for k in range(4)
        ]

    present = (i > 0, i < nx - 1, j > 0, j < ny - 1)

    def hot(line, count):
        parts = []
        for a in range(count // BLOCK):
            inside = jnp.where(lax.shift_right_arithmetic(line, 8) == a, line & 255, -1)
            inside = inside.astype(F32).astype(BF16)
            same = r.iota[:, : line.shape[1]] == inside
            parts.append(jnp.where(same, jnp.ones((), BF16), jnp.zeros((), BF16)))
        return jnp.concatenate(parts, axis=0)

    eye = (
        lax.broadcasted_iota(I32, (W, W), 0) == lax.broadcasted_iota(I32, (W, W), 1)
    ).astype(F32).astype(BF16)

    def turned(block):
        return right_t(eye, block).astype(BF16)

    r.iota[...] = lax.broadcasted_iota(I32, r.iota.shape, 0).astype(F32).astype(BF16)
    loads["slist"].wait()
    r.hot_list[...] = hot(lane_row(r.slist, 0, 4), cells)
    loads["nodes"].wait()
    r.ext_t[:, :cells] = turned(r.nodes[...])
    picked = dot(r.ext_t[:, :cells], r.hot_list[...]).astype(BF16)
    for k in range(4):
        r.pick[k] = picked[:, k * W : (k + 1) * W]
    loads["owner"].wait()
    r.own_t[...] = hot(lane_row(r.owner, 0, cells // W), cells)
    loads["cot"].wait()
    r.cot_src[...] = dot(r.own_t[...], r.cot[...]).astype(BF16).reshape(ny, owned, W)

    pl.semaphore_wait(barrier, ng + nz - 1)
    halo_out = halo_copies(r.pick, r.halo, r.halo_sem)
    for copy in halo_out:
        copy.start()
    row.scatter(r.cot_src, r.cot_got, r.cot_sem)

    loads["snd"].wait()
    loads["rcv"].wait()
    per = tile // W
    alive = r.live[0]

    def mark(t, c):
        r.marks[t, :ext, :] = hot(lane_row(r.snd, t * per, per), ext)
        place = t * tile + lax.broadcasted_iota(I32, (1, tile), 1)
        line = jnp.where(place < alive, lane_row(r.rcv, t * per, per), -1)
        r.marks[t, ext:, :] = hot(line, cells)
        return c

    lax.fori_loop(0, tiles, mark, 0)

    loads["w_edge"].wait()
    loads["bias"].wait()
    ws_t, wr_t, we_t = [turned(r.w_edge[k]) for k in range(3)]
    b_col = jnp.broadcast_to(r.bias[0:1, :], (W, W)).T
    r.table_t[:, ext:] = dot(wr_t, r.ext_t[:, :cells]).astype(BF16)
    loads["feat"].wait()
    for copy in halo_out:
        copy.wait_recv()
    for k in range(4):
        r.ext_t[:, cells + k * W : cells + (k + 1) * W] = jnp.where(
            present[k], r.halo[k].astype(F32), 0.0
        ).astype(BF16)
    r.table_t[:, :ext] = (
        dot(ws_t, r.ext_t[...]) + jnp.concatenate([b_col] * (ext // W), axis=1)
    ).astype(BF16)

    r.h_acc[...] = jnp.zeros_like(r.h_acc)

    def edge_rows(t):
        return pl.ds(pl.multiple_of(t * tile, tile), tile)

    def forward(t, c):
        pre = dot(r.table_t[...], r.marks[t]) + right_t(we_t, r.feat[edge_rows(t), :])
        sigma = sigmoid(pre)
        r.slopes[t] = slope(pre, sigma)
        r.h_acc[...] += right_t(r.marks[t, ext:, :], (pre * sigma).astype(BF16))
        return c

    lax.fori_loop(0, tiles, forward, 0)

    loads["w_node"].wait()
    loads["w_coarse"].wait()
    r.hb[...] = r.h_acc[...].astype(BF16)
    r.agg[...] = dot(r.hb[...], r.w_edge[3]).astype(BF16)
    pre_node = dot(r.nodes[...], r.w_node[0]) + dot(r.agg[...], r.w_node[1]) + r.bias[1:2, :]
    sigma = sigmoid(pre_node)
    r.node_slope[...] = slope(pre_node, sigma)
    r.hid[...] = (pre_node * sigma).astype(BF16)
    r.fine[...] = r.nodes[...].astype(F32) + dot(r.hid[...], r.w_node[2])
    sums = dot(r.own_t[...], r.fine[...].astype(BF16))
    r.fine_src[...] = sums.astype(BF16).reshape(ny, owned, W)
    row.scatter(r.fine_src, r.fine_got, r.fine_sem)

    for q in range(cells // W):
        at = jnp.broadcast_to(r.owner[q : q + 1, :].astype(F32), (W, W)).T
        lanes = lax.broadcasted_iota(I32, (W, W), 1).astype(F32)
        r.own_n[q * W : (q + 1) * W, :] = jnp.concatenate(
            [
                jnp.where(at == lanes + float(k * W), 1.0, 0.0).astype(BF16)
                for k in range(cells // W)
            ],
            axis=1,
        )
    agg_t, hid_t, hb_t = turned(r.agg[...]), turned(r.hid[...]), turned(r.hb[...])

    row.arrive(r.cot_got, r.cot_sem)
    d_coarse = slots_sum(r.cot_got).astype(BF16)
    d_hidden = right_t(d_coarse, r.w_coarse[1])
    row.arrive(r.fine_got, r.fine_sem)
    coarse_bf = (0.0625 * slots_sum(r.fine_got)).astype(BF16)
    pre_coarse = dot(coarse_bf, r.w_coarse[0]) + r.bias[2:3, :]
    sigma = sigmoid(pre_coarse)
    coarse_hid = (pre_coarse * sigma).astype(BF16)
    d_pre_c = d_hidden * slope(pre_coarse, sigma)
    d_pre_c_bf = d_pre_c.astype(BF16)
    r.coarse_all[j] = jnp.concatenate(
        [
            dot(coarse_hid, r.w_coarse[1]).astype(BF16),
            right_t(d_pre_c_bf, r.w_coarse[0]).astype(BF16),
        ],
        axis=1,
    )
    row.gather(r.coarse_all, r.coarse_sem)
    g_v1 = dot(turned(coarse_bf), d_pre_c_bf)
    g_v2 = dot(turned(coarse_hid), d_coarse)
    b_own = r.b_src.shape[1]
    a_own = 6 * W // ng
    share = 3 * W // ng
    r.bias_rows[...] = jnp.zeros_like(r.bias_rows)
    r.bias_rows[share + 2 : share + 3, :] = jnp.sum(d_pre_c, axis=0, keepdims=True)
    row.arrive(r.coarse_all, r.coarse_sem)

    picked = dot(r.own_n[...], r.coarse_all[...].reshape(cells, 2 * W))
    r.node_out[...] = (r.fine[...] + picked[:, :W]).astype(BF16)
    d_fine = r.cot[...].astype(F32) + 0.0625 * picked[:, W:]
    d_fine_bf = d_fine.astype(BF16)
    d_pre_n = right_t(d_fine_bf, r.w_node[2]) * r.node_slope[...]
    d_pre_n_bf = d_pre_n.astype(BF16)
    r.bias_rows[share + 1 : share + 2, :] = jnp.sum(d_pre_n, axis=0, keepdims=True)
    r.d_part[...] = d_fine + right_t(d_pre_n_bf, r.w_node[0])
    d_agg = right_t(d_pre_n_bf, r.w_node[1]).astype(BF16)
    r.table_t[:, ext:] = right_t(r.w_edge[3], d_agg).astype(BF16)
    early = jnp.concatenate(
        [
            dot(hb_t, d_agg),
            dot(r.ext_t[:, :cells], d_pre_n_bf),
            dot(agg_t, d_pre_n_bf),
            dot(hid_t, d_fine_bf),
            g_v1,
            g_v2,
        ],
        axis=0,
    ).reshape(ng, a_own, W)
    spare = r.a_src.shape[1] - a_own
    if spare:
        early = jnp.concatenate([early, jnp.zeros((ng, spare, W), F32)], axis=1)
    r.a_src[...] = early.astype(BF16)
    a_stage.start()

    r.sr_acc[...] = jnp.zeros_like(r.sr_acc)
    r.we_acc[...] = jnp.zeros_like(r.we_acc)

    def backward(t, c):
        d_pre = (dot(r.table_t[:, ext:], r.marks[t, ext:, :]) * r.slopes[t]).astype(BF16)
        r.d_pre[t] = d_pre
        r.sr_acc[...] += right_t(r.marks[t], d_pre)
        r.we_acc[...] += dot(d_pre, r.feat[edge_rows(t), :])
        return c

    def edge_out(t, c):
        r.d_edges[edge_rows(t), :] = dot(r.w_edge[2], r.d_pre[t]).T.astype(BF16)
        return c

    half = tiles // 2
    lax.fori_loop(0, half, backward, 0)
    a_stage.to_column()
    lax.fori_loop(half, tiles, backward, 0)
    a_stage.to_layer()

    s_bf = r.sr_acc[:ext, :].astype(BF16)
    r_bf = r.sr_acc[ext:, :].astype(BF16)
    r.back_src[...] = right_t(s_bf[cells:, :], r.w_edge[0]).astype(BF16).reshape(4, W, W)
    back_out = halo_copies(r.back_src, r.back_got, r.back_sem)
    for copy in back_out:
        copy.start()
    r.bias_rows[share : share + 1, :] = jnp.sum(r.sr_acc[ext:, :], axis=0, keepdims=True)
    r.b_flat[: 3 * W, :] = jnp.concatenate(
        [dot(r.ext_t[...], s_bf), dot(r.ext_t[:, :cells], r_bf), r.we_acc[...].T], axis=0
    )
    r.b_flat[3 * W :, :] = jnp.zeros((b_own, W), F32)
    inner = lax.broadcasted_iota(I32, (b_own, W), 0) < share
    for k in range(ng):
        part = r.b_flat[k * share : k * share + b_own, :]
        r.b_src[k] = jnp.where(inner, part, r.bias_rows[...]).astype(BF16)
    b_stage.start()
    local = (
        r.d_part[...] + right_t(s_bf[:cells, :], r.w_edge[0]) + right_t(r_bf, r.w_edge[1])
    )
    r.d_part[...] = local
    lax.fori_loop(0, half, edge_out, 0)
    b_stage.to_column()
    for copy in back_out:
        copy.wait_recv()
    returned = jnp.concatenate(
        [jnp.where(present[k], r.back_got[k].astype(F32), 0.0) for k in range(4)], axis=0
    ).astype(BF16)
    r.d_nodes[...] = (r.d_part[...] + dot(r.hot_list[...], returned)).astype(BF16)
    lax.fori_loop(half, tiles, edge_out, 0)
    b_stage.to_layer()
    a_stage.finish()
    r.grads[3 * W :, :] = r.a_all[...].astype(F32)[:, :a_own, :].reshape(6 * W, W)
    row.sent(r.cot_got, r.cot_sem)
    row.sent(r.fine_got, r.fine_sem)
    row.sent(r.coarse_all, r.coarse_sem)
    for copy in halo_out + back_out:
        copy.wait_send()
    a_stage.sent()
    r.bias_grads[...] = r.b_sum[share : share + 3, :]
    b_stage.finish()
    for k in range(ng):
        r.grads[k * share : (k + 1) * share, :] = r.b_all[k].astype(F32)[:share, :]
    b_stage.sent()


def settle(*refs):
    count = len(OUTPUTS)
    sems = refs[2 * count]
    copies = [
        pltpu.make_async_copy(refs[k], refs[count + k], sems.at[k]) for k in range(count)
    ]
    for copy in copies:
        copy.start()
    for copy in copies:
        copy.wait()


def body(
    dims,
    nodes,
    edge_feat,
    senders,
    receivers,
    send_lists,
    owner,
    edge_live,
    cotangent,
    w_edge,
    w_node,
    w_coarse,
    biases,
):
    nx, ny, cells, edges, tile = dims
    nz = nx // 2
    ng = 2 * ny
    ext = cells + 4 * W
    owned = cells // ny
    a_rows = -(-(6 * W // ng) // 16) * 16
    b_rows = -(-(3 * W // ng + 3) // 16) * 16
    operands = dict(
        nodes=nodes,
        feat=edge_feat,
        snd=senders.reshape(edges // W, W),
        rcv=receivers.reshape(edges // W, W),
        slist=send_lists.reshape(4, W),
        owner=owner.reshape(cells // W, W),
        cot=cotangent,
        w_edge=w_edge,
        w_node=w_node,
        w_coarse=w_coarse,
        bias=biases,
    )
    scratch = {name: pltpu.VMEM(operands[name].shape, operands[name].dtype) for name in INPUTS}
    scratch |= dict(
        iota=pltpu.VMEM((BLOCK, max(cells, tile)), BF16),
        ext_t=pltpu.VMEM((W, ext), BF16),
        table_t=pltpu.VMEM((W, ext + cells), BF16),
        marks=pltpu.VMEM((edges // tile, ext + cells, tile), BF16),
        hot_list=pltpu.VMEM((cells, 4 * W), BF16),
        own_t=pltpu.VMEM((cells, cells), BF16),
        own_n=pltpu.VMEM((cells, cells), BF16),
        pick=pltpu.VMEM((4, W, W), BF16),
        halo=pltpu.VMEM((4, W, W), BF16),
        slopes=pltpu.VMEM((edges // tile, W, tile), F32),
        d_pre=pltpu.VMEM((edges // tile, W, tile), BF16),
        h_acc=pltpu.VMEM((cells, W), F32),
        sr_acc=pltpu.VMEM((ext + cells, W), F32),
        we_acc=pltpu.VMEM((W, W), F32),
        fine=pltpu.VMEM((cells, W), F32),
        node_slope=pltpu.VMEM((cells, W), F32),
        d_part=pltpu.VMEM((cells, W), F32),
        hb=pltpu.VMEM((cells, W), BF16),
        agg=pltpu.VMEM((cells, W), BF16),
        hid=pltpu.VMEM((cells, W), BF16),
        cot_src=pltpu.VMEM((ny, owned, W), BF16),
        cot_got=pltpu.VMEM((ny, owned, W), BF16),
        fine_src=pltpu.VMEM((ny, owned, W), BF16),
        fine_got=pltpu.VMEM((ny, owned, W), BF16),
        coarse_all=pltpu.VMEM((ny, owned, 2 * W), BF16),
        back_src=pltpu.VMEM((4, W, W), BF16),
        back_got=pltpu.VMEM((4, W, W), BF16),
        bias_rows=pltpu.VMEM((b_rows, W), F32),
        b_flat=pltpu.VMEM((3 * W + b_rows, W), F32),
        load_sem=pltpu.SemaphoreType.DMA((len(INPUTS),)),
        halo_sem=pltpu.SemaphoreType.DMA((2, 4)),
        back_sem=pltpu.SemaphoreType.DMA((2, 4)),
        cot_sem=pltpu.SemaphoreType.DMA((2, ny)),
        fine_sem=pltpu.SemaphoreType.DMA((2, ny)),
        coarse_sem=pltpu.SemaphoreType.DMA((2, ny)),
    )
    for name, rows in (("a", a_rows), ("b", b_rows)):
        scratch |= {
            name + "_src": pltpu.VMEM((ng, rows, W), BF16),
            name + "_in": pltpu.VMEM((ng, rows, W), BF16),
            name + "_z": pltpu.VMEM((nz, rows, W), BF16),
            name + "_all": pltpu.VMEM((ng, rows, W), BF16),
            name + "_sum": pltpu.VMEM((rows, W), F32),
            name + "_rs_sem": pltpu.SemaphoreType.DMA((2, ng)),
            name + "_z_sem": pltpu.SemaphoreType.DMA((2, nz)),
            name + "_ag_sem": pltpu.SemaphoreType.DMA((2, ng)),
        }
    names = tuple(name + "_in" for name in INPUTS) + ("live",) + OUTPUTS + tuple(scratch)
    vmem = pl.BlockSpec(memory_space=pltpu.VMEM)
    smem = pl.BlockSpec(memory_space=pltpu.SMEM)
    hbm = pl.BlockSpec(memory_space=pltpu.HBM)
    shapes = (
        jax.ShapeDtypeStruct((cells, W), BF16),
        jax.ShapeDtypeStruct((cells, W), BF16),
        jax.ShapeDtypeStruct((edges, W), BF16),
        jax.ShapeDtypeStruct((9 * W, W), F32),
        jax.ShapeDtypeStruct((3, W), F32),
    )
    outs = pl.pallas_call(
        functools.partial(kernel, dims, names),
        out_shape=shapes,
        in_specs=[hbm] * len(INPUTS) + [smem],
        out_specs=(vmem,) * 5,
        scratch_shapes=list(scratch.values()),
        compiler_params=pltpu.CompilerParams(
            collective_id=0, has_side_effects=True, vmem_limit_bytes=52 * 1024 * 1024
        ),
        cost_estimate=pl.CostEstimate(
            flops=2 * edges * W * (2 * ext + 4 * cells + 4 * W),
            bytes_accessed=2 * W * (2 * edges + 4 * cells),
            transcendentals=edges * W,
        ),
        name="mesh_step",
    )(*[operands[name] for name in INPUTS], edge_live)
    outs = pl.pallas_call(
        settle,
        out_shape=shapes,
        in_specs=[vmem] * 5,
        out_specs=(hbm,) * 5,
        scratch_shapes=[pltpu.SemaphoreType.DMA((5,))],
        name="settle",
    )(*outs)
    node_out, d_nodes, d_edges, grads, bias_grads = outs
    return node_out, d_nodes, d_edges, grads.reshape(9, W, W), bias_grads


def solution(mesh, cells=1024, edges=4096, tile=1024):
    both = ("gx", "gy")
    dims = (mesh.shape["gx"], mesh.shape["gy"], cells, edges, tile)
    in_specs = (
        P(both, None),
        P(both, None),
        P(both),
        P(both),
        P(both, None, None),
        P(both),
        P(both),
        P(both, None),
        P(),
        P(),
        P(),
        P(),
    )
    out_specs = (P(both, None), P(both, None), P(both, None), P(), P())
    return jax.shard_map(
        functools.partial(body, dims),
        mesh=mesh,
        in_specs=in_specs,
        out_specs=out_specs,
        check_vma=False,
    )
```

```python
import functools
from types import SimpleNamespace

import jax
import jax.numpy as jnp
from jax import lax
from jax.experimental import pallas as pl
from jax.experimental.pallas import tpu as pltpu
from jax.sharding import PartitionSpec as P

F32, BF16, I32 = jnp.float32, jnp.bfloat16, jnp.int32
W = 128
BLOCK = 256
MESH = pl.DeviceIdType.MESH


def dot(left, right):
    return jnp.dot(left, right, preferred_element_type=F32)


def right_t(left, right):
    return lax.dot_general(left, right, (((1,), (1,)), ((), ())), preferred_element_type=F32)


def sigmoid(value):
    return 0.5 * jnp.tanh(0.5 * value) + 0.5


def slope(value, sigma):
    return sigma * (1.0 + value * (1.0 - sigma))


def lane_row(ref, first, count):
    return jnp.concatenate([ref[pl.ds(first + q, 1), :] for q in range(count)], axis=1)


INPUTS = (
    "nodes", "feat", "snd", "rcv", "slist", "owner", "cot", "w_edge", "w_node", "w_coarse", "bias"
)
ORDER = (
    "slist", "nodes", "owner", "cot", "snd", "rcv", "w_edge", "bias", "feat", "w_node", "w_coarse"
)
OUTPUTS = ("node_out", "d_nodes", "d_edges", "grads", "bias_grads")


def kernel(dims, names, *refs):
    r = SimpleNamespace(**dict(zip(names, refs)))
    nx, ny, cells, edges, tile = dims
    nz = nx // 2
    ng = 2 * ny
    ext = cells + 4 * W
    owned = cells // ny
    tiles = edges // tile
    i, j = lax.axis_index("gx"), lax.axis_index("gy")
    core, z = lax.rem(i, 2), lax.div(i, 2)
    g = core * ny + j
    up, down = lax.rem(i + nx - 1, nx), lax.rem(i + 1, nx)
    left, right = lax.rem(j + ny - 1, ny), lax.rem(j + 1, ny)
    across = lax.rem(i + nx - 1 + 2 * core, nx)

    barrier = pltpu.get_barrier_semaphore()

    def greet(gx, gy):
        pl.semaphore_signal(barrier, inc=1, device_id=(gx, gy), device_id_type=MESH)

    def each(count, me, action):
        def step(d, c):
            action(lax.rem(me + d, count))
            return c

        lax.fori_loop(1, count, step, 0)

    greet(across, j)
    loads = {
        name: pltpu.make_async_copy(
            getattr(r, name + "_in"), getattr(r, name), r.load_sem.at[k]
        )
        for k, name in enumerate(ORDER)
    }
    for name in ORDER:
        loads[name].start()
    each(ng, g, lambda t: greet(2 * z + lax.div(t, ny), lax.rem(t, ny)))
    each(nz, z, lambda t: greet(2 * t + core, j))

    def exchange(count, me, place):
        def copy(src, dst, sems, slot, target):
            return pltpu.make_async_remote_copy(
                src_ref=src,
                dst_ref=dst.at[slot],
                send_sem=sems.at[0, target],
                recv_sem=sems.at[1, slot],
                device_id=place(target),
                device_id_type=MESH,
            )

        def scatter(src, dst, sems):
            dst[me] = src[me]
            each(count, me, lambda t: copy(src.at[t], dst, sems, me, t).start())

        def gather(buf, sems):
            each(count, me, lambda t: copy(buf.at[me], buf, sems, me, t).start())

        def arrive(buf, sems):
            each(count, me, lambda t: copy(buf.at[t], buf, sems, t, t).wait_recv())

        def sent(buf, sems):
            each(count, me, lambda t: copy(buf.at[me], buf, sems, me, t).wait_send())

        return SimpleNamespace(scatter=scatter, gather=gather, arrive=arrive, sent=sent)

    row = exchange(ny, j, lambda t: (i, t))
    column = exchange(nz, z, lambda t: (2 * t + core, j))
    layer = exchange(ng, g, lambda t: (2 * z + lax.div(t, ny), lax.rem(t, ny)))

    def slots_sum(ref):
        return jnp.sum(ref[...].astype(F32), axis=0)

    def reduce_stages(src, into, zbuf, everything, sums, sems):
        rs_sem, z_sem, ag_sem = sems

        def start():
            layer.scatter(src, into, rs_sem)

        def to_column():
            layer.arrive(into, rs_sem)
            zbuf[z] = slots_sum(into).astype(BF16)
            column.gather(zbuf, z_sem)

        def to_layer():
            column.arrive(zbuf, z_sem)
            sums[...] = slots_sum(zbuf)
            everything[g] = sums[...].astype(BF16)
            layer.gather(everything, ag_sem)

        def finish():
            layer.arrive(everything, ag_sem)

        def sent():
            layer.sent(into, rs_sem)
            column.sent(zbuf, z_sem)
            layer.sent(everything, ag_sem)

        return SimpleNamespace(
            start=start, to_column=to_column, to_layer=to_layer, finish=finish, sent=sent
        )

    a_stage = reduce_stages(
        r.a_src, r.a_in, r.a_z, r.a_all, r.a_sum, (r.a_rs_sem, r.a_z_sem, r.a_ag_sem)
    )
    b_stage = reduce_stages(
        r.b_src, r.b_in, r.b_z, r.b_all, r.b_sum, (r.b_rs_sem, r.b_z_sem, r.b_ag_sem)
    )

    def halo_copies(src, dst, sems):
        targets = ((up, j), (down, j), (i, left), (i, right))
        return [
            pltpu.make_async_remote_copy(
                src_ref=src.at[k],
                dst_ref=dst.at[k ^ 1],
                send_sem=sems.at[0, k],
                recv_sem=sems.at[1, k ^ 1],
                device_id=targets[k],
                device_id_type=MESH,
            )
            for k in range(4)
        ]

    present = (i > 0, i < nx - 1, j > 0, j < ny - 1)

    half_e, half_c = ext // 2, cells // 2

    def folded(line, half):
        return jnp.where(line >= half, line - half, line)

    def pick_half(high, both):
        return jnp.where(high, both[W:, :], both[:W, :])

    def halves(high, value):
        low = jnp.where(high, 0.0, value)
        return jnp.concatenate([low, value - low], axis=0).astype(BF16)

    def unfold(pairs):
        return jnp.concatenate([pairs[:, :W], pairs[:, W:]], axis=0)

    def fold_t(table, half):
        return jnp.concatenate([table[:, :half], table[:, half:]], axis=0)

    def to_coarse(value):
        low = jnp.where(r.own_high[...] > 0.5, 0.0, value)
        pairs = jnp.concatenate([low, value - low], axis=1).astype(BF16)
        return unfold(dot(r.own_t[...], pairs)).astype(BF16).reshape(ny, owned, W)

    def from_coarse(table):
        flat = table.reshape(cells, W)
        pairs = jnp.concatenate([flat[:half_c], flat[half_c:]], axis=1)
        both = dot(r.own_n[...], pairs)
        return jnp.where(r.own_high[...] > 0.5, both[:, W:], both[:, :W])

    def hot(line, count):
        parts = []
        for a in range(count // BLOCK):
            inside = jnp.where(lax.shift_right_arithmetic(line, 8) == a, line & 255, -1)
            inside = inside.astype(F32).astype(BF16)
            same = r.iota[:, : line.shape[1]] == inside
            parts.append(jnp.where(same, jnp.ones((), BF16), jnp.zeros((), BF16)))
        return jnp.concatenate(parts, axis=0)

    eye = (
        lax.broadcasted_iota(I32, (W, W), 0) == lax.broadcasted_iota(I32, (W, W), 1)
    ).astype(F32).astype(BF16)

    def turned(block):
        return right_t(eye, block).astype(BF16)

    r.iota[...] = lax.broadcasted_iota(I32, r.iota.shape, 0).astype(F32).astype(BF16)
    loads["slist"].wait()
    r.hot_list[...] = hot(lane_row(r.slist, 0, 4), cells)
    loads["nodes"].wait()
    r.ext_t[:, :cells] = turned(r.nodes[...])
    picked = dot(r.ext_t[:, :cells], r.hot_list[...]).astype(BF16)
    for k in range(4):
        r.pick[k] = picked[:, k * W : (k + 1) * W]
    loads["owner"].wait()
    r.own_t[...] = hot(folded(lane_row(r.owner, 0, cells // W), half_c), half_c)
    for q in range(cells // W):
        at = jnp.broadcast_to(r.owner[q : q + 1, :].astype(F32), (W, W)).T
        r.own_at[q * W : (q + 1) * W, :] = at
    r.own_high[...] = jnp.where(r.own_at[...] >= float(half_c), 1.0, 0.0)
    loads["cot"].wait()
    r.cot_src[...] = to_coarse(r.cot[...].astype(F32))

    pl.semaphore_wait(barrier, ng + nz - 1)
    halo_out = halo_copies(r.pick, r.halo, r.halo_sem)
    for copy in halo_out:
        copy.start()
    row.scatter(r.cot_src, r.cot_got, r.cot_sem)

    loads["snd"].wait()
    loads["rcv"].wait()
    per = tile // W
    alive = r.live[0]

    def sender_row(t):
        return lane_row(r.snd, t * per, per)

    def receiver_row(t):
        place = t * tile + lax.broadcasted_iota(I32, (1, tile), 1)
        return jnp.where(place < alive, lane_row(r.rcv, t * per, per), -1)

    def high_s(t):
        return jnp.broadcast_to(sender_row(t), (W, tile)) >= half_e

    def high_r(t):
        return jnp.broadcast_to(receiver_row(t), (W, tile)) >= half_c

    def mark(t, c):
        r.marks[t, :half_e, :] = hot(folded(sender_row(t), half_e), half_e)
        r.marks[t, half_e:, :] = hot(folded(receiver_row(t), half_c), half_c)
        return c

    lax.fori_loop(0, tiles, mark, 0)

    loads["w_edge"].wait()
    loads["bias"].wait()
    ws_t, wr_t, we_t = [turned(r.w_edge[k]) for k in range(3)]
    b_col = jnp.broadcast_to(r.bias[0:1, :], (W, W)).T
    r.table_t[:, half_e:] = fold_t(dot(wr_t, r.ext_t[:, :cells]), half_c).astype(BF16)
    loads["feat"].wait()
    for copy in halo_out:
        copy.wait_recv()
    for k in range(4):
        r.ext_t[:, cells + k * W : cells + (k + 1) * W] = jnp.where(
            present[k], r.halo[k].astype(F32), 0.0
        ).astype(BF16)
    r.table_t[:, :half_e] = fold_t(
        dot(ws_t, r.ext_t[...]) + jnp.concatenate([b_col] * (ext // W), axis=1), half_e
    ).astype(BF16)

    r.h_acc[...] = jnp.zeros_like(r.h_acc)

    def edge_rows(t):
        return pl.ds(pl.multiple_of(t * tile, tile), tile)

    def forward(t, c):
        above = high_r(t)
        pre = (
            pick_half(high_s(t), dot(r.table_t[:, :half_e], r.marks[t, :half_e, :]))
            + pick_half(above, dot(r.table_t[:, half_e:], r.marks[t, half_e:, :]))
            + right_t(we_t, r.feat[edge_rows(t), :])
        )
        sigma = sigmoid(pre)
        r.slopes[t] = slope(pre, sigma)
        r.h_acc[...] += right_t(r.marks[t, half_e:, :], halves(above, pre * sigma))
        return c

    lax.fori_loop(0, tiles, forward, 0)

    loads["w_node"].wait()
    loads["w_coarse"].wait()
    r.hb[...] = unfold(r.h_acc[...]).astype(BF16)
    r.agg[...] = dot(r.hb[...], r.w_edge[3]).astype(BF16)
    pre_node = dot(r.nodes[...], r.w_node[0]) + dot(r.agg[...], r.w_node[1]) + r.bias[1:2, :]
    sigma = sigmoid(pre_node)
    r.node_slope[...] = slope(pre_node, sigma)
    r.hid[...] = (pre_node * sigma).astype(BF16)
    r.fine[...] = r.nodes[...].astype(F32) + dot(r.hid[...], r.w_node[2])
    r.fine_src[...] = to_coarse(r.fine[...])
    row.scatter(r.fine_src, r.fine_got, r.fine_sem)

    lanes = lax.broadcasted_iota(I32, (cells, W), 1).astype(F32)
    at = r.own_at[...] - float(half_c) * r.own_high[...]
    r.own_n[...] = jnp.concatenate(
        [jnp.where(at == lanes + float(k * W), 1.0, 0.0).astype(BF16) for k in range(half_c // W)],
        axis=1,
    )
    agg_t, hid_t, hb_t = turned(r.agg[...]), turned(r.hid[...]), turned(r.hb[...])

    row.arrive(r.cot_got, r.cot_sem)
    d_coarse = slots_sum(r.cot_got).astype(BF16)
    d_hidden = right_t(d_coarse, r.w_coarse[1])
    row.arrive(r.fine_got, r.fine_sem)
    coarse_bf = (0.0625 * slots_sum(r.fine_got)).astype(BF16)
    pre_coarse = dot(coarse_bf, r.w_coarse[0]) + r.bias[2:3, :]
    sigma = sigmoid(pre_coarse)
    coarse_hid = (pre_coarse * sigma).astype(BF16)
    d_pre_c = d_hidden * slope(pre_coarse, sigma)
    d_pre_c_bf = d_pre_c.astype(BF16)
    r.d_coarse_all[j] = right_t(d_pre_c_bf, r.w_coarse[0]).astype(BF16)
    row.gather(r.d_coarse_all, r.d_coarse_sem)
    r.coarse_all[j] = dot(coarse_hid, r.w_coarse[1]).astype(BF16)
    row.gather(r.coarse_all, r.coarse_sem)
    g_v1 = dot(turned(coarse_bf), d_pre_c_bf)
    g_v2 = dot(turned(coarse_hid), d_coarse)
    b_own = r.b_src.shape[1]
    a_own = 6 * W // ng
    share = 3 * W // ng
    r.bias_rows[...] = jnp.zeros_like(r.bias_rows)
    r.bias_rows[share + 2 : share + 3, :] = jnp.sum(d_pre_c, axis=0, keepdims=True)
    row.arrive(r.d_coarse_all, r.d_coarse_sem)

    d_fine = r.cot[...].astype(F32) + 0.0625 * from_coarse(r.d_coarse_all[...])
    d_fine_bf = d_fine.astype(BF16)
    d_pre_n = right_t(d_fine_bf, r.w_node[2]) * r.node_slope[...]
    d_pre_n_bf = d_pre_n.astype(BF16)
    r.bias_rows[share + 1 : share + 2, :] = jnp.sum(d_pre_n, axis=0, keepdims=True)
    r.d_part[...] = d_fine
    r.d_pre_n[...] = d_pre_n_bf
    d_agg = right_t(d_pre_n_bf, r.w_node[1]).astype(BF16)
    r.table_t[:, half_e:] = fold_t(right_t(r.w_edge[3], d_agg), half_c).astype(BF16)
    early = jnp.concatenate(
        [
            dot(hb_t, d_agg),
            dot(r.ext_t[:, :cells], d_pre_n_bf),
            dot(agg_t, d_pre_n_bf),
            dot(hid_t, d_fine_bf),
            g_v1,
            g_v2,
        ],
        axis=0,
    ).reshape(ng, a_own, W)
    spare = r.a_src.shape[1] - a_own
    if spare:
        early = jnp.concatenate([early, jnp.zeros((ng, spare, W), F32)], axis=1)
    r.a_src[...] = early.astype(BF16)
    a_stage.start()

    r.s_acc[...] = jnp.zeros_like(r.s_acc)
    r.r_acc[...] = jnp.zeros_like(r.r_acc)
    r.we_acc[...] = jnp.zeros_like(r.we_acc)

    def backward(t, c):
        above = high_r(t)
        got = pick_half(above, dot(r.table_t[:, half_e:], r.marks[t, half_e:, :]))
        d_pre = got * r.slopes[t]
        d_pre_bf = d_pre.astype(BF16)
        r.d_pre[t] = d_pre_bf
        r.s_acc[...] += right_t(r.marks[t, :half_e, :], halves(high_s(t), d_pre))
        r.r_acc[...] += right_t(r.marks[t, half_e:, :], halves(above, d_pre))
        r.we_acc[...] += dot(d_pre_bf, r.feat[edge_rows(t), :])
        return c

    def edge_out(t, c):
        r.d_edges[edge_rows(t), :] = dot(r.w_edge[2], r.d_pre[t]).T.astype(BF16)
        return c

    leaving = []

    def leave(k, src, dst):
        leaving.append(pltpu.make_async_copy(src, dst, r.out_sem.at[k]))
        leaving[-1].start()

    half = tiles // 2
    lax.fori_loop(0, half, backward, 0)
    a_stage.to_column()
    lax.fori_loop(half, tiles, backward, 0)
    a_stage.to_layer()

    s_bf = unfold(r.s_acc[...]).astype(BF16)
    r_sum = unfold(r.r_acc[...])
    r_bf = r_sum.astype(BF16)
    r.back_src[...] = right_t(s_bf[cells:, :], r.w_edge[0]).astype(BF16).reshape(4, W, W)
    back_out = halo_copies(r.back_src, r.back_got, r.back_sem)
    for copy in back_out:
        copy.start()
    r.bias_rows[share : share + 1, :] = jnp.sum(r_sum, axis=0, keepdims=True)
    r.b_flat[: 3 * W, :] = jnp.concatenate(
        [dot(r.ext_t[...], s_bf), dot(r.ext_t[:, :cells], r_bf), r.we_acc[...].T], axis=0
    )
    r.b_flat[3 * W :, :] = jnp.zeros((b_own, W), F32)
    inner = lax.broadcasted_iota(I32, (b_own, W), 0) < share
    for k in range(ng):
        part = r.b_flat[k * share : k * share + b_own, :]
        r.b_src[k] = jnp.where(inner, part, r.bias_rows[...]).astype(BF16)
    b_stage.start()
    r.d_part[...] = (
        r.d_part[...]
        + right_t(r.d_pre_n[...], r.w_node[0])
        + right_t(s_bf[:cells, :], r.w_edge[0])
        + right_t(r_bf, r.w_edge[1])
    )
    for copy in back_out:
        copy.wait_recv()
    returned = jnp.concatenate(
        [jnp.where(present[k], r.back_got[k].astype(F32), 0.0) for k in range(4)], axis=0
    ).astype(BF16)
    r.d_nodes[...] = (r.d_part[...] + dot(r.hot_list[...], returned)).astype(BF16)
    leave(0, r.d_nodes, r.d_nodes_out)
    b_stage.to_column()
    lax.fori_loop(0, half, edge_out, 0)
    first, second = pl.ds(0, half * tile), pl.ds(half * tile, (tiles - half) * tile)
    leave(1, r.d_edges.at[first], r.d_edges_out.at[first])
    row.arrive(r.coarse_all, r.coarse_sem)
    r.node_out[...] = (r.fine[...] + from_coarse(r.coarse_all[...])).astype(BF16)
    leave(2, r.node_out, r.node_out_out)
    b_stage.to_layer()
    lax.fori_loop(half, tiles, edge_out, 0)
    leave(3, r.d_edges.at[second], r.d_edges_out.at[second])
    r.bias_grads[...] = r.b_sum[share : share + 3, :]
    leave(4, r.bias_grads, r.bias_grads_out)
    a_stage.finish()
    r.grads[3 * W :, :] = r.a_all[...].astype(F32)[:, :a_own, :].reshape(6 * W, W)
    late, soon = pl.ds(0, 3 * W), pl.ds(3 * W, 6 * W)
    leave(5, r.grads.at[soon], r.grads_out.at[soon])
    row.sent(r.cot_got, r.cot_sem)
    row.sent(r.fine_got, r.fine_sem)
    row.sent(r.coarse_all, r.coarse_sem)
    row.sent(r.d_coarse_all, r.d_coarse_sem)
    for copy in halo_out + back_out:
        copy.wait_send()
    a_stage.sent()
    b_stage.finish()
    for k in range(ng):
        r.grads[k * share : (k + 1) * share, :] = r.b_all[k].astype(F32)[:share, :]
    leave(6, r.grads.at[late], r.grads_out.at[late])
    b_stage.sent()
    for copy in leaving:
        copy.wait()


def body(
    dims,
    nodes,
    edge_feat,
    senders,
    receivers,
    send_lists,
    owner,
    edge_live,
    cotangent,
    w_edge,
    w_node,
    w_coarse,
    biases,
):
    nx, ny, cells, edges, tile = dims
    nz = nx // 2
    ng = 2 * ny
    ext = cells + 4 * W
    owned = cells // ny
    a_rows = -(-(6 * W // ng) // 16) * 16
    b_rows = -(-(3 * W // ng + 3) // 16) * 16
    operands = dict(
        nodes=nodes,
        feat=edge_feat,
        snd=senders.reshape(edges // W, W),
        rcv=receivers.reshape(edges // W, W),
        slist=send_lists.reshape(4, W),
        owner=owner.reshape(cells // W, W),
        cot=cotangent,
        w_edge=w_edge,
        w_node=w_node,
        w_coarse=w_coarse,
        bias=biases,
    )
    shapes = (
        jax.ShapeDtypeStruct((cells, W), BF16),
        jax.ShapeDtypeStruct((cells, W), BF16),
        jax.ShapeDtypeStruct((edges, W), BF16),
        jax.ShapeDtypeStruct((9 * W, W), F32),
        jax.ShapeDtypeStruct((3, W), F32),
    )
    scratch = {name: pltpu.VMEM(operands[name].shape, operands[name].dtype) for name in INPUTS}
    scratch |= {name: pltpu.VMEM(s.shape, s.dtype) for name, s in zip(OUTPUTS, shapes)}
    scratch |= dict(
        iota=pltpu.VMEM((BLOCK, max(cells, tile)), BF16),
        ext_t=pltpu.VMEM((W, ext), BF16),
        table_t=pltpu.VMEM((2 * W, (ext + cells) // 2), BF16),
        marks=pltpu.VMEM((edges // tile, (ext + cells) // 2, tile), BF16),
        hot_list=pltpu.VMEM((cells, 4 * W), BF16),
        own_t=pltpu.VMEM((cells // 2, cells), BF16),
        own_n=pltpu.VMEM((cells, cells // 2), BF16),
        own_at=pltpu.VMEM((cells, W), F32),
        own_high=pltpu.VMEM((cells, W), F32),
        pick=pltpu.VMEM((4, W, W), BF16),
        halo=pltpu.VMEM((4, W, W), BF16),
        slopes=pltpu.VMEM((edges // tile, W, tile), F32),
        d_pre=pltpu.VMEM((edges // tile, W, tile), BF16),
        h_acc=pltpu.VMEM((cells // 2, 2 * W), F32),
        s_acc=pltpu.VMEM((ext // 2, 2 * W), F32),
        r_acc=pltpu.VMEM((cells // 2, 2 * W), F32),
        we_acc=pltpu.VMEM((W, W), F32),
        fine=pltpu.VMEM((cells, W), F32),
        node_slope=pltpu.VMEM((cells, W), F32),
        d_part=pltpu.VMEM((cells, W), F32),
        hb=pltpu.VMEM((cells, W), BF16),
        agg=pltpu.VMEM((cells, W), BF16),
        hid=pltpu.VMEM((cells, W), BF16),
        cot_src=pltpu.VMEM((ny, owned, W), BF16),
        cot_got=pltpu.VMEM((ny, owned, W), BF16),
        fine_src=pltpu.VMEM((ny, owned, W), BF16),
        fine_got=pltpu.VMEM((ny, owned, W), BF16),
        coarse_all=pltpu.VMEM((ny, owned, W), BF16),
        d_coarse_all=pltpu.VMEM((ny, owned, W), BF16),
        d_pre_n=pltpu.VMEM((cells, W), BF16),
        back_src=pltpu.VMEM((4, W, W), BF16),
        back_got=pltpu.VMEM((4, W, W), BF16),
        bias_rows=pltpu.VMEM((b_rows, W), F32),
        b_flat=pltpu.VMEM((3 * W + b_rows, W), F32),
        load_sem=pltpu.SemaphoreType.DMA((len(INPUTS),)),
        halo_sem=pltpu.SemaphoreType.DMA((2, 4)),
        back_sem=pltpu.SemaphoreType.DMA((2, 4)),
        cot_sem=pltpu.SemaphoreType.DMA((2, ny)),
        fine_sem=pltpu.SemaphoreType.DMA((2, ny)),
        coarse_sem=pltpu.SemaphoreType.DMA((2, ny)),
        d_coarse_sem=pltpu.SemaphoreType.DMA((2, ny)),
        out_sem=pltpu.SemaphoreType.DMA((7,)),
    )
    for name, rows in (("a", a_rows), ("b", b_rows)):
        scratch |= {
            name + "_src": pltpu.VMEM((ng, rows, W), BF16),
            name + "_in": pltpu.VMEM((ng, rows, W), BF16),
            name + "_z": pltpu.VMEM((nz, rows, W), BF16),
            name + "_all": pltpu.VMEM((ng, rows, W), BF16),
            name + "_sum": pltpu.VMEM((rows, W), F32),
            name + "_rs_sem": pltpu.SemaphoreType.DMA((2, ng)),
            name + "_z_sem": pltpu.SemaphoreType.DMA((2, nz)),
            name + "_ag_sem": pltpu.SemaphoreType.DMA((2, ng)),
        }
    names = tuple(name + "_in" for name in INPUTS) + ("live",)
    names += tuple(name + "_out" for name in OUTPUTS) + tuple(scratch)
    smem = pl.BlockSpec(memory_space=pltpu.SMEM)
    hbm = pl.BlockSpec(memory_space=pltpu.HBM)
    outs = pl.pallas_call(
        functools.partial(kernel, dims, names),
        out_shape=shapes,
        in_specs=[hbm] * len(INPUTS) + [smem],
        out_specs=(hbm,) * 5,
        scratch_shapes=list(scratch.values()),
        compiler_params=pltpu.CompilerParams(
            collective_id=0, has_side_effects=True, vmem_limit_bytes=63 * 1024 * 1024
        ),
        cost_estimate=pl.CostEstimate(
            flops=2 * edges * W * (2 * ext + 4 * cells + 4 * W),
            bytes_accessed=2 * W * (2 * edges + 4 * cells),
            transcendentals=edges * W,
        ),
        name="mesh_step",
    )(*[operands[name] for name in INPUTS], edge_live)
    node_out, d_nodes, d_edges, grads, bias_grads = outs
    return node_out, d_nodes, d_edges, grads.reshape(9, W, W), bias_grads


def solution(mesh, cells=1024, edges=4096, tile=1024):
    both = ("gx", "gy")
    dims = (mesh.shape["gx"], mesh.shape["gy"], cells, edges, tile)
    in_specs = (
        P(both, None),
        P(both, None),
        P(both),
        P(both),
        P(both, None, None),
        P(both),
        P(both),
        P(both, None),
        P(),
        P(),
        P(),
        P(),
    )
    out_specs = (P(both, None), P(both, None), P(both, None), P(), P())
    return jax.shard_map(
        functools.partial(body, dims),
        mesh=mesh,
        in_specs=in_specs,
        out_specs=out_specs,
        check_vma=False,
    )
```

```python
import functools
from types import SimpleNamespace

import jax
import jax.numpy as jnp
from jax import lax
from jax.experimental import pallas as pl
from jax.experimental.pallas import tpu as pltpu
from jax.sharding import PartitionSpec as P

F32, BF16, I32 = jnp.float32, jnp.bfloat16, jnp.int32
W = 128
BLOCK = 256
MESH = pl.DeviceIdType.MESH


def dot(left, right):
    return jnp.dot(left, right, preferred_element_type=F32)


def right_t(left, right):
    return lax.dot_general(left, right, (((1,), (1,)), ((), ())), preferred_element_type=F32)


def sigmoid(value):
    return 0.5 * jnp.tanh(0.5 * value) + 0.5


def slope(value, sigma):
    return sigma * (1.0 + value * (1.0 - sigma))


def lane_row(ref, first, count):
    return jnp.concatenate([ref[pl.ds(first + q, 1), :] for q in range(count)], axis=1)


INPUTS = (
    "nodes", "feat", "snd", "rcv", "slist", "owner", "cot", "w_edge", "w_node", "w_coarse", "bias"
)
ORDER = (
    "slist", "nodes", "owner", "cot", "snd", "rcv", "w_edge", "bias", "feat", "w_node", "w_coarse"
)
OUTPUTS = ("node_out", "d_nodes", "d_edges", "grads", "bias_grads")


def kernel(dims, names, *refs):
    r = SimpleNamespace(**dict(zip(names, refs)))
    nx, ny, cells, edges, tile = dims
    nz = nx // 2
    ng = 2 * ny
    ext = cells + 4 * W
    owned = cells // ny
    tiles = edges // tile
    i, j = lax.axis_index("gx"), lax.axis_index("gy")
    core, z = lax.rem(i, 2), lax.div(i, 2)
    g = core * ny + j
    up, down = lax.rem(i + nx - 1, nx), lax.rem(i + 1, nx)
    left, right = lax.rem(j + ny - 1, ny), lax.rem(j + 1, ny)
    across = lax.rem(i + nx - 1 + 2 * core, nx)

    barrier = pltpu.get_barrier_semaphore()

    def greet(gx, gy):
        pl.semaphore_signal(barrier, inc=1, device_id=(gx, gy), device_id_type=MESH)

    def each(count, me, action):
        def step(d, c):
            action(lax.rem(me + d, count))
            return c

        lax.fori_loop(1, count, step, 0)

    greet(across, j)
    loads = {
        name: pltpu.make_async_copy(
            getattr(r, name + "_in"), getattr(r, name), r.load_sem.at[k]
        )
        for k, name in enumerate(ORDER)
    }
    for name in ORDER:
        loads[name].start()
    each(ng, g, lambda t: greet(2 * z + lax.div(t, ny), lax.rem(t, ny)))
    each(nz, z, lambda t: greet(2 * t + core, j))

    def exchange(count, me, place):
        def copy(src, dst, sems, target):
            return pltpu.make_async_remote_copy(
                src_ref=src,
                dst_ref=dst,
                send_sem=sems.at[0],
                recv_sem=sems.at[1],
                device_id=place(target),
                device_id_type=MESH,
            )

        def scatter(src, dst, sems):
            dst[me] = src[me]
            each(count, me, lambda t: copy(src.at[t], dst.at[me], sems, t).start())

        def gather(buf, sems):
            each(count, me, lambda t: copy(buf.at[me], buf.at[me], sems, t).start())

        def every(buf, sems):
            others = buf.at[pl.ds(0, count - 1)]
            return copy(others, others, sems, lax.rem(me + 1, count))

        def arrive(buf, sems):
            every(buf, sems).wait_recv()

        def sent(buf, sems):
            every(buf, sems).wait_send()

        return SimpleNamespace(scatter=scatter, gather=gather, arrive=arrive, sent=sent)

    row = exchange(ny, j, lambda t: (i, t))
    column = exchange(nz, z, lambda t: (2 * t + core, j))
    layer = exchange(ng, g, lambda t: (2 * z + lax.div(t, ny), lax.rem(t, ny)))

    def slots_sum(ref):
        return jnp.sum(ref[...].astype(F32), axis=0)

    def reduce_stages(src, into, zbuf, everything, sums, sems):
        rs_sem, z_sem, ag_sem = sems

        def start():
            layer.scatter(src, into, rs_sem)

        def to_column():
            layer.arrive(into, rs_sem)
            zbuf[z] = slots_sum(into).astype(BF16)
            column.gather(zbuf, z_sem)

        def to_layer():
            column.arrive(zbuf, z_sem)
            sums[...] = slots_sum(zbuf)
            everything[g] = sums[...].astype(BF16)
            layer.gather(everything, ag_sem)

        def finish():
            layer.arrive(everything, ag_sem)

        def sent():
            layer.sent(into, rs_sem)
            column.sent(zbuf, z_sem)
            layer.sent(everything, ag_sem)

        return SimpleNamespace(
            start=start, to_column=to_column, to_layer=to_layer, finish=finish, sent=sent
        )

    a_stage = reduce_stages(
        r.a_src, r.a_in, r.a_z, r.a_all, r.a_sum, (r.a_rs_sem, r.a_z_sem, r.a_ag_sem)
    )
    b_stage = reduce_stages(
        r.b_src, r.b_in, r.b_z, r.b_all, r.b_sum, (r.b_rs_sem, r.b_z_sem, r.b_ag_sem)
    )

    def halo_copies(src, dst, sems):
        targets = ((up, j), (down, j), (i, left), (i, right))
        return [
            pltpu.make_async_remote_copy(
                src_ref=src.at[k],
                dst_ref=dst.at[k ^ 1],
                send_sem=sems.at[0, k],
                recv_sem=sems.at[1, k ^ 1],
                device_id=targets[k],
                device_id_type=MESH,
            )
            for k in range(4)
        ]

    present = (i > 0, i < nx - 1, j > 0, j < ny - 1)

    half_e, half_c = ext // 2, cells // 2

    def folded(line, half):
        return jnp.where(line >= half, line - half, line)

    def pick_half(high, both):
        return jnp.where(high, both[W:, :], both[:W, :])

    def halves(high, value):
        low = jnp.where(high, 0.0, value)
        return jnp.concatenate([low, value - low], axis=0).astype(BF16)

    def unfold(pairs):
        return jnp.concatenate([pairs[:, :W], pairs[:, W:]], axis=0)

    def fold_t(table, half):
        return jnp.concatenate([table[:, :half], table[:, half:]], axis=0)

    def to_coarse(value):
        low = jnp.where(r.own_high[...] > 0.5, 0.0, value)
        pairs = jnp.concatenate([low, value - low], axis=1).astype(BF16)
        return unfold(dot(r.own_t[...], pairs)).astype(BF16).reshape(ny, owned, W)

    def from_coarse(table):
        flat = table.reshape(cells, W)
        pairs = jnp.concatenate([flat[:half_c], flat[half_c:]], axis=1)
        both = dot(r.own_n[...], pairs)
        return jnp.where(r.own_high[...] > 0.5, both[:, W:], both[:, :W])

    def hot(line, count):
        parts = []
        for a in range(count // BLOCK):
            inside = jnp.where(lax.shift_right_arithmetic(line, 8) == a, line & 255, -1)
            inside = inside.astype(F32).astype(BF16)
            same = r.iota[:, : line.shape[1]] == inside
            parts.append(jnp.where(same, jnp.ones((), BF16), jnp.zeros((), BF16)))
        return jnp.concatenate(parts, axis=0)

    eye = (
        lax.broadcasted_iota(I32, (W, W), 0) == lax.broadcasted_iota(I32, (W, W), 1)
    ).astype(F32).astype(BF16)

    def turned(block):
        return right_t(eye, block).astype(BF16)

    r.iota[...] = lax.broadcasted_iota(I32, r.iota.shape, 0).astype(F32).astype(BF16)
    loads["slist"].wait()
    r.hot_list[...] = hot(lane_row(r.slist, 0, 4), cells)
    loads["nodes"].wait()
    r.ext_t[:, :cells] = turned(r.nodes[...])
    picked = dot(r.ext_t[:, :cells], r.hot_list[...]).astype(BF16)
    for k in range(4):
        r.pick[k] = picked[:, k * W : (k + 1) * W]
    loads["owner"].wait()
    r.own_t[...] = hot(folded(lane_row(r.owner, 0, cells // W), half_c), half_c)
    for q in range(cells // W):
        at = jnp.broadcast_to(r.owner[q : q + 1, :].astype(F32), (W, W)).T
        r.own_at[q * W : (q + 1) * W, :] = at
    r.own_high[...] = jnp.where(r.own_at[...] >= float(half_c), 1.0, 0.0)
    loads["cot"].wait()
    r.cot_src[...] = to_coarse(r.cot[...].astype(F32))

    pl.semaphore_wait(barrier, ng + nz - 1)
    halo_out = halo_copies(r.pick, r.halo, r.halo_sem)
    for copy in halo_out:
        copy.start()
    row.scatter(r.cot_src, r.cot_got, r.cot_sem)

    loads["snd"].wait()
    loads["rcv"].wait()
    per = tile // W
    alive = r.live[0]

    def sender_row(t):
        return lane_row(r.snd, t * per, per)

    def receiver_row(t):
        place = t * tile + lax.broadcasted_iota(I32, (1, tile), 1)
        return jnp.where(place < alive, lane_row(r.rcv, t * per, per), -1)

    def high_s(t):
        return jnp.broadcast_to(sender_row(t), (W, tile)) >= half_e

    def high_r(t):
        return jnp.broadcast_to(receiver_row(t), (W, tile)) >= half_c

    def mark(t, c):
        r.marks[t, :half_e, :] = hot(folded(sender_row(t), half_e), half_e)
        r.marks[t, half_e:, :] = hot(folded(receiver_row(t), half_c), half_c)
        return c

    lax.fori_loop(0, tiles, mark, 0)

    loads["w_edge"].wait()
    loads["bias"].wait()
    ws_t, wr_t, we_t = [turned(r.w_edge[k]) for k in range(3)]
    b_col = jnp.broadcast_to(r.bias[0:1, :], (W, W)).T
    r.table_t[:, half_e:] = fold_t(dot(wr_t, r.ext_t[:, :cells]), half_c).astype(BF16)
    loads["feat"].wait()
    for copy in halo_out:
        copy.wait_recv()
    for k in range(4):
        r.ext_t[:, cells + k * W : cells + (k + 1) * W] = jnp.where(
            present[k], r.halo[k].astype(F32), 0.0
        ).astype(BF16)
    r.table_t[:, :half_e] = fold_t(
        dot(ws_t, r.ext_t[...]) + jnp.concatenate([b_col] * (ext // W), axis=1), half_e
    ).astype(BF16)

    r.h_acc[...] = jnp.zeros_like(r.h_acc)

    def edge_rows(t):
        return pl.ds(pl.multiple_of(t * tile, tile), tile)

    def forward(t, c):
        above = high_r(t)
        pre = (
            pick_half(high_s(t), dot(r.table_t[:, :half_e], r.marks[t, :half_e, :]))
            + pick_half(above, dot(r.table_t[:, half_e:], r.marks[t, half_e:, :]))
            + right_t(we_t, r.feat[edge_rows(t), :])
        )
        sigma = sigmoid(pre)
        r.slopes[t] = slope(pre, sigma)
        r.h_acc[...] += right_t(r.marks[t, half_e:, :], halves(above, pre * sigma))
        return c

    lax.fori_loop(0, tiles, forward, 0)

    loads["w_node"].wait()
    loads["w_coarse"].wait()
    r.hb[...] = unfold(r.h_acc[...]).astype(BF16)
    r.agg[...] = dot(r.hb[...], r.w_edge[3]).astype(BF16)
    pre_node = dot(r.nodes[...], r.w_node[0]) + dot(r.agg[...], r.w_node[1]) + r.bias[1:2, :]
    sigma = sigmoid(pre_node)
    r.node_slope[...] = slope(pre_node, sigma)
    r.hid[...] = (pre_node * sigma).astype(BF16)
    r.fine[...] = r.nodes[...].astype(F32) + dot(r.hid[...], r.w_node[2])
    r.fine_src[...] = to_coarse(r.fine[...])
    row.scatter(r.fine_src, r.fine_got, r.fine_sem)

    lanes = lax.broadcasted_iota(I32, (cells, W), 1).astype(F32)
    at = r.own_at[...] - float(half_c) * r.own_high[...]
    r.own_n[...] = jnp.concatenate(
        [jnp.where(at == lanes + float(k * W), 1.0, 0.0).astype(BF16) for k in range(half_c // W)],
        axis=1,
    )
    agg_t, hid_t, hb_t = turned(r.agg[...]), turned(r.hid[...]), turned(r.hb[...])

    row.arrive(r.cot_got, r.cot_sem)
    d_coarse = slots_sum(r.cot_got).astype(BF16)
    d_hidden = right_t(d_coarse, r.w_coarse[1])
    row.arrive(r.fine_got, r.fine_sem)
    coarse_bf = (0.0625 * slots_sum(r.fine_got)).astype(BF16)
    pre_coarse = dot(coarse_bf, r.w_coarse[0]) + r.bias[2:3, :]
    sigma = sigmoid(pre_coarse)
    coarse_hid = (pre_coarse * sigma).astype(BF16)
    d_pre_c = d_hidden * slope(pre_coarse, sigma)
    d_pre_c_bf = d_pre_c.astype(BF16)
    r.d_coarse_all[j] = right_t(d_pre_c_bf, r.w_coarse[0]).astype(BF16)
    row.gather(r.d_coarse_all, r.d_coarse_sem)
    r.coarse_all[j] = dot(coarse_hid, r.w_coarse[1]).astype(BF16)
    row.gather(r.coarse_all, r.coarse_sem)
    g_v1 = dot(turned(coarse_bf), d_pre_c_bf)
    g_v2 = dot(turned(coarse_hid), d_coarse)
    b_own = r.b_src.shape[1]
    a_own = 6 * W // ng
    share = 3 * W // ng
    r.bias_rows[...] = jnp.zeros_like(r.bias_rows)
    r.bias_rows[share + 2 : share + 3, :] = jnp.sum(d_pre_c, axis=0, keepdims=True)
    row.arrive(r.d_coarse_all, r.d_coarse_sem)

    d_fine = r.cot[...].astype(F32) + 0.0625 * from_coarse(r.d_coarse_all[...])
    d_fine_bf = d_fine.astype(BF16)
    d_pre_n = right_t(d_fine_bf, r.w_node[2]) * r.node_slope[...]
    d_pre_n_bf = d_pre_n.astype(BF16)
    r.bias_rows[share + 1 : share + 2, :] = jnp.sum(d_pre_n, axis=0, keepdims=True)
    r.d_part[...] = d_fine
    r.d_pre_n[...] = d_pre_n_bf
    d_agg = right_t(d_pre_n_bf, r.w_node[1]).astype(BF16)
    r.table_t[:, half_e:] = fold_t(right_t(r.w_edge[3], d_agg), half_c).astype(BF16)
    early = jnp.concatenate(
        [
            dot(hb_t, d_agg),
            dot(r.ext_t[:, :cells], d_pre_n_bf),
            dot(agg_t, d_pre_n_bf),
            dot(hid_t, d_fine_bf),
            g_v1,
            g_v2,
        ],
        axis=0,
    ).reshape(ng, a_own, W)
    spare = r.a_src.shape[1] - a_own
    if spare:
        early = jnp.concatenate([early, jnp.zeros((ng, spare, W), F32)], axis=1)
    r.a_src[...] = early.astype(BF16)
    a_stage.start()

    r.s_acc[...] = jnp.zeros_like(r.s_acc)
    r.r_acc[...] = jnp.zeros_like(r.r_acc)
    r.we_acc[...] = jnp.zeros_like(r.we_acc)

    def backward(t, c):
        above = high_r(t)
        got = pick_half(above, dot(r.table_t[:, half_e:], r.marks[t, half_e:, :]))
        d_pre = got * r.slopes[t]
        d_pre_bf = d_pre.astype(BF16)
        r.d_pre[t] = d_pre_bf
        r.s_acc[...] += right_t(r.marks[t, :half_e, :], halves(high_s(t), d_pre))
        r.r_acc[...] += right_t(r.marks[t, half_e:, :], halves(above, d_pre))
        r.we_acc[...] += dot(d_pre_bf, r.feat[edge_rows(t), :])
        return c

    def edge_out(t, c):
        r.d_edges[edge_rows(t), :] = dot(r.w_edge[2], r.d_pre[t]).T.astype(BF16)
        return c

    leaving = []

    def leave(k, src, dst):
        leaving.append(pltpu.make_async_copy(src, dst, r.out_sem.at[k]))
        leaving[-1].start()

    half = tiles // 2
    lax.fori_loop(0, tiles - 1, backward, 0)
    a_stage.to_column()
    lax.fori_loop(tiles - 1, tiles, backward, 0)

    s_bf = unfold(r.s_acc[...]).astype(BF16)
    r_sum = unfold(r.r_acc[...])
    r_bf = r_sum.astype(BF16)
    r.back_src[...] = right_t(s_bf[cells:, :], r.w_edge[0]).astype(BF16).reshape(4, W, W)
    back_out = halo_copies(r.back_src, r.back_got, r.back_sem)
    for copy in back_out:
        copy.start()
    r.bias_rows[share : share + 1, :] = jnp.sum(r_sum, axis=0, keepdims=True)
    r.b_flat[: 3 * W, :] = jnp.concatenate(
        [dot(r.ext_t[...], s_bf), dot(r.ext_t[:, :cells], r_bf), r.we_acc[...].T], axis=0
    )
    r.b_flat[3 * W :, :] = jnp.zeros((b_own, W), F32)
    inner = lax.broadcasted_iota(I32, (b_own, W), 0) < share
    for k in range(ng):
        part = r.b_flat[k * share : k * share + b_own, :]
        r.b_src[k] = jnp.where(inner, part, r.bias_rows[...]).astype(BF16)
    b_stage.start()
    a_stage.to_layer()
    r.d_part[...] = (
        r.d_part[...]
        + right_t(r.d_pre_n[...], r.w_node[0])
        + right_t(s_bf[:cells, :], r.w_edge[0])
        + right_t(r_bf, r.w_edge[1])
    )
    for copy in back_out:
        copy.wait_recv()
    returned = jnp.concatenate(
        [jnp.where(present[k], r.back_got[k].astype(F32), 0.0) for k in range(4)], axis=0
    ).astype(BF16)
    r.d_nodes[...] = (r.d_part[...] + dot(r.hot_list[...], returned)).astype(BF16)
    leave(0, r.d_nodes, r.d_nodes_out)
    b_stage.to_column()
    lax.fori_loop(0, half, edge_out, 0)
    first, second = pl.ds(0, half * tile), pl.ds(half * tile, (tiles - half) * tile)
    leave(1, r.d_edges.at[first], r.d_edges_out.at[first])
    row.arrive(r.coarse_all, r.coarse_sem)
    r.node_out[...] = (r.fine[...] + from_coarse(r.coarse_all[...])).astype(BF16)
    leave(2, r.node_out, r.node_out_out)
    b_stage.to_layer()
    lax.fori_loop(half, tiles, edge_out, 0)
    leave(3, r.d_edges.at[second], r.d_edges_out.at[second])
    r.bias_grads[...] = r.b_sum[share : share + 3, :]
    leave(4, r.bias_grads, r.bias_grads_out)
    a_stage.finish()
    r.grads[3 * W :, :] = r.a_all[...].astype(F32)[:, :a_own, :].reshape(6 * W, W)
    late, soon = pl.ds(0, 3 * W), pl.ds(3 * W, 6 * W)
    leave(5, r.grads.at[soon], r.grads_out.at[soon])
    row.sent(r.cot_got, r.cot_sem)
    row.sent(r.fine_got, r.fine_sem)
    row.sent(r.coarse_all, r.coarse_sem)
    row.sent(r.d_coarse_all, r.d_coarse_sem)
    for copy in halo_out + back_out:
        copy.wait_send()
    a_stage.sent()
    layer.sent(r.b_in, r.b_rs_sem)
    column.sent(r.b_z, r.b_z_sem)
    b_stage.finish()
    for k in range(ng):
        r.grads[k * share : (k + 1) * share, :] = r.b_all[k].astype(F32)[:share, :]
    leave(6, r.grads.at[late], r.grads_out.at[late])
    layer.sent(r.b_all, r.b_ag_sem)
    for copy in leaving:
        copy.wait()


def settle(cuts, *refs):
    count = len(cuts)
    held, sems = refs[2 * count : 3 * count], refs[3 * count]
    pieces = []
    for k, parts in enumerate(cuts):
        rows = refs[k].shape[0] // parts
        pieces += [(k, pl.ds(p * rows, rows)) for p in range(parts)]
    gets = [
        pltpu.make_async_copy(refs[k].at[here], held[k].at[here], sems.at[0, n])
        for n, (k, here) in enumerate(pieces)
    ]
    puts = [
        pltpu.make_async_copy(held[k].at[here], refs[count + k].at[here], sems.at[1, n])
        for n, (k, here) in enumerate(pieces)
    ]
    for get in gets:
        get.start()
    for get, put in zip(gets, puts):
        get.wait()
        put.start()
    for put in puts:
        put.wait()


def body(
    dims,
    nodes,
    edge_feat,
    senders,
    receivers,
    send_lists,
    owner,
    edge_live,
    cotangent,
    w_edge,
    w_node,
    w_coarse,
    biases,
):
    nx, ny, cells, edges, tile = dims
    nz = nx // 2
    ng = 2 * ny
    ext = cells + 4 * W
    owned = cells // ny
    a_rows = -(-(6 * W // ng) // 16) * 16
    b_rows = -(-(3 * W // ng + 3) // 16) * 16
    operands = dict(
        nodes=nodes,
        feat=edge_feat,
        snd=senders.reshape(edges // W, W),
        rcv=receivers.reshape(edges // W, W),
        slist=send_lists.reshape(4, W),
        owner=owner.reshape(cells // W, W),
        cot=cotangent,
        w_edge=w_edge,
        w_node=w_node,
        w_coarse=w_coarse,
        bias=biases,
    )
    shapes = (
        jax.ShapeDtypeStruct((cells, W), BF16),
        jax.ShapeDtypeStruct((cells, W), BF16),
        jax.ShapeDtypeStruct((edges, W), BF16),
        jax.ShapeDtypeStruct((9 * W, W), F32),
        jax.ShapeDtypeStruct((3, W), F32),
    )
    scratch = {name: pltpu.VMEM(operands[name].shape, operands[name].dtype) for name in INPUTS}
    scratch |= {name: pltpu.VMEM(s.shape, s.dtype) for name, s in zip(OUTPUTS, shapes)}
    scratch |= dict(
        iota=pltpu.VMEM((BLOCK, max(cells, tile)), BF16),
        ext_t=pltpu.VMEM((W, ext), BF16),
        table_t=pltpu.VMEM((2 * W, (ext + cells) // 2), BF16),
        marks=pltpu.VMEM((edges // tile, (ext + cells) // 2, tile), BF16),
        hot_list=pltpu.VMEM((cells, 4 * W), BF16),
        own_t=pltpu.VMEM((cells // 2, cells), BF16),
        own_n=pltpu.VMEM((cells, cells // 2), BF16),
        own_at=pltpu.VMEM((cells, W), F32),
        own_high=pltpu.VMEM((cells, W), F32),
        pick=pltpu.VMEM((4, W, W), BF16),
        halo=pltpu.VMEM((4, W, W), BF16),
        slopes=pltpu.VMEM((edges // tile, W, tile), F32),
        d_pre=pltpu.VMEM((edges // tile, W, tile), BF16),
        h_acc=pltpu.VMEM((cells // 2, 2 * W), F32),
        s_acc=pltpu.VMEM((ext // 2, 2 * W), F32),
        r_acc=pltpu.VMEM((cells // 2, 2 * W), F32),
        we_acc=pltpu.VMEM((W, W), F32),
        fine=pltpu.VMEM((cells, W), F32),
        node_slope=pltpu.VMEM((cells, W), F32),
        d_part=pltpu.VMEM((cells, W), F32),
        hb=pltpu.VMEM((cells, W), BF16),
        agg=pltpu.VMEM((cells, W), BF16),
        hid=pltpu.VMEM((cells, W), BF16),
        cot_src=pltpu.VMEM((ny, owned, W), BF16),
        cot_got=pltpu.VMEM((ny, owned, W), BF16),
        fine_src=pltpu.VMEM((ny, owned, W), BF16),
        fine_got=pltpu.VMEM((ny, owned, W), BF16),
        coarse_all=pltpu.VMEM((ny, owned, W), BF16),
        d_coarse_all=pltpu.VMEM((ny, owned, W), BF16),
        d_pre_n=pltpu.VMEM((cells, W), BF16),
        back_src=pltpu.VMEM((4, W, W), BF16),
        back_got=pltpu.VMEM((4, W, W), BF16),
        bias_rows=pltpu.VMEM((b_rows, W), F32),
        b_flat=pltpu.VMEM((3 * W + b_rows, W), F32),
        load_sem=pltpu.SemaphoreType.DMA((len(INPUTS),)),
        halo_sem=pltpu.SemaphoreType.DMA((2, 4)),
        back_sem=pltpu.SemaphoreType.DMA((2, 4)),
        cot_sem=pltpu.SemaphoreType.DMA((2,)),
        fine_sem=pltpu.SemaphoreType.DMA((2,)),
        coarse_sem=pltpu.SemaphoreType.DMA((2,)),
        d_coarse_sem=pltpu.SemaphoreType.DMA((2,)),
        out_sem=pltpu.SemaphoreType.DMA((7,)),
    )
    for name, rows in (("a", a_rows), ("b", b_rows)):
        scratch |= {
            name + "_src": pltpu.VMEM((ng, rows, W), BF16),
            name + "_in": pltpu.VMEM((ng, rows, W), BF16),
            name + "_z": pltpu.VMEM((nz, rows, W), BF16),
            name + "_all": pltpu.VMEM((ng, rows, W), BF16),
            name + "_sum": pltpu.VMEM((rows, W), F32),
            name + "_rs_sem": pltpu.SemaphoreType.DMA((2,)),
            name + "_z_sem": pltpu.SemaphoreType.DMA((2,)),
            name + "_ag_sem": pltpu.SemaphoreType.DMA((2,)),
        }
    names = tuple(name + "_in" for name in INPUTS) + ("live",)
    names += tuple(name + "_out" for name in OUTPUTS) + tuple(scratch)
    smem = pl.BlockSpec(memory_space=pltpu.SMEM)
    hbm = pl.BlockSpec(memory_space=pltpu.HBM)
    outs = pl.pallas_call(
        functools.partial(kernel, dims, names),
        out_shape=shapes,
        in_specs=[hbm] * len(INPUTS) + [smem],
        out_specs=(hbm,) * 5,
        scratch_shapes=list(scratch.values()),
        compiler_params=pltpu.CompilerParams(
            collective_id=0, has_side_effects=True, vmem_limit_bytes=61440 * 1024
        ),
        cost_estimate=pl.CostEstimate(
            flops=2 * edges * W * (2 * ext + 4 * cells + 4 * W),
            bytes_accessed=2 * W * (2 * edges + 4 * cells),
            transcendentals=edges * W,
        ),
        name="mesh_step",
    )(*[operands[name] for name in INPUTS], edge_live)
    cuts = (1, 1, 4, 2, 1)
    outs = pl.pallas_call(
        functools.partial(settle, cuts),
        out_shape=shapes,
        in_specs=[hbm] * 5,
        out_specs=(hbm,) * 5,
        scratch_shapes=[pltpu.VMEM(s.shape, s.dtype) for s in shapes]
        + [pltpu.SemaphoreType.DMA((2, sum(cuts)))],
        compiler_params=pltpu.CompilerParams(vmem_limit_bytes=60 * 1024 * 1024),
        name="settle",
    )(*outs)
    node_out, d_nodes, d_edges, grads, bias_grads = outs
    return node_out, d_nodes, d_edges, grads.reshape(9, W, W), bias_grads


def solution(mesh, cells=1024, edges=4096, tile=1024):
    both = ("gx", "gy")
    dims = (mesh.shape["gx"], mesh.shape["gy"], cells, edges, tile)
    in_specs = (
        P(both, None),
        P(both, None),
        P(both),
        P(both),
        P(both, None, None),
        P(both),
        P(both),
        P(both, None),
        P(),
        P(),
        P(),
        P(),
    )
    out_specs = (P(both, None), P(both, None), P(both, None), P(), P())
    return jax.shard_map(
        functools.partial(body, dims),
        mesh=mesh,
        in_specs=in_specs,
        out_specs=out_specs,
        check_vma=False,
    )
```

```python
import functools
from types import SimpleNamespace

import jax
import jax.numpy as jnp
from jax import lax
from jax.experimental import pallas as pl
from jax.experimental.pallas import tpu as pltpu
from jax.sharding import PartitionSpec as P

F32, BF16, I32 = jnp.float32, jnp.bfloat16, jnp.int32
W = 128
BLOCK = 256
MESH = pl.DeviceIdType.MESH


def dot(left, right):
    return jnp.dot(left, right, preferred_element_type=F32)


def right_t(left, right):
    return lax.dot_general(left, right, (((1,), (1,)), ((), ())), preferred_element_type=F32)


def sigmoid(value):
    return 0.5 * jnp.tanh(0.5 * value) + 0.5


def slope(value, sigma):
    return sigma * (1.0 + value * (1.0 - sigma))


def lane_row(ref, first, count):
    return jnp.concatenate([ref[pl.ds(first + q, 1), :] for q in range(count)], axis=1)


INPUTS = (
    "nodes", "feat", "snd", "rcv", "slist", "owner", "cot", "w_edge", "w_node", "w_coarse", "bias"
)
ORDER = (
    "slist", "nodes", "owner", "cot", "snd", "rcv", "w_edge", "bias", "feat", "w_node", "w_coarse"
)
OUTPUTS = ("node_out", "d_nodes", "d_edges", "grads", "bias_grads")


def kernel(dims, names, *refs):
    r = SimpleNamespace(**dict(zip(names, refs)))
    nx, ny, cells, edges, tile = dims
    nz = nx // 2
    ng = 2 * ny
    ext = cells + 4 * W
    owned = cells // ny
    tiles = edges // tile
    i, j = lax.axis_index("gx"), lax.axis_index("gy")
    core, z = lax.rem(i, 2), lax.div(i, 2)
    g = core * ny + j
    up, down = lax.rem(i + nx - 1, nx), lax.rem(i + 1, nx)
    left, right = lax.rem(j + ny - 1, ny), lax.rem(j + 1, ny)
    across = lax.rem(i + nx - 1 + 2 * core, nx)

    barrier = pltpu.get_barrier_semaphore()

    def greet(gx, gy):
        pl.semaphore_signal(barrier, inc=1, device_id=(gx, gy), device_id_type=MESH)

    def each(count, me, action):
        some = 5 if count > 5 else 1
        first = 1 + (count - 1) % some
        for d in range(1, first):
            action(me ^ d)

        def step(k, c):
            for u in range(some):
                action(me ^ (first + k * some + u))
            return c

        lax.fori_loop(0, (count - first) // some, step, 0)

    shift = ny.bit_length() - 1

    def layer_place(t):
        return 2 * z + lax.shift_right_logical(t, shift), t & (ny - 1)

    greet(across, j)
    loads = {
        name: pltpu.make_async_copy(
            getattr(r, name + "_in"), getattr(r, name), r.load_sem.at[k]
        )
        for k, name in enumerate(ORDER)
    }
    for name in ORDER:
        loads[name].start()
    each(ng, g, lambda t: greet(*layer_place(t)))
    each(nz, z, lambda t: greet(2 * t + core, j))

    def exchange(count, me, place):
        def copy(src, dst, sems, target):
            return pltpu.make_async_remote_copy(
                src_ref=src,
                dst_ref=dst,
                send_sem=sems.at[0],
                recv_sem=sems.at[1],
                device_id=place(target),
                device_id_type=MESH,
            )

        def scatter(src, dst, sems):
            dst[me] = src[me]
            each(count, me, lambda t: copy(src.at[t], dst.at[me], sems, t).start())

        def gather(buf, sems):
            each(count, me, lambda t: copy(buf.at[me], buf.at[me], sems, t).start())

        def every(buf, sems):
            others = buf.at[pl.ds(0, count - 1)]
            return copy(others, others, sems, me ^ 1)

        def arrive(buf, sems):
            every(buf, sems).wait_recv()

        def sent(buf, sems):
            every(buf, sems).wait_send()

        return SimpleNamespace(scatter=scatter, gather=gather, arrive=arrive, sent=sent)

    row = exchange(ny, j, lambda t: (i, t))
    column = exchange(nz, z, lambda t: (2 * t + core, j))
    layer = exchange(ng, g, layer_place)

    def slots_sum(ref):
        return jnp.sum(ref[...].astype(F32), axis=0)

    def reduce_stages(src, into, zbuf, everything, sums, sems):
        rs_sem, z_sem, ag_sem = sems

        def start():
            layer.scatter(src, into, rs_sem)

        def to_column():
            layer.arrive(into, rs_sem)
            zbuf[z] = slots_sum(into).astype(BF16)
            column.gather(zbuf, z_sem)

        def to_layer():
            column.arrive(zbuf, z_sem)
            sums[...] = slots_sum(zbuf)
            everything[g] = sums[...].astype(BF16)
            layer.gather(everything, ag_sem)

        def finish():
            layer.arrive(everything, ag_sem)

        def sent():
            layer.sent(into, rs_sem)
            column.sent(zbuf, z_sem)
            layer.sent(everything, ag_sem)

        return SimpleNamespace(
            start=start, to_column=to_column, to_layer=to_layer, finish=finish, sent=sent
        )

    a_stage = reduce_stages(
        r.a_src, r.a_in, r.a_z, r.a_all, r.a_sum, (r.a_rs_sem, r.a_z_sem, r.a_ag_sem)
    )
    b_stage = reduce_stages(
        r.b_src, r.b_in, r.b_z, r.b_all, r.b_sum, (r.b_rs_sem, r.b_z_sem, r.b_ag_sem)
    )

    def halo_copies(src, dst, sems):
        targets = ((up, j), (down, j), (i, left), (i, right))
        return [
            pltpu.make_async_remote_copy(
                src_ref=src.at[k],
                dst_ref=dst.at[k ^ 1],
                send_sem=sems.at[0, k],
                recv_sem=sems.at[1, k ^ 1],
                device_id=targets[k],
                device_id_type=MESH,
            )
            for k in range(4)
        ]

    present = (i > 0, i < nx - 1, j > 0, j < ny - 1)

    half_e, half_c = ext // 2, cells // 2

    def folded(line, half):
        return jnp.where(line >= half, line - half, line)

    def pick_half(high, both):
        return jnp.where(high, both[W:, :], both[:W, :])

    def halves(high, value):
        low = jnp.where(high, 0.0, value)
        return jnp.concatenate([low, value - low], axis=0).astype(BF16)

    def unfold(pairs):
        return jnp.concatenate([pairs[:, :W], pairs[:, W:]], axis=0)

    def fold_t(table, half):
        return jnp.concatenate([table[:, :half], table[:, half:]], axis=0)

    def to_coarse(value):
        low = jnp.where(r.own_high[...] > 0.5, 0.0, value)
        pairs = jnp.concatenate([low, value - low], axis=1).astype(BF16)
        return unfold(dot(r.own_t[...], pairs)).astype(BF16).reshape(ny, owned, W)

    def from_coarse(table):
        flat = table.reshape(cells, W)
        pairs = jnp.concatenate([flat[:half_c], flat[half_c:]], axis=1)
        both = dot(r.own_n[...], pairs)
        return jnp.where(r.own_high[...] > 0.5, both[:, W:], both[:, :W])

    def hot(line, count):
        parts = []
        for a in range(count // BLOCK):
            inside = jnp.where(lax.shift_right_arithmetic(line, 8) == a, line & 255, -1)
            inside = inside.astype(F32).astype(BF16)
            same = r.iota[:, : line.shape[1]] == inside
            parts.append(jnp.where(same, jnp.ones((), BF16), jnp.zeros((), BF16)))
        return jnp.concatenate(parts, axis=0)

    eye = (
        lax.broadcasted_iota(I32, (W, W), 0) == lax.broadcasted_iota(I32, (W, W), 1)
    ).astype(F32).astype(BF16)

    def turned(block):
        return right_t(eye, block).astype(BF16)

    r.iota[...] = lax.broadcasted_iota(I32, r.iota.shape, 0).astype(F32).astype(BF16)
    loads["slist"].wait()
    r.hot_list[...] = hot(lane_row(r.slist, 0, 4), cells)
    loads["nodes"].wait()
    r.ext_t[:, :cells] = turned(r.nodes[...])
    picked = dot(r.ext_t[:, :cells], r.hot_list[...]).astype(BF16)
    for k in range(4):
        r.pick[k] = picked[:, k * W : (k + 1) * W]
    loads["owner"].wait()
    r.own_t[...] = hot(folded(lane_row(r.owner, 0, cells // W), half_c), half_c)
    for q in range(cells // W):
        at = jnp.broadcast_to(r.owner[q : q + 1, :].astype(F32), (W, W)).T
        r.own_at[q * W : (q + 1) * W, :] = at
    r.own_high[...] = jnp.where(r.own_at[...] >= float(half_c), 1.0, 0.0)
    loads["cot"].wait()
    r.cot_src[...] = to_coarse(r.cot[...].astype(F32))

    pl.semaphore_wait(barrier, ng + nz - 1)
    halo_out = halo_copies(r.pick, r.halo, r.halo_sem)
    for copy in halo_out:
        copy.start()
    row.scatter(r.cot_src, r.cot_got, r.cot_sem)

    loads["snd"].wait()
    loads["rcv"].wait()
    per = tile // W
    alive = r.live[0]

    def sender_row(t):
        return lane_row(r.snd, t * per, per)

    def receiver_row(t):
        place = t * tile + lax.broadcasted_iota(I32, (1, tile), 1)
        return jnp.where(place < alive, lane_row(r.rcv, t * per, per), -1)

    def high_s(t):
        return jnp.broadcast_to(sender_row(t), (W, tile)) >= half_e

    def high_r(t):
        return jnp.broadcast_to(receiver_row(t), (W, tile)) >= half_c

    def mark(t, c):
        r.marks[t, :half_e, :] = hot(folded(sender_row(t), half_e), half_e)
        r.marks[t, half_e:, :] = hot(folded(receiver_row(t), half_c), half_c)
        return c

    lax.fori_loop(0, tiles, mark, 0)

    loads["w_edge"].wait()
    loads["bias"].wait()
    ws_t, wr_t, we_t = [turned(r.w_edge[k]) for k in range(3)]
    b_col = jnp.broadcast_to(r.bias[0:1, :], (W, W)).T
    r.table_t[:, half_e:] = fold_t(dot(wr_t, r.ext_t[:, :cells]), half_c).astype(BF16)
    loads["feat"].wait()
    for copy in halo_out:
        copy.wait_recv()
    for k in range(4):
        r.ext_t[:, cells + k * W : cells + (k + 1) * W] = jnp.where(
            present[k], r.halo[k].astype(F32), 0.0
        ).astype(BF16)
    r.table_t[:, :half_e] = fold_t(
        dot(ws_t, r.ext_t[...]) + jnp.concatenate([b_col] * (ext // W), axis=1), half_e
    ).astype(BF16)

    r.h_acc[...] = jnp.zeros_like(r.h_acc)

    def edge_rows(t):
        return pl.ds(pl.multiple_of(t * tile, tile), tile)

    def forward(t, c):
        above = high_r(t)
        pre = (
            pick_half(high_s(t), dot(r.table_t[:, :half_e], r.marks[t, :half_e, :]))
            + pick_half(above, dot(r.table_t[:, half_e:], r.marks[t, half_e:, :]))
            + right_t(we_t, r.feat[edge_rows(t), :])
        )
        sigma = sigmoid(pre)
        r.slopes[t] = slope(pre, sigma)
        r.h_acc[...] += right_t(r.marks[t, half_e:, :], halves(above, pre * sigma))
        return c

    lax.fori_loop(0, tiles, forward, 0, unroll=2)

    loads["w_node"].wait()
    loads["w_coarse"].wait()
    r.hb[...] = unfold(r.h_acc[...]).astype(BF16)
    r.agg[...] = dot(r.hb[...], r.w_edge[3]).astype(BF16)
    pre_node = dot(r.nodes[...], r.w_node[0]) + dot(r.agg[...], r.w_node[1]) + r.bias[1:2, :]
    sigma = sigmoid(pre_node)
    r.node_slope[...] = slope(pre_node, sigma)
    r.hid[...] = (pre_node * sigma).astype(BF16)
    r.fine[...] = r.nodes[...].astype(F32) + dot(r.hid[...], r.w_node[2])
    r.fine_src[...] = to_coarse(r.fine[...])
    row.scatter(r.fine_src, r.fine_got, r.fine_sem)

    lanes = lax.broadcasted_iota(I32, (cells, W), 1).astype(F32)
    at = r.own_at[...] - float(half_c) * r.own_high[...]
    r.own_n[...] = jnp.concatenate(
        [jnp.where(at == lanes + float(k * W), 1.0, 0.0).astype(BF16) for k in range(half_c // W)],
        axis=1,
    )
    agg_t, hid_t, hb_t = turned(r.agg[...]), turned(r.hid[...]), turned(r.hb[...])

    row.arrive(r.cot_got, r.cot_sem)
    d_coarse = slots_sum(r.cot_got).astype(BF16)
    d_hidden = right_t(d_coarse, r.w_coarse[1])
    row.arrive(r.fine_got, r.fine_sem)
    coarse_bf = (0.0625 * slots_sum(r.fine_got)).astype(BF16)
    pre_coarse = dot(coarse_bf, r.w_coarse[0]) + r.bias[2:3, :]
    sigma = sigmoid(pre_coarse)
    coarse_hid = (pre_coarse * sigma).astype(BF16)
    d_pre_c = d_hidden * slope(pre_coarse, sigma)
    d_pre_c_bf = d_pre_c.astype(BF16)
    r.d_coarse_all[j] = right_t(d_pre_c_bf, r.w_coarse[0]).astype(BF16)
    row.gather(r.d_coarse_all, r.d_coarse_sem)
    r.coarse_all[j] = dot(coarse_hid, r.w_coarse[1]).astype(BF16)
    row.gather(r.coarse_all, r.coarse_sem)
    g_v1 = dot(turned(coarse_bf), d_pre_c_bf)
    g_v2 = dot(turned(coarse_hid), d_coarse)
    b_own = r.b_src.shape[1]
    a_own = 6 * W // ng
    share = 3 * W // ng
    r.bias_rows[...] = jnp.zeros_like(r.bias_rows)
    r.bias_rows[share + 2 : share + 3, :] = jnp.sum(d_pre_c, axis=0, keepdims=True)
    row.arrive(r.d_coarse_all, r.d_coarse_sem)

    d_fine = r.cot[...].astype(F32) + 0.0625 * from_coarse(r.d_coarse_all[...])
    d_fine_bf = d_fine.astype(BF16)
    d_pre_n = right_t(d_fine_bf, r.w_node[2]) * r.node_slope[...]
    d_pre_n_bf = d_pre_n.astype(BF16)
    r.bias_rows[share + 1 : share + 2, :] = jnp.sum(d_pre_n, axis=0, keepdims=True)
    r.d_part[...] = d_fine
    r.d_pre_n[...] = d_pre_n_bf
    d_agg = right_t(d_pre_n_bf, r.w_node[1]).astype(BF16)
    r.table_t[:, half_e:] = fold_t(right_t(r.w_edge[3], d_agg), half_c).astype(BF16)
    early = jnp.concatenate(
        [
            dot(hb_t, d_agg),
            dot(r.ext_t[:, :cells], d_pre_n_bf),
            dot(agg_t, d_pre_n_bf),
            dot(hid_t, d_fine_bf),
            g_v1,
            g_v2,
        ],
        axis=0,
    ).reshape(ng, a_own, W)
    spare = r.a_src.shape[1] - a_own
    if spare:
        early = jnp.concatenate([early, jnp.zeros((ng, spare, W), F32)], axis=1)
    r.a_src[...] = early.astype(BF16)
    a_stage.start()

    r.s_acc[...] = jnp.zeros_like(r.s_acc)
    r.r_acc[...] = jnp.zeros_like(r.r_acc)
    r.we_acc[...] = jnp.zeros_like(r.we_acc)

    def backward(t, c):
        above = high_r(t)
        got = pick_half(above, dot(r.table_t[:, half_e:], r.marks[t, half_e:, :]))
        d_pre = got * r.slopes[t]
        d_pre_bf = d_pre.astype(BF16)
        r.d_pre[t] = d_pre_bf
        r.s_acc[...] += right_t(r.marks[t, :half_e, :], halves(high_s(t), d_pre))
        r.r_acc[...] += right_t(r.marks[t, half_e:, :], halves(above, d_pre))
        r.we_acc[...] += dot(d_pre_bf, r.feat[edge_rows(t), :])
        return c

    def edge_out(t, c):
        r.d_edges[edge_rows(t), :] = dot(r.w_edge[2], r.d_pre[t]).T.astype(BF16)
        return c

    leaving = []

    def leave(k, src, dst):
        leaving.append(pltpu.make_async_copy(src, dst, r.out_sem.at[k]))
        leaving[-1].start()

    half = tiles // 2
    lax.fori_loop(0, tiles, backward, 0, unroll=2)
    a_stage.to_column()

    s_bf = unfold(r.s_acc[...]).astype(BF16)
    r_sum = unfold(r.r_acc[...])
    r_bf = r_sum.astype(BF16)
    r.back_src[...] = right_t(s_bf[cells:, :], r.w_edge[0]).astype(BF16).reshape(4, W, W)
    back_out = halo_copies(r.back_src, r.back_got, r.back_sem)
    for copy in back_out:
        copy.start()
    r.bias_rows[share : share + 1, :] = jnp.sum(r_sum, axis=0, keepdims=True)
    r.b_flat[: 3 * W, :] = jnp.concatenate(
        [dot(r.ext_t[...], s_bf), dot(r.ext_t[:, :cells], r_bf), r.we_acc[...].T], axis=0
    )
    r.b_flat[3 * W :, :] = jnp.zeros((b_own, W), F32)
    inner = lax.broadcasted_iota(I32, (b_own, W), 0) < share
    for k in range(ng):
        part = r.b_flat[k * share : k * share + b_own, :]
        r.b_src[k] = jnp.where(inner, part, r.bias_rows[...]).astype(BF16)
    b_stage.start()
    r.d_part[...] = (
        r.d_part[...]
        + right_t(r.d_pre_n[...], r.w_node[0])
        + right_t(s_bf[:cells, :], r.w_edge[0])
        + right_t(r_bf, r.w_edge[1])
    )
    for copy in back_out:
        copy.wait_recv()
    returned = jnp.concatenate(
        [jnp.where(present[k], r.back_got[k].astype(F32), 0.0) for k in range(4)], axis=0
    ).astype(BF16)
    r.d_nodes[...] = (r.d_part[...] + dot(r.hot_list[...], returned)).astype(BF16)
    leave(0, r.d_nodes, r.d_nodes_out)
    b_stage.to_column()
    a_stage.to_layer()
    lax.fori_loop(0, half, edge_out, 0)
    first, second = pl.ds(0, half * tile), pl.ds(half * tile, (tiles - half) * tile)
    leave(1, r.d_edges.at[first], r.d_edges_out.at[first])
    row.arrive(r.coarse_all, r.coarse_sem)
    r.node_out[...] = (r.fine[...] + from_coarse(r.coarse_all[...])).astype(BF16)
    leave(2, r.node_out, r.node_out_out)
    b_stage.to_layer()
    lax.fori_loop(half, tiles, edge_out, 0)
    leave(3, r.d_edges.at[second], r.d_edges_out.at[second])
    r.bias_grads[...] = r.b_sum[share : share + 3, :]
    leave(4, r.bias_grads, r.bias_grads_out)
    a_stage.finish()
    r.grads[3 * W :, :] = r.a_all[...].astype(F32)[:, :a_own, :].reshape(6 * W, W)
    late, soon = pl.ds(0, 3 * W), pl.ds(3 * W, 6 * W)
    leave(5, r.grads.at[soon], r.grads_out.at[soon])
    row.sent(r.cot_got, r.cot_sem)
    row.sent(r.fine_got, r.fine_sem)
    row.sent(r.coarse_all, r.coarse_sem)
    row.sent(r.d_coarse_all, r.d_coarse_sem)
    for copy in halo_out + back_out:
        copy.wait_send()
    a_stage.sent()
    layer.sent(r.b_in, r.b_rs_sem)
    column.sent(r.b_z, r.b_z_sem)
    b_stage.finish()
    for k in range(ng):
        r.grads[k * share : (k + 1) * share, :] = r.b_all[k].astype(F32)[:share, :]
    leave(6, r.grads.at[late], r.grads_out.at[late])
    layer.sent(r.b_all, r.b_ag_sem)
    for copy in leaving:
        copy.wait()


def settle(cuts, *refs):
    count = len(cuts)
    held, sems = refs[2 * count : 3 * count], refs[3 * count]
    pieces = []
    for k, parts in enumerate(cuts):
        rows = refs[k].shape[0] // parts
        pieces += [(k, pl.ds(p * rows, rows)) for p in range(parts)]
    gets = [
        pltpu.make_async_copy(refs[k].at[here], held[k].at[here], sems.at[0, n])
        for n, (k, here) in enumerate(pieces)
    ]
    puts = [
        pltpu.make_async_copy(held[k].at[here], refs[count + k].at[here], sems.at[1, n])
        for n, (k, here) in enumerate(pieces)
    ]
    for get in gets:
        get.start()
    for get, put in zip(gets, puts):
        get.wait()
        put.start()
    for put in puts:
        put.wait()


def body(
    dims,
    nodes,
    edge_feat,
    senders,
    receivers,
    send_lists,
    owner,
    edge_live,
    cotangent,
    w_edge,
    w_node,
    w_coarse,
    biases,
):
    nx, ny, cells, edges, tile = dims
    nz = nx // 2
    ng = 2 * ny
    ext = cells + 4 * W
    owned = cells // ny
    a_rows = -(-(6 * W // ng) // 16) * 16
    b_rows = -(-(3 * W // ng + 3) // 16) * 16
    operands = dict(
        nodes=nodes,
        feat=edge_feat,
        snd=senders.reshape(edges // W, W),
        rcv=receivers.reshape(edges // W, W),
        slist=send_lists.reshape(4, W),
        owner=owner.reshape(cells // W, W),
        cot=cotangent,
        w_edge=w_edge,
        w_node=w_node,
        w_coarse=w_coarse,
        bias=biases,
    )
    shapes = (
        jax.ShapeDtypeStruct((cells, W), BF16),
        jax.ShapeDtypeStruct((cells, W), BF16),
        jax.ShapeDtypeStruct((edges, W), BF16),
        jax.ShapeDtypeStruct((9 * W, W), F32),
        jax.ShapeDtypeStruct((3, W), F32),
    )
    scratch = {name: pltpu.VMEM(operands[name].shape, operands[name].dtype) for name in INPUTS}
    scratch |= {name: pltpu.VMEM(s.shape, s.dtype) for name, s in zip(OUTPUTS, shapes)}
    scratch |= dict(
        iota=pltpu.VMEM((BLOCK, max(cells, tile)), BF16),
        ext_t=pltpu.VMEM((W, ext), BF16),
        table_t=pltpu.VMEM((2 * W, (ext + cells) // 2), BF16),
        marks=pltpu.VMEM((edges // tile, (ext + cells) // 2, tile), BF16),
        hot_list=pltpu.VMEM((cells, 4 * W), BF16),
        own_t=pltpu.VMEM((cells // 2, cells), BF16),
        own_n=pltpu.VMEM((cells, cells // 2), BF16),
        own_at=pltpu.VMEM((cells, W), F32),
        own_high=pltpu.VMEM((cells, W), F32),
        pick=pltpu.VMEM((4, W, W), BF16),
        halo=pltpu.VMEM((4, W, W), BF16),
        slopes=pltpu.VMEM((edges // tile, W, tile), F32),
        d_pre=pltpu.VMEM((edges // tile, W, tile), BF16),
        h_acc=pltpu.VMEM((cells // 2, 2 * W), F32),
        s_acc=pltpu.VMEM((ext // 2, 2 * W), F32),
        r_acc=pltpu.VMEM((cells // 2, 2 * W), F32),
        we_acc=pltpu.VMEM((W, W), F32),
        fine=pltpu.VMEM((cells, W), F32),
        node_slope=pltpu.VMEM((cells, W), F32),
        d_part=pltpu.VMEM((cells, W), F32),
        hb=pltpu.VMEM((cells, W), BF16),
        agg=pltpu.VMEM((cells, W), BF16),
        hid=pltpu.VMEM((cells, W), BF16),
        cot_src=pltpu.VMEM((ny, owned, W), BF16),
        cot_got=pltpu.VMEM((ny, owned, W), BF16),
        fine_src=pltpu.VMEM((ny, owned, W), BF16),
        fine_got=pltpu.VMEM((ny, owned, W), BF16),
        coarse_all=pltpu.VMEM((ny, owned, W), BF16),
        d_coarse_all=pltpu.VMEM((ny, owned, W), BF16),
        d_pre_n=pltpu.VMEM((cells, W), BF16),
        back_src=pltpu.VMEM((4, W, W), BF16),
        back_got=pltpu.VMEM((4, W, W), BF16),
        bias_rows=pltpu.VMEM((b_rows, W), F32),
        b_flat=pltpu.VMEM((3 * W + b_rows, W), F32),
        load_sem=pltpu.SemaphoreType.DMA((len(INPUTS),)),
        halo_sem=pltpu.SemaphoreType.DMA((2, 4)),
        back_sem=pltpu.SemaphoreType.DMA((2, 4)),
        cot_sem=pltpu.SemaphoreType.DMA((2,)),
        fine_sem=pltpu.SemaphoreType.DMA((2,)),
        coarse_sem=pltpu.SemaphoreType.DMA((2,)),
        d_coarse_sem=pltpu.SemaphoreType.DMA((2,)),
        out_sem=pltpu.SemaphoreType.DMA((7,)),
    )
    for name, rows in (("a", a_rows), ("b", b_rows)):
        scratch |= {
            name + "_src": pltpu.VMEM((ng, rows, W), BF16),
            name + "_in": pltpu.VMEM((ng, rows, W), BF16),
            name + "_z": pltpu.VMEM((nz, rows, W), BF16),
            name + "_all": pltpu.VMEM((ng, rows, W), BF16),
            name + "_sum": pltpu.VMEM((rows, W), F32),
            name + "_rs_sem": pltpu.SemaphoreType.DMA((2,)),
            name + "_z_sem": pltpu.SemaphoreType.DMA((2,)),
            name + "_ag_sem": pltpu.SemaphoreType.DMA((2,)),
        }
    names = tuple(name + "_in" for name in INPUTS) + ("live",)
    names += tuple(name + "_out" for name in OUTPUTS) + tuple(scratch)
    smem = pl.BlockSpec(memory_space=pltpu.SMEM)
    hbm = pl.BlockSpec(memory_space=pltpu.HBM)
    outs = pl.pallas_call(
        functools.partial(kernel, dims, names),
        out_shape=shapes,
        in_specs=[hbm] * len(INPUTS) + [smem],
        out_specs=(hbm,) * 5,
        scratch_shapes=list(scratch.values()),
        compiler_params=pltpu.CompilerParams(
            collective_id=0, has_side_effects=True, vmem_limit_bytes=61440 * 1024
        ),
        cost_estimate=pl.CostEstimate(
            flops=2 * edges * W * (2 * ext + 4 * cells + 4 * W),
            bytes_accessed=2 * W * (2 * edges + 4 * cells),
            transcendentals=edges * W,
        ),
        name="mesh_step",
    )(*[operands[name] for name in INPUTS], edge_live)
    cuts = (1, 1, 4, 2, 1)
    outs = pl.pallas_call(
        functools.partial(settle, cuts),
        out_shape=shapes,
        in_specs=[hbm] * 5,
        out_specs=(hbm,) * 5,
        scratch_shapes=[pltpu.VMEM(s.shape, s.dtype) for s in shapes]
        + [pltpu.SemaphoreType.DMA((2, sum(cuts)))],
        compiler_params=pltpu.CompilerParams(vmem_limit_bytes=60 * 1024 * 1024),
        name="settle",
    )(*outs)
    node_out, d_nodes, d_edges, grads, bias_grads = outs
    return node_out, d_nodes, d_edges, grads.reshape(9, W, W), bias_grads


def solution(mesh, cells=1024, edges=4096, tile=1024):
    both = ("gx", "gy")
    dims = (mesh.shape["gx"], mesh.shape["gy"], cells, edges, tile)
    in_specs = (
        P(both, None),
        P(both, None),
        P(both),
        P(both),
        P(both, None, None),
        P(both),
        P(both),
        P(both, None),
        P(),
        P(),
        P(),
        P(),
    )
    out_specs = (P(both, None), P(both, None), P(both, None), P(), P())
    return jax.shard_map(
        functools.partial(body, dims),
        mesh=mesh,
        in_specs=in_specs,
        out_specs=out_specs,
        check_vma=False,
    )
```

```python
import functools
from types import SimpleNamespace

import jax
import jax.numpy as jnp
from jax import lax
from jax.experimental import pallas as pl
from jax.experimental.pallas import tpu as pltpu
from jax.sharding import PartitionSpec as P

F32, BF16, I32 = jnp.float32, jnp.bfloat16, jnp.int32
W = 128
BLOCK = 256
MESH = pl.DeviceIdType.MESH


def dot(left, right):
    return jnp.dot(left, right, preferred_element_type=F32)


def right_t(left, right):
    return lax.dot_general(left, right, (((1,), (1,)), ((), ())), preferred_element_type=F32)


def sigmoid(value):
    return 0.5 * jnp.tanh(0.5 * value) + 0.5


def slope(value, sigma):
    return sigma * (1.0 + value * (1.0 - sigma))


def lane_row(ref, first, count):
    return jnp.concatenate([ref[pl.ds(first + q, 1), :] for q in range(count)], axis=1)


INPUTS = (
    "nodes", "feat", "snd", "rcv", "slist", "owner", "cot", "w_edge", "w_node", "w_coarse", "bias"
)
ORDER = (
    "slist", "nodes", "owner", "cot", "snd", "rcv", "w_edge", "bias", "feat", "w_node", "w_coarse"
)
OUTPUTS = ("node_out", "d_nodes", "d_edges", "grads", "bias_grads")


def kernel(dims, names, *refs):
    r = SimpleNamespace(**dict(zip(names, refs)))
    nx, ny, cells, edges, tile = dims
    nz = nx // 2
    ng = 2 * ny
    ext = cells + 4 * W
    owned = cells // ny
    tiles = edges // tile
    i, j = lax.axis_index("gx"), lax.axis_index("gy")
    core, z = lax.rem(i, 2), lax.div(i, 2)
    g = core * ny + j
    up, down = lax.rem(i + nx - 1, nx), lax.rem(i + 1, nx)
    left, right = lax.rem(j + ny - 1, ny), lax.rem(j + 1, ny)
    across = lax.rem(i + nx - 1 + 2 * core, nx)

    barrier = pltpu.get_barrier_semaphore()

    def greet(gx, gy):
        pl.semaphore_signal(barrier, inc=1, device_id=(gx, gy), device_id_type=MESH)

    def each(count, me, action):
        for d in range(1, count):
            action(me ^ d)

    shift = ny.bit_length() - 1

    def layer_place(t):
        return 2 * z + lax.shift_right_logical(t, shift), t & (ny - 1)

    greet(across, j)
    loads = {
        name: pltpu.make_async_copy(
            getattr(r, name + "_in"), getattr(r, name), r.load_sem.at[k]
        )
        for k, name in enumerate(ORDER)
    }
    for name in ORDER:
        loads[name].start()
    live_load = pltpu.make_async_copy(r.live_in, r.live, r.load_sem.at[len(ORDER)])
    live_load.start()
    each(ng, g, lambda t: greet(*layer_place(t)))
    each(nz, z, lambda t: greet(2 * t + core, j))

    def exchange(count, me, place):
        def copy(src, dst, sems, target):
            return pltpu.make_async_remote_copy(
                src_ref=src,
                dst_ref=dst,
                send_sem=sems.at[0],
                recv_sem=sems.at[1],
                device_id=place(target),
                device_id_type=MESH,
            )

        def scatter(src, dst, sems):
            dst[me] = src[me]
            each(count, me, lambda t: copy(src.at[t], dst.at[me], sems, t).start())

        def gather(buf, sems):
            each(count, me, lambda t: copy(buf.at[me], buf.at[me], sems, t).start())

        def every(buf, sems):
            others = buf.at[pl.ds(0, count - 1)]
            return copy(others, others, sems, me ^ 1)

        def arrive(buf, sems):
            every(buf, sems).wait_recv()

        def sent(buf, sems):
            every(buf, sems).wait_send()

        return SimpleNamespace(scatter=scatter, gather=gather, arrive=arrive, sent=sent)

    row = exchange(ny, j, lambda t: (i, t))
    column = exchange(nz, z, lambda t: (2 * t + core, j))
    layer = exchange(ng, g, layer_place)

    def slots_sum(ref):
        return jnp.sum(ref[...].astype(F32), axis=0)

    def reduce_stages(src, into, zbuf, everything, sums, sems):
        rs_sem, z_sem, ag_sem = sems

        def start():
            layer.scatter(src, into, rs_sem)

        def to_column():
            layer.arrive(into, rs_sem)
            zbuf[z] = slots_sum(into).astype(BF16)
            column.gather(zbuf, z_sem)

        def to_layer():
            column.arrive(zbuf, z_sem)
            sums[...] = slots_sum(zbuf)
            everything[g] = sums[...].astype(BF16)
            layer.gather(everything, ag_sem)

        def finish():
            layer.arrive(everything, ag_sem)

        def sent():
            layer.sent(into, rs_sem)
            column.sent(zbuf, z_sem)
            layer.sent(everything, ag_sem)

        return SimpleNamespace(
            start=start, to_column=to_column, to_layer=to_layer, finish=finish, sent=sent
        )

    a_stage = reduce_stages(
        r.a_src, r.a_in, r.a_z, r.a_all, r.a_sum, (r.a_rs_sem, r.a_z_sem, r.a_ag_sem)
    )
    b_stage = reduce_stages(
        r.b_src, r.b_in, r.b_z, r.b_all, r.b_sum, (r.b_rs_sem, r.b_z_sem, r.b_ag_sem)
    )

    def halo_copies(src, dst, sems):
        targets = ((up, j), (down, j), (i, left), (i, right))
        return [
            pltpu.make_async_remote_copy(
                src_ref=src.at[k],
                dst_ref=dst.at[k ^ 1],
                send_sem=sems.at[0, k],
                recv_sem=sems.at[1, k ^ 1],
                device_id=targets[k],
                device_id_type=MESH,
            )
            for k in range(4)
        ]

    present = (i > 0, i < nx - 1, j > 0, j < ny - 1)

    half_e, half_c = ext // 2, cells // 2

    def folded(line, half):
        return jnp.where(line >= half, line - half, line)

    def pick_half(high, both):
        return jnp.where(high, both[W:, :], both[:W, :])

    def halves(high, value):
        low = jnp.where(high, 0.0, value)
        return jnp.concatenate([low, value - low], axis=0).astype(BF16)

    def unfold(pairs):
        return jnp.concatenate([pairs[:, :W], pairs[:, W:]], axis=0)

    def fold_t(table, half):
        return jnp.concatenate([table[:, :half], table[:, half:]], axis=0)

    def to_coarse(value):
        low = jnp.where(r.own_high[...] > 0.5, 0.0, value)
        pairs = jnp.concatenate([low, value - low], axis=1).astype(BF16)
        return unfold(dot(r.own_t[...], pairs)).astype(BF16).reshape(ny, owned, W)

    def from_coarse(table):
        flat = table.reshape(cells, W)
        pairs = jnp.concatenate([flat[:half_c], flat[half_c:]], axis=1)
        both = dot(r.own_n[...], pairs)
        return jnp.where(r.own_high[...] > 0.5, both[:, W:], both[:, :W])

    def hot(line, count):
        parts = []
        for a in range(count // BLOCK):
            inside = jnp.where(lax.shift_right_arithmetic(line, 8) == a, line & 255, -1)
            inside = inside.astype(F32).astype(BF16)
            same = r.iota[:, : line.shape[1]] == inside
            parts.append(jnp.where(same, jnp.ones((), BF16), jnp.zeros((), BF16)))
        return jnp.concatenate(parts, axis=0)

    eye = (
        lax.broadcasted_iota(I32, (W, W), 0) == lax.broadcasted_iota(I32, (W, W), 1)
    ).astype(F32).astype(BF16)

    def turned(block):
        return right_t(eye, block).astype(BF16)

    r.iota[...] = lax.broadcasted_iota(I32, r.iota.shape, 0).astype(F32).astype(BF16)
    loads["slist"].wait()
    r.hot_list[...] = hot(lane_row(r.slist, 0, 4), cells)
    loads["nodes"].wait()
    r.ext_t[:, :cells] = turned(r.nodes[...])
    picked = dot(r.ext_t[:, :cells], r.hot_list[...]).astype(BF16)
    for k in range(4):
        r.pick[k] = picked[:, k * W : (k + 1) * W]
    loads["owner"].wait()
    r.own_t[...] = hot(folded(lane_row(r.owner, 0, cells // W), half_c), half_c)
    for q in range(cells // W):
        at = jnp.broadcast_to(r.owner[q : q + 1, :].astype(F32), (W, W)).T
        r.own_at[q * W : (q + 1) * W, :] = at
    r.own_high[...] = jnp.where(r.own_at[...] >= float(half_c), 1.0, 0.0)
    loads["cot"].wait()
    r.cot_src[...] = to_coarse(r.cot[...].astype(F32))

    pl.semaphore_wait(barrier, ng + nz - 1)
    halo_out = halo_copies(r.pick, r.halo, r.halo_sem)
    for copy in halo_out:
        copy.start()
    row.scatter(r.cot_src, r.cot_got, r.cot_sem)

    loads["snd"].wait()
    loads["rcv"].wait()
    per = tile // W
    live_load.wait()
    alive = r.live[0]

    def sender_row(t):
        return lane_row(r.snd, t * per, per)

    def receiver_row(t):
        place = t * tile + lax.broadcasted_iota(I32, (1, tile), 1)
        return jnp.where(place < alive, lane_row(r.rcv, t * per, per), -1)

    def high_s(t):
        return jnp.broadcast_to(sender_row(t), (W, tile)) >= half_e

    def high_r(t):
        return jnp.broadcast_to(receiver_row(t), (W, tile)) >= half_c

    def mark(t, c):
        r.marks[t, :half_e, :] = hot(folded(sender_row(t), half_e), half_e)
        r.marks[t, half_e:, :] = hot(folded(receiver_row(t), half_c), half_c)
        return c

    lax.fori_loop(0, tiles, mark, 0)

    loads["w_edge"].wait()
    loads["bias"].wait()
    ws_t, wr_t, we_t = [turned(r.w_edge[k]) for k in range(3)]
    b_col = jnp.broadcast_to(r.bias[0:1, :], (W, W)).T
    r.table_t[:, half_e:] = fold_t(dot(wr_t, r.ext_t[:, :cells]), half_c).astype(BF16)
    loads["feat"].wait()
    for copy in halo_out:
        copy.wait_recv()
    for k in range(4):
        r.ext_t[:, cells + k * W : cells + (k + 1) * W] = jnp.where(
            present[k], r.halo[k].astype(F32), 0.0
        ).astype(BF16)
    r.table_t[:, :half_e] = fold_t(
        dot(ws_t, r.ext_t[...]) + jnp.concatenate([b_col] * (ext // W), axis=1), half_e
    ).astype(BF16)

    r.h_acc[...] = jnp.zeros_like(r.h_acc)

    def edge_rows(t):
        return pl.ds(pl.multiple_of(t * tile, tile), tile)

    def forward(t, c):
        above = high_r(t)
        pre = (
            pick_half(high_s(t), dot(r.table_t[:, :half_e], r.marks[t, :half_e, :]))
            + pick_half(above, dot(r.table_t[:, half_e:], r.marks[t, half_e:, :]))
            + right_t(we_t, r.feat[edge_rows(t), :])
        )
        sigma = sigmoid(pre)
        r.slopes[t] = slope(pre, sigma)
        r.h_acc[...] += right_t(r.marks[t, half_e:, :], halves(above, pre * sigma))
        return c

    lax.fori_loop(0, tiles, forward, 0, unroll=2)

    loads["w_node"].wait()
    loads["w_coarse"].wait()
    r.hb[...] = unfold(r.h_acc[...]).astype(BF16)
    r.agg[...] = dot(r.hb[...], r.w_edge[3]).astype(BF16)
    pre_node = dot(r.nodes[...], r.w_node[0]) + dot(r.agg[...], r.w_node[1]) + r.bias[1:2, :]
    sigma = sigmoid(pre_node)
    r.node_slope[...] = slope(pre_node, sigma)
    r.hid[...] = (pre_node * sigma).astype(BF16)
    r.fine[...] = r.nodes[...].astype(F32) + dot(r.hid[...], r.w_node[2])
    r.fine_src[...] = to_coarse(r.fine[...])
    row.scatter(r.fine_src, r.fine_got, r.fine_sem)

    lanes = lax.broadcasted_iota(I32, (cells, W), 1).astype(F32)
    at = r.own_at[...] - float(half_c) * r.own_high[...]
    r.own_n[...] = jnp.concatenate(
        [jnp.where(at == lanes + float(k * W), 1.0, 0.0).astype(BF16) for k in range(half_c // W)],
        axis=1,
    )
    agg_t, hid_t, hb_t = turned(r.agg[...]), turned(r.hid[...]), turned(r.hb[...])

    row.arrive(r.cot_got, r.cot_sem)
    d_coarse = slots_sum(r.cot_got).astype(BF16)
    d_hidden = right_t(d_coarse, r.w_coarse[1])
    row.arrive(r.fine_got, r.fine_sem)
    coarse_bf = (0.0625 * slots_sum(r.fine_got)).astype(BF16)
    pre_coarse = dot(coarse_bf, r.w_coarse[0]) + r.bias[2:3, :]
    sigma = sigmoid(pre_coarse)
    coarse_hid = (pre_coarse * sigma).astype(BF16)
    d_pre_c = d_hidden * slope(pre_coarse, sigma)
    d_pre_c_bf = d_pre_c.astype(BF16)
    r.d_coarse_all[j] = right_t(d_pre_c_bf, r.w_coarse[0]).astype(BF16)
    row.gather(r.d_coarse_all, r.d_coarse_sem)
    r.coarse_all[j] = dot(coarse_hid, r.w_coarse[1]).astype(BF16)
    row.gather(r.coarse_all, r.coarse_sem)
    g_v1 = dot(turned(coarse_bf), d_pre_c_bf)
    g_v2 = dot(turned(coarse_hid), d_coarse)
    b_own = r.b_src.shape[1]
    a_own = 6 * W // ng
    share = 3 * W // ng
    r.bias_rows[...] = jnp.zeros_like(r.bias_rows)
    r.bias_rows[share + 2 : share + 3, :] = jnp.sum(d_pre_c, axis=0, keepdims=True)
    row.arrive(r.d_coarse_all, r.d_coarse_sem)

    d_fine = r.cot[...].astype(F32) + 0.0625 * from_coarse(r.d_coarse_all[...])
    d_fine_bf = d_fine.astype(BF16)
    d_pre_n = right_t(d_fine_bf, r.w_node[2]) * r.node_slope[...]
    d_pre_n_bf = d_pre_n.astype(BF16)
    r.bias_rows[share + 1 : share + 2, :] = jnp.sum(d_pre_n, axis=0, keepdims=True)
    r.d_part[...] = d_fine
    r.d_pre_n[...] = d_pre_n_bf
    d_agg = right_t(d_pre_n_bf, r.w_node[1]).astype(BF16)
    r.table_t[:, half_e:] = fold_t(right_t(r.w_edge[3], d_agg), half_c).astype(BF16)
    early = jnp.concatenate(
        [
            dot(hb_t, d_agg),
            dot(r.ext_t[:, :cells], d_pre_n_bf),
            dot(agg_t, d_pre_n_bf),
            dot(hid_t, d_fine_bf),
            g_v1,
            g_v2,
        ],
        axis=0,
    ).reshape(ng, a_own, W)
    spare = r.a_src.shape[1] - a_own
    if spare:
        early = jnp.concatenate([early, jnp.zeros((ng, spare, W), F32)], axis=1)
    r.a_src[...] = early.astype(BF16)
    a_stage.start()

    r.s_acc[...] = jnp.zeros_like(r.s_acc)
    r.r_acc[...] = jnp.zeros_like(r.r_acc)
    r.we_acc[...] = jnp.zeros_like(r.we_acc)

    def backward(t, c):
        above = high_r(t)
        got = pick_half(above, dot(r.table_t[:, half_e:], r.marks[t, half_e:, :]))
        d_pre = got * r.slopes[t]
        d_pre_bf = d_pre.astype(BF16)
        r.d_pre[t] = d_pre_bf
        r.s_acc[...] += right_t(r.marks[t, :half_e, :], halves(high_s(t), d_pre))
        r.r_acc[...] += right_t(r.marks[t, half_e:, :], halves(above, d_pre))
        r.we_acc[...] += dot(d_pre_bf, r.feat[edge_rows(t), :])
        return c

    def edge_out(t, c):
        r.d_edges[edge_rows(t), :] = dot(r.w_edge[2], r.d_pre[t]).T.astype(BF16)
        return c

    leaving = []

    def leave(k, src, dst):
        leaving.append(pltpu.make_async_copy(src, dst, r.out_sem.at[k]))
        leaving[-1].start()

    half = tiles // 2
    lax.fori_loop(0, tiles, backward, 0, unroll=2)
    a_stage.to_column()

    s_bf = unfold(r.s_acc[...]).astype(BF16)
    r_sum = unfold(r.r_acc[...])
    r_bf = r_sum.astype(BF16)
    r.back_src[...] = right_t(s_bf[cells:, :], r.w_edge[0]).astype(BF16).reshape(4, W, W)
    back_out = halo_copies(r.back_src, r.back_got, r.back_sem)
    for copy in back_out:
        copy.start()
    r.bias_rows[share : share + 1, :] = jnp.sum(r_sum, axis=0, keepdims=True)
    r.b_flat[: 3 * W, :] = jnp.concatenate(
        [dot(r.ext_t[...], s_bf), dot(r.ext_t[:, :cells], r_bf), r.we_acc[...].T], axis=0
    )
    r.b_flat[3 * W :, :] = jnp.zeros((b_own, W), F32)
    inner = lax.broadcasted_iota(I32, (b_own, W), 0) < share
    for k in range(ng):
        part = r.b_flat[k * share : k * share + b_own, :]
        r.b_src[k] = jnp.where(inner, part, r.bias_rows[...]).astype(BF16)
    b_stage.start()
    r.d_part[...] = (
        r.d_part[...]
        + right_t(r.d_pre_n[...], r.w_node[0])
        + right_t(s_bf[:cells, :], r.w_edge[0])
        + right_t(r_bf, r.w_edge[1])
    )
    for copy in back_out:
        copy.wait_recv()
    returned = jnp.concatenate(
        [jnp.where(present[k], r.back_got[k].astype(F32), 0.0) for k in range(4)], axis=0
    ).astype(BF16)
    r.d_nodes[...] = (r.d_part[...] + dot(r.hot_list[...], returned)).astype(BF16)
    leave(0, r.d_nodes, r.d_nodes_out)
    b_stage.to_column()
    a_stage.to_layer()
    lax.fori_loop(0, half, edge_out, 0)
    first, second = pl.ds(0, half * tile), pl.ds(half * tile, (tiles - half) * tile)
    leave(1, r.d_edges.at[first], r.d_edges_out.at[first])
    row.arrive(r.coarse_all, r.coarse_sem)
    r.node_out[...] = (r.fine[...] + from_coarse(r.coarse_all[...])).astype(BF16)
    leave(2, r.node_out, r.node_out_out)
    b_stage.to_layer()
    lax.fori_loop(half, tiles, edge_out, 0)
    leave(3, r.d_edges.at[second], r.d_edges_out.at[second])
    r.bias_grads[...] = r.b_sum[share : share + 3, :]
    leave(4, r.bias_grads, r.bias_grads_out)
    a_stage.finish()
    r.grads[3 * W :, :] = r.a_all[...].astype(F32)[:, :a_own, :].reshape(6 * W, W)
    late, soon = pl.ds(0, 3 * W), pl.ds(3 * W, 6 * W)
    leave(5, r.grads.at[soon], r.grads_out.at[soon])
    row.sent(r.cot_got, r.cot_sem)
    row.sent(r.fine_got, r.fine_sem)
    row.sent(r.coarse_all, r.coarse_sem)
    row.sent(r.d_coarse_all, r.d_coarse_sem)
    for copy in halo_out + back_out:
        copy.wait_send()
    a_stage.sent()
    layer.sent(r.b_in, r.b_rs_sem)
    column.sent(r.b_z, r.b_z_sem)
    b_stage.finish()
    for k in range(ng):
        r.grads[k * share : (k + 1) * share, :] = r.b_all[k].astype(F32)[:share, :]
    leave(6, r.grads.at[late], r.grads_out.at[late])
    layer.sent(r.b_all, r.b_ag_sem)
    for copy in leaving:
        copy.wait()


def settle(cuts, *refs):
    count = len(cuts)
    held, sems = refs[2 * count : 3 * count], refs[3 * count]
    pieces = []
    for k, parts in enumerate(cuts):
        rows = refs[k].shape[0] // parts
        pieces += [(k, pl.ds(p * rows, rows)) for p in range(parts)]
    gets = [
        pltpu.make_async_copy(refs[k].at[here], held[k].at[here], sems.at[0, n])
        for n, (k, here) in enumerate(pieces)
    ]
    puts = [
        pltpu.make_async_copy(held[k].at[here], refs[count + k].at[here], sems.at[1, n])
        for n, (k, here) in enumerate(pieces)
    ]
    for get in gets:
        get.start()
    for get, put in zip(gets, puts):
        get.wait()
        put.start()
    for put in puts:
        put.wait()


def body(
    dims,
    nodes,
    edge_feat,
    senders,
    receivers,
    send_lists,
    owner,
    edge_live,
    cotangent,
    w_edge,
    w_node,
    w_coarse,
    biases,
):
    nx, ny, cells, edges, tile = dims
    nz = nx // 2
    ng = 2 * ny
    ext = cells + 4 * W
    owned = cells // ny
    a_rows = -(-(6 * W // ng) // 16) * 16
    b_rows = -(-(3 * W // ng + 3) // 16) * 16
    operands = dict(
        nodes=nodes,
        feat=edge_feat,
        snd=senders.reshape(edges // W, W),
        rcv=receivers.reshape(edges // W, W),
        slist=send_lists.reshape(4, W),
        owner=owner.reshape(cells // W, W),
        cot=cotangent,
        w_edge=w_edge,
        w_node=w_node,
        w_coarse=w_coarse,
        bias=biases,
    )
    shapes = (
        jax.ShapeDtypeStruct((cells, W), BF16),
        jax.ShapeDtypeStruct((cells, W), BF16),
        jax.ShapeDtypeStruct((edges, W), BF16),
        jax.ShapeDtypeStruct((9 * W, W), F32),
        jax.ShapeDtypeStruct((3, W), F32),
    )
    scratch = {name: pltpu.VMEM(operands[name].shape, operands[name].dtype) for name in INPUTS}
    scratch |= {name: pltpu.VMEM(s.shape, s.dtype) for name, s in zip(OUTPUTS, shapes)}
    scratch |= dict(
        iota=pltpu.VMEM((BLOCK, max(cells, tile)), BF16),
        ext_t=pltpu.VMEM((W, ext), BF16),
        table_t=pltpu.VMEM((2 * W, (ext + cells) // 2), BF16),
        marks=pltpu.VMEM((edges // tile, (ext + cells) // 2, tile), BF16),
        hot_list=pltpu.VMEM((cells, 4 * W), BF16),
        own_t=pltpu.VMEM((cells // 2, cells), BF16),
        own_n=pltpu.VMEM((cells, cells // 2), BF16),
        own_at=pltpu.VMEM((cells, W), F32),
        own_high=pltpu.VMEM((cells, W), F32),
        pick=pltpu.VMEM((4, W, W), BF16),
        halo=pltpu.VMEM((4, W, W), BF16),
        slopes=pltpu.VMEM((edges // tile, W, tile), F32),
        d_pre=pltpu.VMEM((edges // tile, W, tile), BF16),
        h_acc=pltpu.VMEM((cells // 2, 2 * W), F32),
        s_acc=pltpu.VMEM((ext // 2, 2 * W), F32),
        r_acc=pltpu.VMEM((cells // 2, 2 * W), F32),
        we_acc=pltpu.VMEM((W, W), F32),
        fine=pltpu.VMEM((cells, W), F32),
        node_slope=pltpu.VMEM((cells, W), F32),
        d_part=pltpu.VMEM((cells, W), F32),
        hb=pltpu.VMEM((cells, W), BF16),
        agg=pltpu.VMEM((cells, W), BF16),
        hid=pltpu.VMEM((cells, W), BF16),
        cot_src=pltpu.VMEM((ny, owned, W), BF16),
        cot_got=pltpu.VMEM((ny, owned, W), BF16),
        fine_src=pltpu.VMEM((ny, owned, W), BF16),
        fine_got=pltpu.VMEM((ny, owned, W), BF16),
        coarse_all=pltpu.VMEM((ny, owned, W), BF16),
        d_coarse_all=pltpu.VMEM((ny, owned, W), BF16),
        d_pre_n=pltpu.VMEM((cells, W), BF16),
        back_src=pltpu.VMEM((4, W, W), BF16),
        back_got=pltpu.VMEM((4, W, W), BF16),
        bias_rows=pltpu.VMEM((b_rows, W), F32),
        b_flat=pltpu.VMEM((3 * W + b_rows, W), F32),
        live=pltpu.SMEM((1,), I32),
        load_sem=pltpu.SemaphoreType.DMA((len(INPUTS) + 1,)),
        halo_sem=pltpu.SemaphoreType.DMA((2, 4)),
        back_sem=pltpu.SemaphoreType.DMA((2, 4)),
        cot_sem=pltpu.SemaphoreType.DMA((2,)),
        fine_sem=pltpu.SemaphoreType.DMA((2,)),
        coarse_sem=pltpu.SemaphoreType.DMA((2,)),
        d_coarse_sem=pltpu.SemaphoreType.DMA((2,)),
        out_sem=pltpu.SemaphoreType.DMA((7,)),
    )
    for name, rows in (("a", a_rows), ("b", b_rows)):
        scratch |= {
            name + "_src": pltpu.VMEM((ng, rows, W), BF16),
            name + "_in": pltpu.VMEM((ng, rows, W), BF16),
            name + "_z": pltpu.VMEM((nz, rows, W), BF16),
            name + "_all": pltpu.VMEM((ng, rows, W), BF16),
            name + "_sum": pltpu.VMEM((rows, W), F32),
            name + "_rs_sem": pltpu.SemaphoreType.DMA((2,)),
            name + "_z_sem": pltpu.SemaphoreType.DMA((2,)),
            name + "_ag_sem": pltpu.SemaphoreType.DMA((2,)),
        }
    names = tuple(name + "_in" for name in INPUTS) + ("live_in",)
    names += tuple(name + "_out" for name in OUTPUTS) + tuple(scratch)
    hbm = pl.BlockSpec(memory_space=pltpu.HBM)
    outs = pl.pallas_call(
        functools.partial(kernel, dims, names),
        out_shape=shapes,
        in_specs=[hbm] * (len(INPUTS) + 1),
        out_specs=(hbm,) * 5,
        scratch_shapes=list(scratch.values()),
        compiler_params=pltpu.CompilerParams(
            collective_id=0, has_side_effects=True, vmem_limit_bytes=61440 * 1024
        ),
        cost_estimate=pl.CostEstimate(
            flops=2 * edges * W * (2 * ext + 4 * cells + 4 * W),
            bytes_accessed=2 * W * (2 * edges + 4 * cells),
            transcendentals=edges * W,
        ),
        name="mesh_step",
    )(*[operands[name] for name in INPUTS], edge_live)
    cuts = (1, 1, 4, 2, 1)
    outs = pl.pallas_call(
        functools.partial(settle, cuts),
        out_shape=shapes,
        in_specs=[hbm] * 5,
        out_specs=(hbm,) * 5,
        scratch_shapes=[pltpu.VMEM(s.shape, s.dtype) for s in shapes]
        + [pltpu.SemaphoreType.DMA((2, sum(cuts)))],
        compiler_params=pltpu.CompilerParams(vmem_limit_bytes=60 * 1024 * 1024),
        name="settle",
    )(*outs)
    node_out, d_nodes, d_edges, grads, bias_grads = outs
    return node_out, d_nodes, d_edges, grads.reshape(9, W, W), bias_grads


def solution(mesh, cells=1024, edges=4096, tile=1024):
    both = ("gx", "gy")
    dims = (mesh.shape["gx"], mesh.shape["gy"], cells, edges, tile)
    in_specs = (
        P(both, None),
        P(both, None),
        P(both),
        P(both),
        P(both, None, None),
        P(both),
        P(both),
        P(both, None),
        P(),
        P(),
        P(),
        P(),
    )
    out_specs = (P(both, None), P(both, None), P(both, None), P(), P())
    return jax.shard_map(
        functools.partial(body, dims),
        mesh=mesh,
        in_specs=in_specs,
        out_specs=out_specs,
        check_vma=False,
    )
```

```python
import functools
from types import SimpleNamespace

import jax
import jax.numpy as jnp
from jax import lax
from jax.experimental import pallas as pl
from jax.experimental.pallas import tpu as pltpu
from jax.sharding import PartitionSpec as P

F32, BF16, I32 = jnp.float32, jnp.bfloat16, jnp.int32
W = 128
BLOCK = 256
MESH = pl.DeviceIdType.MESH


def dot(left, right):
    return jnp.dot(left, right, preferred_element_type=F32)


def right_t(left, right):
    return lax.dot_general(left, right, (((1,), (1,)), ((), ())), preferred_element_type=F32)


def sigmoid(value):
    return 0.5 * jnp.tanh(0.5 * value) + 0.5


def slope(value, sigma):
    return sigma * (1.0 + value * (1.0 - sigma))


def lane_row(ref, first, count):
    return jnp.concatenate([ref[pl.ds(first + q, 1), :] for q in range(count)], axis=1)


INPUTS = (
    "nodes", "feat", "snd", "rcv", "slist", "owner", "cot", "w_edge", "w_node", "w_coarse", "bias"
)
ORDER = (
    "slist", "nodes", "owner", "cot", "snd", "rcv", "w_edge", "bias", "feat", "w_node", "w_coarse"
)
OUTPUTS = ("node_out", "d_nodes", "d_edges", "grads", "bias_grads")


def kernel(dims, names, *refs):
    r = SimpleNamespace(**dict(zip(names, refs)))
    nx, ny, cells, edges, tile = dims
    nz = nx // 2
    ng = 2 * ny
    ext = cells + 4 * W
    owned = cells // ny
    tiles = edges // tile
    i, j = lax.axis_index("gx"), lax.axis_index("gy")
    core, z = lax.rem(i, 2), lax.div(i, 2)
    g = core * ny + j
    up, down = lax.rem(i + nx - 1, nx), lax.rem(i + 1, nx)
    left, right = lax.rem(j + ny - 1, ny), lax.rem(j + 1, ny)
    across = lax.rem(i + nx - 1 + 2 * core, nx)

    barrier = pltpu.get_barrier_semaphore()

    def greet(gx, gy):
        pl.semaphore_signal(barrier, inc=1, device_id=(gx, gy), device_id_type=MESH)

    def each(count, me, action):
        some = 5 if count > 5 else 1
        first = 1 + (count - 1) % some
        for d in range(1, first):
            action(me ^ d)

        def step(k, c):
            for u in range(some):
                action(me ^ (first + k * some + u))
            return c

        lax.fori_loop(0, (count - first) // some, step, 0)

    shift = ny.bit_length() - 1

    def layer_place(t):
        return 2 * z + lax.shift_right_logical(t, shift), t & (ny - 1)

    greet(across, j)
    loads = {
        name: pltpu.make_async_copy(
            getattr(r, name + "_in"), getattr(r, name), r.load_sem.at[k]
        )
        for k, name in enumerate(ORDER)
    }
    for name in ORDER:
        loads[name].start()
    each(ng, g, lambda t: greet(*layer_place(t)))
    each(nz, z, lambda t: greet(2 * t + core, j))

    def exchange(count, me, place):
        def copy(src, dst, sems, target):
            return pltpu.make_async_remote_copy(
                src_ref=src,
                dst_ref=dst,
                send_sem=sems.at[0],
                recv_sem=sems.at[1],
                device_id=place(target),
                device_id_type=MESH,
            )

        def scatter(src, dst, sems):
            dst[me] = src[me]
            each(count, me, lambda t: copy(src.at[t], dst.at[me], sems, t).start())

        def gather(buf, sems):
            each(count, me, lambda t: copy(buf.at[me], buf.at[me], sems, t).start())

        def every(buf, sems):
            others = buf.at[pl.ds(0, count - 1)]
            return copy(others, others, sems, me ^ 1)

        def arrive(buf, sems):
            every(buf, sems).wait_recv()

        def sent(buf, sems):
            every(buf, sems).wait_send()

        return SimpleNamespace(scatter=scatter, gather=gather, arrive=arrive, sent=sent)

    row = exchange(ny, j, lambda t: (i, t))
    column = exchange(nz, z, lambda t: (2 * t + core, j))
    layer = exchange(ng, g, layer_place)

    def slots_sum(ref):
        return jnp.sum(ref[...].astype(F32), axis=0)

    def reduce_stages(src, into, zbuf, everything, sums, sems):
        rs_sem, z_sem, ag_sem = sems

        def start():
            layer.scatter(src, into, rs_sem)

        def to_column():
            layer.arrive(into, rs_sem)
            zbuf[z] = slots_sum(into).astype(BF16)
            column.gather(zbuf, z_sem)

        def to_layer():
            column.arrive(zbuf, z_sem)
            sums[...] = slots_sum(zbuf)
            everything[g] = sums[...].astype(BF16)
            layer.gather(everything, ag_sem)

        def finish():
            layer.arrive(everything, ag_sem)

        def sent():
            layer.sent(into, rs_sem)
            column.sent(zbuf, z_sem)
            layer.sent(everything, ag_sem)

        return SimpleNamespace(
            start=start, to_column=to_column, to_layer=to_layer, finish=finish, sent=sent
        )

    a_stage = reduce_stages(
        r.a_src, r.a_in, r.a_z, r.a_all, r.a_sum, (r.a_rs_sem, r.a_z_sem, r.a_ag_sem)
    )
    b_stage = reduce_stages(
        r.b_src, r.b_in, r.b_z, r.b_all, r.b_sum, (r.b_rs_sem, r.b_z_sem, r.b_ag_sem)
    )

    def halo_copies(src, dst, sems):
        targets = ((up, j), (down, j), (i, left), (i, right))
        return [
            pltpu.make_async_remote_copy(
                src_ref=src.at[k],
                dst_ref=dst.at[k ^ 1],
                send_sem=sems.at[0, k],
                recv_sem=sems.at[1, k ^ 1],
                device_id=targets[k],
                device_id_type=MESH,
            )
            for k in range(4)
        ]

    present = (i > 0, i < nx - 1, j > 0, j < ny - 1)

    half_e, half_c = ext // 2, cells // 2

    def folded(line, half):
        return jnp.where(line >= half, line - half, line)

    def pick_half(high, both):
        return jnp.where(high, both[W:, :], both[:W, :])

    def halves(high, value):
        low = jnp.where(high, 0.0, value)
        return jnp.concatenate([low, value - low], axis=0).astype(BF16)

    def unfold(pairs):
        return jnp.concatenate([pairs[:, :W], pairs[:, W:]], axis=0)

    def fold_t(table, half):
        return jnp.concatenate([table[:, :half], table[:, half:]], axis=0)

    def to_coarse(value):
        low = jnp.where(r.own_high[...] > 0.5, 0.0, value)
        pairs = jnp.concatenate([low, value - low], axis=1).astype(BF16)
        return unfold(dot(r.own_t[...], pairs)).astype(BF16).reshape(ny, owned, W)

    def from_coarse(table):
        flat = table.reshape(cells, W)
        pairs = jnp.concatenate([flat[:half_c], flat[half_c:]], axis=1)
        both = dot(r.own_n[...], pairs)
        return jnp.where(r.own_high[...] > 0.5, both[:, W:], both[:, :W])

    def hot(line, count):
        parts = []
        for a in range(count // BLOCK):
            inside = jnp.where(lax.shift_right_arithmetic(line, 8) == a, line & 255, -1)
            inside = inside.astype(F32).astype(BF16)
            same = r.iota[:, : line.shape[1]] == inside
            parts.append(jnp.where(same, jnp.ones((), BF16), jnp.zeros((), BF16)))
        return jnp.concatenate(parts, axis=0)

    eye = (
        lax.broadcasted_iota(I32, (W, W), 0) == lax.broadcasted_iota(I32, (W, W), 1)
    ).astype(F32).astype(BF16)

    def turned(block):
        return right_t(eye, block).astype(BF16)

    r.iota[...] = lax.broadcasted_iota(I32, r.iota.shape, 0).astype(F32).astype(BF16)
    loads["slist"].wait()
    r.hot_list[...] = hot(lane_row(r.slist, 0, 4), cells)
    loads["nodes"].wait()
    r.ext_t[:, :cells] = turned(r.nodes[...])
    picked = dot(r.ext_t[:, :cells], r.hot_list[...]).astype(BF16)
    for k in range(4):
        r.pick[k] = picked[:, k * W : (k + 1) * W]
    loads["owner"].wait()
    r.own_t[...] = hot(folded(lane_row(r.owner, 0, cells // W), half_c), half_c)
    for q in range(cells // W):
        at = jnp.broadcast_to(r.owner[q : q + 1, :].astype(F32), (W, W)).T
        r.own_at[q * W : (q + 1) * W, :] = at
    r.own_high[...] = jnp.where(r.own_at[...] >= float(half_c), 1.0, 0.0)
    loads["cot"].wait()
    r.cot_src[...] = to_coarse(r.cot[...].astype(F32))

    pl.semaphore_wait(barrier, ng + nz - 1)
    halo_out = halo_copies(r.pick, r.halo, r.halo_sem)
    for copy in halo_out:
        copy.start()
    row.scatter(r.cot_src, r.cot_got, r.cot_sem)

    loads["snd"].wait()
    loads["rcv"].wait()
    per = tile // W
    alive = r.live[0]

    def sender_row(t):
        return lane_row(r.snd, t * per, per)

    def receiver_row(t):
        place = t * tile + lax.broadcasted_iota(I32, (1, tile), 1)
        return jnp.where(place < alive, lane_row(r.rcv, t * per, per), -1)

    def high_s(t):
        return jnp.broadcast_to(sender_row(t), (W, tile)) >= half_e

    def high_r(t):
        return jnp.broadcast_to(receiver_row(t), (W, tile)) >= half_c

    def mark(t, c):
        r.marks[t, :half_e, :] = hot(folded(sender_row(t), half_e), half_e)
        r.marks[t, half_e:, :] = hot(folded(receiver_row(t), half_c), half_c)
        return c

    mark(0, 0)

    loads["w_edge"].wait()
    loads["bias"].wait()
    ws_t, wr_t, we_t = [turned(r.w_edge[k]) for k in range(3)]
    b_col = jnp.broadcast_to(r.bias[0:1, :], (W, W)).T
    r.table_t[:, half_e:] = fold_t(dot(wr_t, r.ext_t[:, :cells]), half_c).astype(BF16)
    loads["feat"].wait()
    for copy in halo_out:
        copy.wait_recv()
    for k in range(4):
        r.ext_t[:, cells + k * W : cells + (k + 1) * W] = jnp.where(
            present[k], r.halo[k].astype(F32), 0.0
        ).astype(BF16)
    r.table_t[:, :half_e] = fold_t(
        dot(ws_t, r.ext_t[...]) + jnp.concatenate([b_col] * (ext // W), axis=1), half_e
    ).astype(BF16)

    r.h_acc[...] = jnp.zeros_like(r.h_acc)

    def edge_rows(t):
        return pl.ds(t * tile if isinstance(t, int) else pl.multiple_of(t * tile, tile), tile)

    def forward(t, c):
        above = high_r(t)
        pre = (
            pick_half(high_s(t), dot(r.table_t[:, :half_e], r.marks[t, :half_e, :]))
            + pick_half(above, dot(r.table_t[:, half_e:], r.marks[t, half_e:, :]))
            + right_t(we_t, r.feat[edge_rows(t), :])
        )
        sigma = sigmoid(pre)
        r.slopes[t] = slope(pre, sigma)
        r.h_acc[...] += right_t(r.marks[t, half_e:, :], halves(above, pre * sigma))
        return c

    for t in range(tiles):
        if t + 1 < tiles:
            mark(t + 1, 0)
        forward(t, 0)

    loads["w_node"].wait()
    loads["w_coarse"].wait()
    r.hb[...] = unfold(r.h_acc[...]).astype(BF16)
    r.agg[...] = dot(r.hb[...], r.w_edge[3]).astype(BF16)
    pre_node = dot(r.nodes[...], r.w_node[0]) + dot(r.agg[...], r.w_node[1]) + r.bias[1:2, :]
    sigma = sigmoid(pre_node)
    r.node_slope[...] = slope(pre_node, sigma)
    r.hid[...] = (pre_node * sigma).astype(BF16)
    r.fine[...] = r.nodes[...].astype(F32) + dot(r.hid[...], r.w_node[2])
    r.fine_src[...] = to_coarse(r.fine[...])
    row.scatter(r.fine_src, r.fine_got, r.fine_sem)

    lanes = lax.broadcasted_iota(I32, (cells, W), 1).astype(F32)
    at = r.own_at[...] - float(half_c) * r.own_high[...]
    r.own_n[...] = jnp.concatenate(
        [jnp.where(at == lanes + float(k * W), 1.0, 0.0).astype(BF16) for k in range(half_c // W)],
        axis=1,
    )
    agg_t, hid_t, hb_t = turned(r.agg[...]), turned(r.hid[...]), turned(r.hb[...])

    row.arrive(r.cot_got, r.cot_sem)
    d_coarse = slots_sum(r.cot_got).astype(BF16)
    d_hidden = right_t(d_coarse, r.w_coarse[1])
    row.arrive(r.fine_got, r.fine_sem)
    coarse_bf = (0.0625 * slots_sum(r.fine_got)).astype(BF16)
    pre_coarse = dot(coarse_bf, r.w_coarse[0]) + r.bias[2:3, :]
    sigma = sigmoid(pre_coarse)
    coarse_hid = (pre_coarse * sigma).astype(BF16)
    d_pre_c = d_hidden * slope(pre_coarse, sigma)
    d_pre_c_bf = d_pre_c.astype(BF16)
    r.d_coarse_all[j] = right_t(d_pre_c_bf, r.w_coarse[0]).astype(BF16)
    row.gather(r.d_coarse_all, r.d_coarse_sem)
    r.coarse_all[j] = dot(coarse_hid, r.w_coarse[1]).astype(BF16)
    row.gather(r.coarse_all, r.coarse_sem)
    g_v1 = dot(turned(coarse_bf), d_pre_c_bf)
    g_v2 = dot(turned(coarse_hid), d_coarse)
    b_own = r.b_src.shape[1]
    a_own = 6 * W // ng
    share = 3 * W // ng
    r.bias_rows[...] = jnp.zeros_like(r.bias_rows)
    r.bias_rows[share + 2 : share + 3, :] = jnp.sum(d_pre_c, axis=0, keepdims=True)
    row.arrive(r.d_coarse_all, r.d_coarse_sem)

    d_fine = r.cot[...].astype(F32) + 0.0625 * from_coarse(r.d_coarse_all[...])
    d_fine_bf = d_fine.astype(BF16)
    d_pre_n = right_t(d_fine_bf, r.w_node[2]) * r.node_slope[...]
    d_pre_n_bf = d_pre_n.astype(BF16)
    r.bias_rows[share + 1 : share + 2, :] = jnp.sum(d_pre_n, axis=0, keepdims=True)
    r.d_part[...] = d_fine
    r.d_pre_n[...] = d_pre_n_bf
    d_agg = right_t(d_pre_n_bf, r.w_node[1]).astype(BF16)
    r.table_t[:, half_e:] = fold_t(right_t(r.w_edge[3], d_agg), half_c).astype(BF16)
    early = jnp.concatenate(
        [
            dot(hb_t, d_agg),
            dot(r.ext_t[:, :cells], d_pre_n_bf),
            dot(agg_t, d_pre_n_bf),
            dot(hid_t, d_fine_bf),
            g_v1,
            g_v2,
        ],
        axis=0,
    ).reshape(ng, a_own, W)
    spare = r.a_src.shape[1] - a_own
    if spare:
        early = jnp.concatenate([early, jnp.zeros((ng, spare, W), F32)], axis=1)
    r.a_src[...] = early.astype(BF16)
    a_stage.start()

    r.s_acc[...] = jnp.zeros_like(r.s_acc)
    r.r_acc[...] = jnp.zeros_like(r.r_acc)
    r.we_acc[...] = jnp.zeros_like(r.we_acc)

    def backward(t, c):
        above = high_r(t)
        got = pick_half(above, dot(r.table_t[:, half_e:], r.marks[t, half_e:, :]))
        d_pre = got * r.slopes[t]
        d_pre_bf = d_pre.astype(BF16)
        r.d_pre[t] = d_pre_bf
        r.s_acc[...] += right_t(r.marks[t, :half_e, :], halves(high_s(t), d_pre))
        r.r_acc[...] += right_t(r.marks[t, half_e:, :], halves(above, d_pre))
        r.we_acc[...] += dot(d_pre_bf, r.feat[edge_rows(t), :])
        return c

    def edge_out(t, c):
        r.d_edges[edge_rows(t), :] = dot(r.w_edge[2], r.d_pre[t]).T.astype(BF16)
        return c

    leaving = []

    def leave(k, src, dst):
        leaving.append(pltpu.make_async_copy(src, dst, r.out_sem.at[k]))
        leaving[-1].start()

    half = tiles // 2
    for t in range(tiles):
        backward(t, 0)
    a_stage.to_column()

    s_bf = unfold(r.s_acc[...]).astype(BF16)
    r_sum = unfold(r.r_acc[...])
    r_bf = r_sum.astype(BF16)
    r.back_src[...] = right_t(s_bf[cells:, :], r.w_edge[0]).astype(BF16).reshape(4, W, W)
    back_out = halo_copies(r.back_src, r.back_got, r.back_sem)
    for copy in back_out:
        copy.start()
    r.bias_rows[share : share + 1, :] = jnp.sum(r_sum, axis=0, keepdims=True)
    r.b_flat[: 3 * W, :] = jnp.concatenate(
        [dot(r.ext_t[...], s_bf), dot(r.ext_t[:, :cells], r_bf), r.we_acc[...].T], axis=0
    )
    r.b_flat[3 * W :, :] = jnp.zeros((b_own, W), F32)
    inner = lax.broadcasted_iota(I32, (b_own, W), 0) < share
    for k in range(ng):
        part = r.b_flat[k * share : k * share + b_own, :]
        r.b_src[k] = jnp.where(inner, part, r.bias_rows[...]).astype(BF16)
    b_stage.start()
    r.d_part[...] = (
        r.d_part[...]
        + right_t(r.d_pre_n[...], r.w_node[0])
        + right_t(s_bf[:cells, :], r.w_edge[0])
        + right_t(r_bf, r.w_edge[1])
    )
    for copy in back_out:
        copy.wait_recv()
    returned = jnp.concatenate(
        [jnp.where(present[k], r.back_got[k].astype(F32), 0.0) for k in range(4)], axis=0
    ).astype(BF16)
    r.d_nodes[...] = (r.d_part[...] + dot(r.hot_list[...], returned)).astype(BF16)
    leave(0, r.d_nodes, r.d_nodes_out)
    b_stage.to_column()
    a_stage.to_layer()
    lax.fori_loop(0, half, edge_out, 0)
    first, second = pl.ds(0, half * tile), pl.ds(half * tile, (tiles - half) * tile)
    leave(1, r.d_edges.at[first], r.d_edges_out.at[first])
    row.arrive(r.coarse_all, r.coarse_sem)
    r.node_out[...] = (r.fine[...] + from_coarse(r.coarse_all[...])).astype(BF16)
    leave(2, r.node_out, r.node_out_out)
    b_stage.to_layer()
    lax.fori_loop(half, tiles, edge_out, 0)
    leave(3, r.d_edges.at[second], r.d_edges_out.at[second])
    r.bias_grads[...] = r.b_sum[share : share + 3, :]
    leave(4, r.bias_grads, r.bias_grads_out)
    a_stage.finish()
    r.grads[3 * W :, :] = r.a_all[...].astype(F32)[:, :a_own, :].reshape(6 * W, W)
    late, soon = pl.ds(0, 3 * W), pl.ds(3 * W, 6 * W)
    leave(5, r.grads.at[soon], r.grads_out.at[soon])
    row.sent(r.cot_got, r.cot_sem)
    row.sent(r.fine_got, r.fine_sem)
    row.sent(r.coarse_all, r.coarse_sem)
    row.sent(r.d_coarse_all, r.d_coarse_sem)
    for copy in halo_out + back_out:
        copy.wait_send()
    a_stage.sent()
    layer.sent(r.b_in, r.b_rs_sem)
    column.sent(r.b_z, r.b_z_sem)
    b_stage.finish()
    for k in range(ng):
        r.grads[k * share : (k + 1) * share, :] = r.b_all[k].astype(F32)[:share, :]
    leave(6, r.grads.at[late], r.grads_out.at[late])
    layer.sent(r.b_all, r.b_ag_sem)
    for copy in leaving:
        copy.wait()


def settle(cuts, *refs):
    count = len(cuts)
    held, sems = refs[2 * count : 3 * count], refs[3 * count]
    pieces = []
    for k, parts in enumerate(cuts):
        rows = refs[k].shape[0] // parts
        pieces += [(k, pl.ds(p * rows, rows)) for p in range(parts)]
    gets = [
        pltpu.make_async_copy(refs[k].at[here], held[k].at[here], sems.at[0, n])
        for n, (k, here) in enumerate(pieces)
    ]
    puts = [
        pltpu.make_async_copy(held[k].at[here], refs[count + k].at[here], sems.at[1, n])
        for n, (k, here) in enumerate(pieces)
    ]
    for get in gets:
        get.start()
    for get, put in zip(gets, puts):
        get.wait()
        put.start()
    for put in puts:
        put.wait()


def body(
    dims,
    nodes,
    edge_feat,
    senders,
    receivers,
    send_lists,
    owner,
    edge_live,
    cotangent,
    w_edge,
    w_node,
    w_coarse,
    biases,
):
    nx, ny, cells, edges, tile = dims
    nz = nx // 2
    ng = 2 * ny
    ext = cells + 4 * W
    owned = cells // ny
    a_rows = -(-(6 * W // ng) // 16) * 16
    b_rows = -(-(3 * W // ng + 3) // 16) * 16
    operands = dict(
        nodes=nodes,
        feat=edge_feat,
        snd=senders.reshape(edges // W, W),
        rcv=receivers.reshape(edges // W, W),
        slist=send_lists.reshape(4, W),
        owner=owner.reshape(cells // W, W),
        cot=cotangent,
        w_edge=w_edge,
        w_node=w_node,
        w_coarse=w_coarse,
        bias=biases,
    )
    shapes = (
        jax.ShapeDtypeStruct((cells, W), BF16),
        jax.ShapeDtypeStruct((cells, W), BF16),
        jax.ShapeDtypeStruct((edges, W), BF16),
        jax.ShapeDtypeStruct((9 * W, W), F32),
        jax.ShapeDtypeStruct((3, W), F32),
    )
    scratch = {name: pltpu.VMEM(operands[name].shape, operands[name].dtype) for name in INPUTS}
    scratch |= {name: pltpu.VMEM(s.shape, s.dtype) for name, s in zip(OUTPUTS, shapes)}
    scratch |= dict(
        iota=pltpu.VMEM((BLOCK, max(cells, tile)), BF16),
        ext_t=pltpu.VMEM((W, ext), BF16),
        table_t=pltpu.VMEM((2 * W, (ext + cells) // 2), BF16),
        marks=pltpu.VMEM((edges // tile, (ext + cells) // 2, tile), BF16),
        hot_list=pltpu.VMEM((cells, 4 * W), BF16),
        own_t=pltpu.VMEM((cells // 2, cells), BF16),
        own_n=pltpu.VMEM((cells, cells // 2), BF16),
        own_at=pltpu.VMEM((cells, W), F32),
        own_high=pltpu.VMEM((cells, W), F32),
        pick=pltpu.VMEM((4, W, W), BF16),
        halo=pltpu.VMEM((4, W, W), BF16),
        slopes=pltpu.VMEM((edges // tile, W, tile), F32),
        d_pre=pltpu.VMEM((edges // tile, W, tile), BF16),
        h_acc=pltpu.VMEM((cells // 2, 2 * W), F32),
        s_acc=pltpu.VMEM((ext // 2, 2 * W), F32),
        r_acc=pltpu.VMEM((cells // 2, 2 * W), F32),
        we_acc=pltpu.VMEM((W, W), F32),
        fine=pltpu.VMEM((cells, W), F32),
        node_slope=pltpu.VMEM((cells, W), F32),
        d_part=pltpu.VMEM((cells, W), F32),
        hb=pltpu.VMEM((cells, W), BF16),
        agg=pltpu.VMEM((cells, W), BF16),
        hid=pltpu.VMEM((cells, W), BF16),
        cot_src=pltpu.VMEM((ny, owned, W), BF16),
        cot_got=pltpu.VMEM((ny, owned, W), BF16),
        fine_src=pltpu.VMEM((ny, owned, W), BF16),
        fine_got=pltpu.VMEM((ny, owned, W), BF16),
        coarse_all=pltpu.VMEM((ny, owned, W), BF16),
        d_coarse_all=pltpu.VMEM((ny, owned, W), BF16),
        d_pre_n=pltpu.VMEM((cells, W), BF16),
        back_src=pltpu.VMEM((4, W, W), BF16),
        back_got=pltpu.VMEM((4, W, W), BF16),
        bias_rows=pltpu.VMEM((b_rows, W), F32),
        b_flat=pltpu.VMEM((3 * W + b_rows, W), F32),
        load_sem=pltpu.SemaphoreType.DMA((len(INPUTS),)),
        halo_sem=pltpu.SemaphoreType.DMA((2, 4)),
        back_sem=pltpu.SemaphoreType.DMA((2, 4)),
        cot_sem=pltpu.SemaphoreType.DMA((2,)),
        fine_sem=pltpu.SemaphoreType.DMA((2,)),
        coarse_sem=pltpu.SemaphoreType.DMA((2,)),
        d_coarse_sem=pltpu.SemaphoreType.DMA((2,)),
        out_sem=pltpu.SemaphoreType.DMA((7,)),
    )
    for name, rows in (("a", a_rows), ("b", b_rows)):
        scratch |= {
            name + "_src": pltpu.VMEM((ng, rows, W), BF16),
            name + "_in": pltpu.VMEM((ng, rows, W), BF16),
            name + "_z": pltpu.VMEM((nz, rows, W), BF16),
            name + "_all": pltpu.VMEM((ng, rows, W), BF16),
            name + "_sum": pltpu.VMEM((rows, W), F32),
            name + "_rs_sem": pltpu.SemaphoreType.DMA((2,)),
            name + "_z_sem": pltpu.SemaphoreType.DMA((2,)),
            name + "_ag_sem": pltpu.SemaphoreType.DMA((2,)),
        }
    names = tuple(name + "_in" for name in INPUTS) + ("live",)
    names += tuple(name + "_out" for name in OUTPUTS) + tuple(scratch)
    smem = pl.BlockSpec(memory_space=pltpu.SMEM)
    hbm = pl.BlockSpec(memory_space=pltpu.HBM)
    outs = pl.pallas_call(
        functools.partial(kernel, dims, names),
        out_shape=shapes,
        in_specs=[hbm] * len(INPUTS) + [smem],
        out_specs=(hbm,) * 5,
        scratch_shapes=list(scratch.values()),
        compiler_params=pltpu.CompilerParams(
            collective_id=0, has_side_effects=True, vmem_limit_bytes=61440 * 1024
        ),
        cost_estimate=pl.CostEstimate(
            flops=2 * edges * W * (2 * ext + 4 * cells + 4 * W),
            bytes_accessed=2 * W * (2 * edges + 4 * cells),
            transcendentals=edges * W,
        ),
        name="mesh_step",
    )(*[operands[name] for name in INPUTS], edge_live)
    cuts = (1, 1, 4, 2, 1)
    outs = pl.pallas_call(
        functools.partial(settle, cuts),
        out_shape=shapes,
        in_specs=[hbm] * 5,
        out_specs=(hbm,) * 5,
        scratch_shapes=[pltpu.VMEM(s.shape, s.dtype) for s in shapes]
        + [pltpu.SemaphoreType.DMA((2, sum(cuts)))],
        compiler_params=pltpu.CompilerParams(vmem_limit_bytes=60 * 1024 * 1024),
        name="settle",
    )(*outs)
    node_out, d_nodes, d_edges, grads, bias_grads = outs
    return node_out, d_nodes, d_edges, grads.reshape(9, W, W), bias_grads


def solution(mesh, cells=1024, edges=4096, tile=1024):
    both = ("gx", "gy")
    dims = (mesh.shape["gx"], mesh.shape["gy"], cells, edges, tile)
    in_specs = (
        P(both, None),
        P(both, None),
        P(both),
        P(both),
        P(both, None, None),
        P(both),
        P(both),
        P(both, None),
        P(),
        P(),
        P(),
        P(),
    )
    out_specs = (P(both, None), P(both, None), P(both, None), P(), P())
    return jax.shard_map(
        functools.partial(body, dims),
        mesh=mesh,
        in_specs=in_specs,
        out_specs=out_specs,
        check_vma=False,
    )
```

```python
import functools
from types import SimpleNamespace

import jax
import jax.numpy as jnp
from jax import lax
from jax.experimental import pallas as pl
from jax.experimental.pallas import tpu as pltpu
from jax.sharding import PartitionSpec as P

F32, BF16, I32 = jnp.float32, jnp.bfloat16, jnp.int32
W = 128
BLOCK = 256
MESH = pl.DeviceIdType.MESH


def dot(left, right):
    return jnp.dot(left, right, preferred_element_type=F32)


def right_t(left, right):
    return lax.dot_general(left, right, (((1,), (1,)), ((), ())), preferred_element_type=F32)


def sigmoid(value):
    return 0.5 * jnp.tanh(0.5 * value) + 0.5


def slope(value, sigma):
    return sigma * (1.0 + value * (1.0 - sigma))


def lane_row(ref, first, count):
    return jnp.concatenate([ref[pl.ds(first + q, 1), :] for q in range(count)], axis=1)


INPUTS = (
    "nodes", "feat", "snd", "rcv", "slist", "owner", "cot", "w_edge", "w_node", "w_coarse", "bias"
)
ORDER = (
    "slist", "nodes", "owner", "cot", "snd", "rcv", "w_edge", "bias", "feat", "w_node", "w_coarse"
)
OUTPUTS = ("node_out", "d_nodes", "d_edges", "grads", "bias_grads")


def kernel(dims, names, *refs):
    r = SimpleNamespace(**dict(zip(names, refs)))
    nx, ny, cells, edges, tile = dims
    nz = nx // 2
    ng = 2 * ny
    ext = cells + 4 * W
    owned = cells // ny
    tiles = edges // tile
    i, j = lax.axis_index("gx"), lax.axis_index("gy")
    core, z = lax.rem(i, 2), lax.div(i, 2)
    g = core * ny + j
    up, down = lax.rem(i + nx - 1, nx), lax.rem(i + 1, nx)
    left, right = lax.rem(j + ny - 1, ny), lax.rem(j + 1, ny)
    across = lax.rem(i + nx - 1 + 2 * core, nx)

    barrier = pltpu.get_barrier_semaphore()

    def greet(gx, gy):
        pl.semaphore_signal(barrier, inc=1, device_id=(gx, gy), device_id_type=MESH)

    def each(count, me, action):
        some = 5 if count > 5 else 1
        first = 1 + (count - 1) % some
        for d in range(1, first):
            action(me ^ (count - d))

        def step(k, c):
            for u in range(some):
                action(me ^ (count - first - k * some - u))
            return c

        lax.fori_loop(0, (count - first) // some, step, 0)

    shift = ny.bit_length() - 1

    def layer_place(t):
        return 2 * z + lax.shift_right_logical(t, shift), t & (ny - 1)

    greet(across, j)
    loads = {
        name: pltpu.make_async_copy(
            getattr(r, name + "_in"), getattr(r, name), r.load_sem.at[k]
        )
        for k, name in enumerate(ORDER)
    }
    for name in ORDER:
        loads[name].start()
    each(ng, g, lambda t: greet(*layer_place(t)))
    each(nz, z, lambda t: greet(2 * t + core, j))

    def exchange(count, me, place):
        def copy(src, dst, sems, target):
            return pltpu.make_async_remote_copy(
                src_ref=src,
                dst_ref=dst,
                send_sem=sems.at[0],
                recv_sem=sems.at[1],
                device_id=place(target),
                device_id_type=MESH,
            )

        def scatter(src, dst, sems):
            dst[me] = src[me]
            each(count, me, lambda t: copy(src.at[t], dst.at[me], sems, t).start())

        def gather(buf, sems):
            each(count, me, lambda t: copy(buf.at[me], buf.at[me], sems, t).start())

        def every(buf, sems):
            others = buf.at[pl.ds(0, count - 1)]
            return copy(others, others, sems, me ^ 1)

        def arrive(buf, sems):
            every(buf, sems).wait_recv()

        def sent(buf, sems):
            every(buf, sems).wait_send()

        return SimpleNamespace(scatter=scatter, gather=gather, arrive=arrive, sent=sent)

    row = exchange(ny, j, lambda t: (i, t))
    column = exchange(nz, z, lambda t: (2 * t + core, j))
    layer = exchange(ng, g, layer_place)

    def slots_sum(ref):
        return jnp.sum(ref[...].astype(F32), axis=0)

    def reduce_stages(src, into, zbuf, everything, sums, sems):
        rs_sem, z_sem, ag_sem = sems

        def start():
            layer.scatter(src, into, rs_sem)

        def to_column():
            layer.arrive(into, rs_sem)
            zbuf[z] = slots_sum(into).astype(BF16)
            column.gather(zbuf, z_sem)

        def to_layer():
            column.arrive(zbuf, z_sem)
            sums[...] = slots_sum(zbuf)
            everything[g] = sums[...].astype(BF16)
            layer.gather(everything, ag_sem)

        def finish():
            layer.arrive(everything, ag_sem)

        def sent():
            layer.sent(into, rs_sem)
            column.sent(zbuf, z_sem)
            layer.sent(everything, ag_sem)

        return SimpleNamespace(
            start=start, to_column=to_column, to_layer=to_layer, finish=finish, sent=sent
        )

    a_stage = reduce_stages(
        r.a_src, r.a_in, r.a_z, r.a_all, r.a_sum, (r.a_rs_sem, r.a_z_sem, r.a_ag_sem)
    )
    b_stage = reduce_stages(
        r.b_src, r.b_in, r.b_z, r.b_all, r.b_sum, (r.b_rs_sem, r.b_z_sem, r.b_ag_sem)
    )

    def halo_copies(src, dst, sems):
        targets = ((up, j), (down, j), (i, left), (i, right))
        return [
            pltpu.make_async_remote_copy(
                src_ref=src.at[k],
                dst_ref=dst.at[k ^ 1],
                send_sem=sems.at[0, k],
                recv_sem=sems.at[1, k ^ 1],
                device_id=targets[k],
                device_id_type=MESH,
            )
            for k in range(4)
        ]

    present = (i > 0, i < nx - 1, j > 0, j < ny - 1)

    half_e, half_c = ext // 2, cells // 2

    def folded(line, half):
        return jnp.where(line >= half, line - half, line)

    def pick_half(high, both):
        return jnp.where(high, both[W:, :], both[:W, :])

    def halves(line, half, value):
        high = jnp.where(line >= half, 1.0, 0.0)
        low = jnp.broadcast_to((1.0 - high).astype(BF16), value.shape)
        high = jnp.broadcast_to(high.astype(BF16), value.shape)
        return jnp.concatenate([value * low, value * high], axis=0)

    def unfold(pairs):
        return jnp.concatenate([pairs[:, :W], pairs[:, W:]], axis=0)

    def fold_t(table, half):
        return jnp.concatenate([table[:, :half], table[:, half:]], axis=0)

    def to_coarse(value):
        low = jnp.where(r.own_high[...] > 0.5, 0.0, value)
        pairs = jnp.concatenate([low, value - low], axis=1).astype(BF16)
        return unfold(dot(r.own_t[...], pairs)).astype(BF16).reshape(ny, owned, W)

    def from_coarse(table):
        flat = table.reshape(cells, W)
        pairs = jnp.concatenate([flat[:half_c], flat[half_c:]], axis=1)
        both = dot(r.own_n[...], pairs)
        return jnp.where(r.own_high[...] > 0.5, both[:, W:], both[:, :W])

    def hot(line, count):
        parts = []
        for a in range(count // BLOCK):
            inside = jnp.where(lax.shift_right_arithmetic(line, 8) == a, line & 255, -1)
            inside = inside.astype(F32).astype(BF16)
            same = r.iota[:, : line.shape[1]] == inside
            parts.append(jnp.where(same, jnp.ones((), BF16), jnp.zeros((), BF16)))
        return jnp.concatenate(parts, axis=0)

    eye = (
        lax.broadcasted_iota(I32, (W, W), 0) == lax.broadcasted_iota(I32, (W, W), 1)
    ).astype(F32).astype(BF16)

    def turned(block):
        return right_t(eye, block).astype(BF16)

    r.iota[...] = lax.broadcasted_iota(I32, r.iota.shape, 0).astype(F32).astype(BF16)
    loads["slist"].wait()
    r.hot_list[...] = hot(lane_row(r.slist, 0, 4), cells)
    loads["nodes"].wait()
    r.ext_t[:, :cells] = turned(r.nodes[...])
    picked = dot(r.ext_t[:, :cells], r.hot_list[...]).astype(BF16)
    for k in range(4):
        r.pick[k] = picked[:, k * W : (k + 1) * W]
    loads["owner"].wait()
    r.own_t[...] = hot(folded(lane_row(r.owner, 0, cells // W), half_c), half_c)
    for q in range(cells // W):
        at = jnp.broadcast_to(r.owner[q : q + 1, :].astype(F32), (W, W)).T
        r.own_at[q * W : (q + 1) * W, :] = at
    r.own_high[...] = jnp.where(r.own_at[...] >= float(half_c), 1.0, 0.0)
    loads["cot"].wait()
    r.cot_src[...] = to_coarse(r.cot[...].astype(F32))

    pl.semaphore_wait(barrier, ng + nz - 1)
    halo_out = halo_copies(r.pick, r.halo, r.halo_sem)
    for copy in halo_out:
        copy.start()
    row.scatter(r.cot_src, r.cot_got, r.cot_sem)

    loads["snd"].wait()
    loads["rcv"].wait()
    per = tile // W
    alive = r.live[0]

    def sender_row(t):
        return lane_row(r.snd, t * per, per)

    def receiver_row(t):
        place = t * tile + lax.broadcasted_iota(I32, (1, tile), 1)
        return jnp.where(place < alive, lane_row(r.rcv, t * per, per), -1)

    def high_s(t):
        return jnp.broadcast_to(sender_row(t), (W, tile)) >= half_e

    def high_r(t):
        return jnp.broadcast_to(receiver_row(t), (W, tile)) >= half_c

    def mark(t, c):
        r.marks[t, :half_e, :] = hot(folded(sender_row(t), half_e), half_e)
        r.marks[t, half_e:, :] = hot(folded(receiver_row(t), half_c), half_c)
        return c

    mark(0, 0)

    loads["w_edge"].wait()
    loads["bias"].wait()
    ws_t, wr_t, we_t = [turned(r.w_edge[k]) for k in range(3)]
    b_col = jnp.broadcast_to(r.bias[0:1, :], (W, W)).T
    r.table_t[:, half_e:] = fold_t(dot(wr_t, r.ext_t[:, :cells]), half_c).astype(BF16)
    loads["feat"].wait()
    loads["w_node"].wait()
    loads["w_coarse"].wait()
    for copy in halo_out:
        copy.wait_recv()
    for k in range(4):
        r.ext_t[:, cells + k * W : cells + (k + 1) * W] = jnp.where(
            present[k], r.halo[k].astype(F32), 0.0
        ).astype(BF16)
    r.table_t[:, :half_e] = fold_t(
        dot(ws_t, r.ext_t[...]) + jnp.concatenate([b_col] * (ext // W), axis=1), half_e
    ).astype(BF16)

    r.h_acc[...] = jnp.zeros_like(r.h_acc)

    def edge_rows(t):
        return pl.ds(t * tile if isinstance(t, int) else pl.multiple_of(t * tile, tile), tile)

    def forward(t, c):
        above = high_r(t)
        pre = (
            pick_half(high_s(t), dot(r.table_t[:, :half_e], r.marks[t, :half_e, :]))
            + pick_half(above, dot(r.table_t[:, half_e:], r.marks[t, half_e:, :]))
            + right_t(we_t, r.feat[edge_rows(t), :])
        )
        sigma = sigmoid(pre)
        r.slopes[t] = slope(pre, sigma)
        r.h_acc[...] += right_t(r.marks[t, half_e:, :], halves(receiver_row(t), half_c, (pre * sigma).astype(BF16)))
        return c

    for t in range(tiles):
        if t + 1 < tiles:
            mark(t + 1, 0)
        forward(t, 0)

    r.hb[...] = unfold(r.h_acc[...]).astype(BF16)
    r.agg[...] = dot(r.hb[...], r.w_edge[3]).astype(BF16)
    pre_node = dot(r.nodes[...], r.w_node[0]) + dot(r.agg[...], r.w_node[1]) + r.bias[1:2, :]
    sigma = sigmoid(pre_node)
    r.node_slope[...] = slope(pre_node, sigma)
    r.hid[...] = (pre_node * sigma).astype(BF16)
    r.fine[...] = r.nodes[...].astype(F32) + dot(r.hid[...], r.w_node[2])
    r.fine_src[...] = to_coarse(r.fine[...])
    row.scatter(r.fine_src, r.fine_got, r.fine_sem)

    lanes = lax.broadcasted_iota(I32, (cells, W), 1).astype(F32)
    at = r.own_at[...] - float(half_c) * r.own_high[...]
    r.own_n[...] = jnp.concatenate(
        [jnp.where(at == lanes + float(k * W), 1.0, 0.0).astype(BF16) for k in range(half_c // W)],
        axis=1,
    )
    agg_t, hid_t, hb_t = turned(r.agg[...]), turned(r.hid[...]), turned(r.hb[...])

    row.arrive(r.cot_got, r.cot_sem)
    d_coarse = slots_sum(r.cot_got).astype(BF16)
    d_hidden = right_t(d_coarse, r.w_coarse[1])
    row.arrive(r.fine_got, r.fine_sem)
    coarse_bf = (0.0625 * slots_sum(r.fine_got)).astype(BF16)
    pre_coarse = dot(coarse_bf, r.w_coarse[0]) + r.bias[2:3, :]
    sigma = sigmoid(pre_coarse)
    coarse_hid = (pre_coarse * sigma).astype(BF16)
    d_pre_c = d_hidden * slope(pre_coarse, sigma)
    d_pre_c_bf = d_pre_c.astype(BF16)
    r.d_coarse_all[j] = right_t(d_pre_c_bf, r.w_coarse[0]).astype(BF16)
    row.gather(r.d_coarse_all, r.d_coarse_sem)
    r.coarse_all[j] = dot(coarse_hid, r.w_coarse[1]).astype(BF16)
    row.gather(r.coarse_all, r.coarse_sem)
    g_v1 = dot(turned(coarse_bf), d_pre_c_bf)
    g_v2 = dot(turned(coarse_hid), d_coarse)
    b_own = r.b_src.shape[1]
    a_own = 6 * W // ng
    share = 3 * W // ng
    r.bias_rows[...] = jnp.zeros_like(r.bias_rows)
    r.bias_rows[share + 2 : share + 3, :] = jnp.sum(d_pre_c, axis=0, keepdims=True)
    row.arrive(r.d_coarse_all, r.d_coarse_sem)

    d_fine = r.cot[...].astype(F32) + 0.0625 * from_coarse(r.d_coarse_all[...])
    d_fine_bf = d_fine.astype(BF16)
    d_pre_n = right_t(d_fine_bf, r.w_node[2]) * r.node_slope[...]
    d_pre_n_bf = d_pre_n.astype(BF16)
    r.bias_rows[share + 1 : share + 2, :] = jnp.sum(d_pre_n, axis=0, keepdims=True)
    r.d_part[...] = d_fine
    r.d_pre_n[...] = d_pre_n_bf
    d_agg = right_t(d_pre_n_bf, r.w_node[1]).astype(BF16)
    r.table_t[:, half_e:] = fold_t(right_t(r.w_edge[3], d_agg), half_c).astype(BF16)
    early = jnp.concatenate(
        [
            dot(hb_t, d_agg),
            dot(r.ext_t[:, :cells], d_pre_n_bf),
            dot(agg_t, d_pre_n_bf),
            dot(hid_t, d_fine_bf),
            g_v1,
            g_v2,
        ],
        axis=0,
    ).reshape(ng, a_own, W)
    spare = r.a_src.shape[1] - a_own
    if spare:
        early = jnp.concatenate([early, jnp.zeros((ng, spare, W), F32)], axis=1)
    r.a_src[...] = early.astype(BF16)
    a_stage.start()

    r.s_acc[...] = jnp.zeros_like(r.s_acc)
    r.r_acc[...] = jnp.zeros_like(r.r_acc)
    r.we_acc[...] = jnp.zeros_like(r.we_acc)

    def backward(t, c):
        above = high_r(t)
        got = pick_half(above, dot(r.table_t[:, half_e:], r.marks[t, half_e:, :]))
        d_pre = got * r.slopes[t]
        d_pre_bf = d_pre.astype(BF16)
        r.d_pre[t] = d_pre_bf
        r.s_acc[...] += right_t(r.marks[t, :half_e, :], halves(sender_row(t), half_e, d_pre_bf))
        r.r_acc[...] += right_t(r.marks[t, half_e:, :], halves(receiver_row(t), half_c, d_pre_bf))
        r.we_acc[...] += dot(d_pre_bf, r.feat[edge_rows(t), :])
        return c

    def edge_out(t, c):
        r.d_edges[edge_rows(t), :] = dot(r.w_edge[2], r.d_pre[t]).T.astype(BF16)
        return c

    leaving = []

    def leave(k, src, dst):
        leaving.append(pltpu.make_async_copy(src, dst, r.out_sem.at[k]))
        leaving[-1].start()

    half = tiles // 2
    for t in range(tiles):
        backward(t, 0)
    a_stage.to_column()

    s_bf = unfold(r.s_acc[...]).astype(BF16)
    r_sum = unfold(r.r_acc[...])
    r_bf = r_sum.astype(BF16)
    r.back_src[...] = right_t(s_bf[cells:, :], r.w_edge[0]).astype(BF16).reshape(4, W, W)
    back_out = halo_copies(r.back_src, r.back_got, r.back_sem)
    for copy in back_out:
        copy.start()
    r.bias_rows[share : share + 1, :] = jnp.sum(r_sum, axis=0, keepdims=True)
    r.b_flat[: 3 * W, :] = jnp.concatenate(
        [dot(r.ext_t[...], s_bf), dot(r.ext_t[:, :cells], r_bf), r.we_acc[...].T], axis=0
    )
    r.b_flat[3 * W :, :] = jnp.zeros((b_own, W), F32)
    inner = lax.broadcasted_iota(I32, (b_own, W), 0) < share
    for k in range(ng):
        part = r.b_flat[k * share : k * share + b_own, :]
        r.b_src[k] = jnp.where(inner, part, r.bias_rows[...]).astype(BF16)
    b_stage.start()
    r.d_part[...] = (
        r.d_part[...]
        + right_t(r.d_pre_n[...], r.w_node[0])
        + right_t(s_bf[:cells, :], r.w_edge[0])
        + right_t(r_bf, r.w_edge[1])
    )
    for copy in back_out:
        copy.wait_recv()
    returned = jnp.concatenate(
        [jnp.where(present[k], r.back_got[k].astype(F32), 0.0) for k in range(4)], axis=0
    ).astype(BF16)
    r.d_nodes[...] = (r.d_part[...] + dot(r.hot_list[...], returned)).astype(BF16)
    leave(0, r.d_nodes, r.d_nodes_out)
    b_stage.to_column()
    a_stage.to_layer()
    lax.fori_loop(0, half, edge_out, 0)
    first, second = pl.ds(0, half * tile), pl.ds(half * tile, (tiles - half) * tile)
    leave(1, r.d_edges.at[first], r.d_edges_out.at[first])
    row.arrive(r.coarse_all, r.coarse_sem)
    r.node_out[...] = (r.fine[...] + from_coarse(r.coarse_all[...])).astype(BF16)
    leave(2, r.node_out, r.node_out_out)
    b_stage.to_layer()
    lax.fori_loop(half, tiles, edge_out, 0)
    leave(3, r.d_edges.at[second], r.d_edges_out.at[second])
    r.bias_grads[...] = r.b_sum[share : share + 3, :]
    leave(4, r.bias_grads, r.bias_grads_out)
    a_stage.finish()
    r.grads[3 * W :, :] = r.a_all[...].astype(F32)[:, :a_own, :].reshape(6 * W, W)
    late, soon = pl.ds(0, 3 * W), pl.ds(3 * W, 6 * W)
    leave(5, r.grads.at[soon], r.grads_out.at[soon])
    row.sent(r.cot_got, r.cot_sem)
    row.sent(r.fine_got, r.fine_sem)
    row.sent(r.coarse_all, r.coarse_sem)
    row.sent(r.d_coarse_all, r.d_coarse_sem)
    for copy in halo_out + back_out:
        copy.wait_send()
    a_stage.sent()
    layer.sent(r.b_in, r.b_rs_sem)
    column.sent(r.b_z, r.b_z_sem)
    b_stage.finish()
    for k in range(ng):
        r.grads[k * share : (k + 1) * share, :] = r.b_all[k].astype(F32)[:share, :]
    leave(6, r.grads.at[late], r.grads_out.at[late])
    layer.sent(r.b_all, r.b_ag_sem)
    for copy in leaving:
        copy.wait()


def settle(cuts, *refs):
    count = len(cuts)
    held, sems = refs[2 * count : 3 * count], refs[3 * count]
    pieces = []
    for k, parts in enumerate(cuts):
        rows = refs[k].shape[0] // parts
        pieces += [(k, pl.ds(p * rows, rows)) for p in range(parts)]
    gets = [
        pltpu.make_async_copy(refs[k].at[here], held[k].at[here], sems.at[0, n])
        for n, (k, here) in enumerate(pieces)
    ]
    puts = [
        pltpu.make_async_copy(held[k].at[here], refs[count + k].at[here], sems.at[1, n])
        for n, (k, here) in enumerate(pieces)
    ]
    for get in gets:
        get.start()
    for get, put in zip(gets, puts):
        get.wait()
        put.start()
    for put in puts:
        put.wait()


def body(
    dims,
    nodes,
    edge_feat,
    senders,
    receivers,
    send_lists,
    owner,
    edge_live,
    cotangent,
    w_edge,
    w_node,
    w_coarse,
    biases,
):
    nx, ny, cells, edges, tile = dims
    nz = nx // 2
    ng = 2 * ny
    ext = cells + 4 * W
    owned = cells // ny
    a_rows = -(-(6 * W // ng) // 16) * 16
    b_rows = -(-(3 * W // ng + 3) // 16) * 16
    operands = dict(
        nodes=nodes,
        feat=edge_feat,
        snd=senders.reshape(edges // W, W),
        rcv=receivers.reshape(edges // W, W),
        slist=send_lists.reshape(4, W),
        owner=owner.reshape(cells // W, W),
        cot=cotangent,
        w_edge=w_edge,
        w_node=w_node,
        w_coarse=w_coarse,
        bias=biases,
    )
    shapes = (
        jax.ShapeDtypeStruct((cells, W), BF16),
        jax.ShapeDtypeStruct((cells, W), BF16),
        jax.ShapeDtypeStruct((edges, W), BF16),
        jax.ShapeDtypeStruct((9 * W, W), F32),
        jax.ShapeDtypeStruct((3, W), F32),
    )
    scratch = {name: pltpu.VMEM(operands[name].shape, operands[name].dtype) for name in INPUTS}
    scratch |= {name: pltpu.VMEM(s.shape, s.dtype) for name, s in zip(OUTPUTS, shapes)}
    scratch |= dict(
        iota=pltpu.VMEM((BLOCK, max(cells, tile)), BF16),
        ext_t=pltpu.VMEM((W, ext), BF16),
        table_t=pltpu.VMEM((2 * W, (ext + cells) // 2), BF16),
        marks=pltpu.VMEM((edges // tile, (ext + cells) // 2, tile), BF16),
        hot_list=pltpu.VMEM((cells, 4 * W), BF16),
        own_t=pltpu.VMEM((cells // 2, cells), BF16),
        own_n=pltpu.VMEM((cells, cells // 2), BF16),
        own_at=pltpu.VMEM((cells, W), F32),
        own_high=pltpu.VMEM((cells, W), F32),
        pick=pltpu.VMEM((4, W, W), BF16),
        halo=pltpu.VMEM((4, W, W), BF16),
        slopes=pltpu.VMEM((edges // tile, W, tile), F32),
        d_pre=pltpu.VMEM((edges // tile, W, tile), BF16),
        h_acc=pltpu.VMEM((cells // 2, 2 * W), F32),
        s_acc=pltpu.VMEM((ext // 2, 2 * W), F32),
        r_acc=pltpu.VMEM((cells // 2, 2 * W), F32),
        we_acc=pltpu.VMEM((W, W), F32),
        fine=pltpu.VMEM((cells, W), F32),
        node_slope=pltpu.VMEM((cells, W), F32),
        d_part=pltpu.VMEM((cells, W), F32),
        hb=pltpu.VMEM((cells, W), BF16),
        agg=pltpu.VMEM((cells, W), BF16),
        hid=pltpu.VMEM((cells, W), BF16),
        cot_src=pltpu.VMEM((ny, owned, W), BF16),
        cot_got=pltpu.VMEM((ny, owned, W), BF16),
        fine_src=pltpu.VMEM((ny, owned, W), BF16),
        fine_got=pltpu.VMEM((ny, owned, W), BF16),
        coarse_all=pltpu.VMEM((ny, owned, W), BF16),
        d_coarse_all=pltpu.VMEM((ny, owned, W), BF16),
        d_pre_n=pltpu.VMEM((cells, W), BF16),
        back_src=pltpu.VMEM((4, W, W), BF16),
        back_got=pltpu.VMEM((4, W, W), BF16),
        bias_rows=pltpu.VMEM((b_rows, W), F32),
        b_flat=pltpu.VMEM((3 * W + b_rows, W), F32),
        load_sem=pltpu.SemaphoreType.DMA((len(INPUTS),)),
        halo_sem=pltpu.SemaphoreType.DMA((2, 4)),
        back_sem=pltpu.SemaphoreType.DMA((2, 4)),
        cot_sem=pltpu.SemaphoreType.DMA((2,)),
        fine_sem=pltpu.SemaphoreType.DMA((2,)),
        coarse_sem=pltpu.SemaphoreType.DMA((2,)),
        d_coarse_sem=pltpu.SemaphoreType.DMA((2,)),
        out_sem=pltpu.SemaphoreType.DMA((7,)),
    )
    for name, rows in (("a", a_rows), ("b", b_rows)):
        scratch |= {
            name + "_src": pltpu.VMEM((ng, rows, W), BF16),
            name + "_in": pltpu.VMEM((ng, rows, W), BF16),
            name + "_z": pltpu.VMEM((nz, rows, W), BF16),
            name + "_all": pltpu.VMEM((ng, rows, W), BF16),
            name + "_sum": pltpu.VMEM((rows, W), F32),
            name + "_rs_sem": pltpu.SemaphoreType.DMA((2,)),
            name + "_z_sem": pltpu.SemaphoreType.DMA((2,)),
            name + "_ag_sem": pltpu.SemaphoreType.DMA((2,)),
        }
    names = tuple(name + "_in" for name in INPUTS) + ("live",)
    names += tuple(name + "_out" for name in OUTPUTS) + tuple(scratch)
    smem = pl.BlockSpec(memory_space=pltpu.SMEM)
    hbm = pl.BlockSpec(memory_space=pltpu.HBM)
    outs = pl.pallas_call(
        functools.partial(kernel, dims, names),
        out_shape=shapes,
        in_specs=[hbm] * len(INPUTS) + [smem],
        out_specs=(hbm,) * 5,
        scratch_shapes=list(scratch.values()),
        compiler_params=pltpu.CompilerParams(
            collective_id=0, has_side_effects=True, vmem_limit_bytes=61440 * 1024
        ),
        cost_estimate=pl.CostEstimate(
            flops=2 * edges * W * (2 * ext + 4 * cells + 4 * W),
            bytes_accessed=2 * W * (2 * edges + 4 * cells),
            transcendentals=edges * W,
        ),
        name="mesh_step",
    )(*[operands[name] for name in INPUTS], edge_live)
    cuts = (1, 1, 4, 2, 1)
    outs = pl.pallas_call(
        functools.partial(settle, cuts),
        out_shape=shapes,
        in_specs=[hbm] * 5,
        out_specs=(hbm,) * 5,
        scratch_shapes=[pltpu.VMEM(s.shape, s.dtype) for s in shapes]
        + [pltpu.SemaphoreType.DMA((2, sum(cuts)))],
        compiler_params=pltpu.CompilerParams(vmem_limit_bytes=60 * 1024 * 1024),
        name="settle",
    )(*outs)
    node_out, d_nodes, d_edges, grads, bias_grads = outs
    return node_out, d_nodes, d_edges, grads.reshape(9, W, W), bias_grads


def solution(mesh, cells=1024, edges=4096, tile=1024):
    both = ("gx", "gy")
    dims = (mesh.shape["gx"], mesh.shape["gy"], cells, edges, tile)
    in_specs = (
        P(both, None),
        P(both, None),
        P(both),
        P(both),
        P(both, None, None),
        P(both),
        P(both),
        P(both, None),
        P(),
        P(),
        P(),
        P(),
    )
    out_specs = (P(both, None), P(both, None), P(both, None), P(), P())
    return jax.shard_map(
        functools.partial(body, dims),
        mesh=mesh,
        in_specs=in_specs,
        out_specs=out_specs,
        check_vma=False,
    )
```

```python
import functools
from types import SimpleNamespace

import jax
import jax.numpy as jnp
from jax import lax
from jax.experimental import pallas as pl
from jax.experimental.pallas import tpu as pltpu
from jax.sharding import PartitionSpec as P

F32, BF16, I32 = jnp.float32, jnp.bfloat16, jnp.int32
W = 128
BLOCK = 256
MESH = pl.DeviceIdType.MESH


def dot(left, right):
    return jnp.dot(left, right, preferred_element_type=F32)


def right_t(left, right):
    return lax.dot_general(left, right, (((1,), (1,)), ((), ())), preferred_element_type=F32)


def sigmoid(value):
    return 0.5 * jnp.tanh(0.5 * value) + 0.5


def slope(value, sigma):
    return sigma * (1.0 + value * (1.0 - sigma))


def lane_row(ref, first, count):
    return jnp.concatenate([ref[pl.ds(first + q, 1), :] for q in range(count)], axis=1)


INPUTS = (
    "nodes", "feat", "snd", "rcv", "slist", "owner", "cot", "w_edge", "w_node", "w_coarse", "bias"
)
ORDER = (
    "slist", "nodes", "owner", "cot", "snd", "rcv", "w_edge", "bias", "feat", "w_node", "w_coarse"
)
OUTPUTS = ("node_out", "d_nodes", "d_edges", "grads", "bias_grads")


def kernel(dims, names, *refs):
    r = SimpleNamespace(**dict(zip(names, refs)))
    nx, ny, cells, edges, tile = dims
    nz = nx // 2
    ng = 2 * ny
    ext = cells + 4 * W
    owned = cells // ny
    tiles = edges // tile
    i, j = lax.axis_index("gx"), lax.axis_index("gy")
    core, z = lax.rem(i, 2), lax.div(i, 2)
    g = core * ny + j
    up, down = lax.rem(i + nx - 1, nx), lax.rem(i + 1, nx)
    left, right = lax.rem(j + ny - 1, ny), lax.rem(j + 1, ny)
    across = lax.rem(i + nx - 1 + 2 * core, nx)

    barrier = pltpu.get_barrier_semaphore()

    def greet(gx, gy):
        pl.semaphore_signal(barrier, inc=1, device_id=(gx, gy), device_id_type=MESH)

    def each(count, me, action):
        some = 5 if count > 5 else 1
        first = 1 + (count - 1) % some
        for d in range(1, first):
            action(me ^ (count - d))

        def step(k, c):
            for u in range(some):
                action(me ^ (count - first - k * some - u))
            return c

        lax.fori_loop(0, (count - first) // some, step, 0)

    shift = ny.bit_length() - 1

    def layer_place(t):
        return 2 * z + lax.shift_right_logical(t, shift), t & (ny - 1)

    greet(across, j)
    loads = {
        name: pltpu.make_async_copy(
            getattr(r, name + "_in"), getattr(r, name), r.load_sem.at[k]
        )
        for k, name in enumerate(ORDER)
    }
    for name in ORDER:
        loads[name].start()
    each(ng, g, lambda t: greet(*layer_place(t)))
    each(nz, z, lambda t: greet(2 * t + core, j))

    def exchange(count, me, place):
        def copy(src, dst, sems, target):
            return pltpu.make_async_remote_copy(
                src_ref=src,
                dst_ref=dst,
                send_sem=sems.at[0],
                recv_sem=sems.at[1],
                device_id=place(target),
                device_id_type=MESH,
            )

        def scatter(src, dst, sems):
            dst[me] = src[me]
            each(count, me, lambda t: copy(src.at[t], dst.at[me], sems, t).start())

        def gather(buf, sems):
            each(count, me, lambda t: copy(buf.at[me], buf.at[me], sems, t).start())

        def every(buf, sems):
            others = buf.at[pl.ds(0, count - 1)]
            return copy(others, others, sems, me ^ 1)

        def arrive(buf, sems):
            every(buf, sems).wait_recv()

        def sent(buf, sems):
            every(buf, sems).wait_send()

        return SimpleNamespace(scatter=scatter, gather=gather, arrive=arrive, sent=sent)

    row = exchange(ny, j, lambda t: (i, t))
    column = exchange(nz, z, lambda t: (2 * t + core, j))
    layer = exchange(ng, g, layer_place)

    def slots_sum(ref):
        return jnp.sum(ref[...].astype(F32), axis=0)

    def reduce_stages(src, into, zbuf, everything, sums, sems):
        rs_sem, z_sem, ag_sem = sems

        def start():
            layer.scatter(src, into, rs_sem)

        def to_column():
            layer.arrive(into, rs_sem)
            zbuf[z] = slots_sum(into).astype(BF16)
            column.gather(zbuf, z_sem)

        def to_layer():
            column.arrive(zbuf, z_sem)
            sums[...] = slots_sum(zbuf)
            everything[g] = sums[...].astype(BF16)
            layer.gather(everything, ag_sem)

        def finish():
            layer.arrive(everything, ag_sem)

        def sent():
            layer.sent(into, rs_sem)
            column.sent(zbuf, z_sem)
            layer.sent(everything, ag_sem)

        return SimpleNamespace(
            start=start, to_column=to_column, to_layer=to_layer, finish=finish, sent=sent
        )

    a_stage = reduce_stages(
        r.a_src, r.a_in, r.a_z, r.a_all, r.a_sum, (r.a_rs_sem, r.a_z_sem, r.a_ag_sem)
    )
    b_stage = reduce_stages(
        r.b_src, r.b_in, r.b_z, r.b_all, r.b_sum, (r.b_rs_sem, r.b_z_sem, r.b_ag_sem)
    )

    def halo_copies(src, dst, sems):
        targets = ((up, j), (down, j), (i, left), (i, right))
        return [
            pltpu.make_async_remote_copy(
                src_ref=src.at[k],
                dst_ref=dst.at[k ^ 1],
                send_sem=sems.at[0, k],
                recv_sem=sems.at[1, k ^ 1],
                device_id=targets[k],
                device_id_type=MESH,
            )
            for k in range(4)
        ]

    present = (i > 0, i < nx - 1, j > 0, j < ny - 1)

    half_e, half_c = ext // 2, cells // 2

    def folded(line, half):
        return jnp.where(line >= half, line - half, line)

    def pick_half(high, both):
        return jnp.where(high, both[W:, :], both[:W, :])

    def halves(line, half, value):
        high = jnp.where(line >= half, 1.0, 0.0)
        low = jnp.broadcast_to((1.0 - high).astype(BF16), value.shape)
        high = jnp.broadcast_to(high.astype(BF16), value.shape)
        return jnp.concatenate([value * low, value * high], axis=0)

    def unfold(pairs):
        return jnp.concatenate([pairs[:, :W], pairs[:, W:]], axis=0)

    def fold_t(table, half):
        return jnp.concatenate([table[:, :half], table[:, half:]], axis=0)

    def to_coarse(value):
        high = r.own_high[...]
        pairs = jnp.concatenate(
            [value * (1.0 - high).astype(BF16), value * high.astype(BF16)], axis=1
        )
        return unfold(dot(r.own_t[...], pairs)).astype(BF16).reshape(ny, owned, W)

    def from_coarse(table):
        flat = table.reshape(cells, W)
        pairs = jnp.concatenate([flat[:half_c], flat[half_c:]], axis=1)
        both = dot(r.own_n[...], pairs)
        return jnp.where(r.own_high[...] > 0.5, both[:, W:], both[:, :W])

    def hot(line, count):
        parts = []
        for a in range(count // BLOCK):
            inside = jnp.where(lax.shift_right_arithmetic(line, 8) == a, line & 255, -1)
            inside = inside.astype(F32).astype(BF16)
            same = r.iota[:, : line.shape[1]] == inside
            parts.append(jnp.where(same, jnp.ones((), BF16), jnp.zeros((), BF16)))
        return jnp.concatenate(parts, axis=0)

    eye = (
        lax.broadcasted_iota(I32, (W, W), 0) == lax.broadcasted_iota(I32, (W, W), 1)
    ).astype(F32).astype(BF16)

    def turned(block):
        return right_t(eye, block).astype(BF16)

    r.iota[...] = lax.broadcasted_iota(I32, r.iota.shape, 0).astype(F32).astype(BF16)
    loads["slist"].wait()
    r.hot_list[...] = hot(lane_row(r.slist, 0, 4), cells)
    loads["nodes"].wait()
    r.ext_t[:, :cells] = turned(r.nodes[...])
    picked = dot(r.ext_t[:, :cells], r.hot_list[...]).astype(BF16)
    for k in range(4):
        r.pick[k] = picked[:, k * W : (k + 1) * W]
    loads["owner"].wait()
    r.own_t[...] = hot(folded(lane_row(r.owner, 0, cells // W), half_c), half_c)
    for q in range(cells // W):
        at = jnp.broadcast_to(r.owner[q : q + 1, :].astype(F32), (W, W)).T
        r.own_at[q * W : (q + 1) * W, :] = at
    r.own_high[...] = jnp.where(r.own_at[...] >= float(half_c), 1.0, 0.0)
    loads["cot"].wait()
    r.cot_src[...] = to_coarse(r.cot[...])

    pl.semaphore_wait(barrier, ng + nz - 1)
    halo_out = halo_copies(r.pick, r.halo, r.halo_sem)
    for copy in halo_out:
        copy.start()
    row.scatter(r.cot_src, r.cot_got, r.cot_sem)

    loads["snd"].wait()
    loads["rcv"].wait()
    per = tile // W
    alive = r.live[0]

    def sender_row(t):
        return lane_row(r.snd, t * per, per)

    def receiver_row(t):
        place = t * tile + lax.broadcasted_iota(I32, (1, tile), 1)
        return jnp.where(place < alive, lane_row(r.rcv, t * per, per), -1)

    def high_s(t):
        return jnp.broadcast_to(sender_row(t), (W, tile)) >= half_e

    def high_r(t):
        return jnp.broadcast_to(receiver_row(t), (W, tile)) >= half_c

    def mark(t, c):
        r.marks[t, :half_e, :] = hot(folded(sender_row(t), half_e), half_e)
        r.marks[t, half_e:, :] = hot(folded(receiver_row(t), half_c), half_c)
        return c

    mark(0, 0)

    loads["w_edge"].wait()
    loads["bias"].wait()
    ws_t, wr_t, we_t = [turned(r.w_edge[k]) for k in range(3)]
    b_col = jnp.broadcast_to(r.bias[0:1, :], (W, W)).T
    r.table_t[:, half_e:] = fold_t(dot(wr_t, r.ext_t[:, :cells]), half_c).astype(BF16)
    loads["feat"].wait()
    loads["w_node"].wait()
    loads["w_coarse"].wait()
    for copy in halo_out:
        copy.wait_recv()
    for k in range(4):
        r.ext_t[:, cells + k * W : cells + (k + 1) * W] = jnp.where(
            present[k], r.halo[k].astype(F32), 0.0
        ).astype(BF16)
    r.table_t[:, :half_e] = fold_t(
        dot(ws_t, r.ext_t[...]) + jnp.concatenate([b_col] * (ext // W), axis=1), half_e
    ).astype(BF16)

    r.h_acc[...] = jnp.zeros_like(r.h_acc)

    def edge_rows(t):
        return pl.ds(t * tile if isinstance(t, int) else pl.multiple_of(t * tile, tile), tile)

    def forward(t, c):
        above = high_r(t)
        pre = (
            pick_half(high_s(t), dot(r.table_t[:, :half_e], r.marks[t, :half_e, :]))
            + pick_half(above, dot(r.table_t[:, half_e:], r.marks[t, half_e:, :]))
            + right_t(we_t, r.feat[edge_rows(t), :])
        )
        sigma = sigmoid(pre)
        r.slopes[t] = slope(pre, sigma)
        r.h_acc[...] += right_t(r.marks[t, half_e:, :], halves(receiver_row(t), half_c, (pre * sigma).astype(BF16)))
        return c

    for t in range(tiles):
        if t + 1 < tiles:
            mark(t + 1, 0)
        forward(t, 0)

    r.hb[...] = unfold(r.h_acc[...]).astype(BF16)
    r.agg[...] = dot(r.hb[...], r.w_edge[3]).astype(BF16)
    pre_node = dot(r.nodes[...], r.w_node[0]) + dot(r.agg[...], r.w_node[1]) + r.bias[1:2, :]
    sigma = sigmoid(pre_node)
    r.node_slope[...] = slope(pre_node, sigma)
    r.hid[...] = (pre_node * sigma).astype(BF16)
    r.fine[...] = r.nodes[...].astype(F32) + dot(r.hid[...], r.w_node[2])
    r.fine_src[...] = to_coarse(r.fine[...].astype(BF16))
    row.scatter(r.fine_src, r.fine_got, r.fine_sem)

    lanes = lax.broadcasted_iota(I32, (cells, W), 1).astype(F32)
    at = r.own_at[...] - float(half_c) * r.own_high[...]
    r.own_n[...] = jnp.concatenate(
        [jnp.where(at == lanes + float(k * W), 1.0, 0.0).astype(BF16) for k in range(half_c // W)],
        axis=1,
    )
    agg_t, hid_t, hb_t = turned(r.agg[...]), turned(r.hid[...]), turned(r.hb[...])

    row.arrive(r.cot_got, r.cot_sem)
    d_coarse = slots_sum(r.cot_got).astype(BF16)
    d_hidden = right_t(d_coarse, r.w_coarse[1])
    row.arrive(r.fine_got, r.fine_sem)
    coarse_bf = (0.0625 * slots_sum(r.fine_got)).astype(BF16)
    pre_coarse = dot(coarse_bf, r.w_coarse[0]) + r.bias[2:3, :]
    sigma = sigmoid(pre_coarse)
    coarse_hid = (pre_coarse * sigma).astype(BF16)
    d_pre_c = d_hidden * slope(pre_coarse, sigma)
    d_pre_c_bf = d_pre_c.astype(BF16)
    r.d_coarse_all[j] = right_t(d_pre_c_bf, r.w_coarse[0]).astype(BF16)
    row.gather(r.d_coarse_all, r.d_coarse_sem)
    r.coarse_all[j] = dot(coarse_hid, r.w_coarse[1]).astype(BF16)
    row.gather(r.coarse_all, r.coarse_sem)
    g_v1 = dot(turned(coarse_bf), d_pre_c_bf)
    g_v2 = dot(turned(coarse_hid), d_coarse)
    b_own = r.b_src.shape[1]
    a_own = 6 * W // ng
    share = 3 * W // ng
    r.bias_rows[...] = jnp.zeros_like(r.bias_rows)
    r.bias_rows[share + 2 : share + 3, :] = jnp.sum(d_pre_c, axis=0, keepdims=True)
    row.arrive(r.d_coarse_all, r.d_coarse_sem)

    d_fine = r.cot[...].astype(F32) + 0.0625 * from_coarse(r.d_coarse_all[...])
    d_fine_bf = d_fine.astype(BF16)
    d_pre_n = right_t(d_fine_bf, r.w_node[2]) * r.node_slope[...]
    d_pre_n_bf = d_pre_n.astype(BF16)
    r.bias_rows[share + 1 : share + 2, :] = jnp.sum(d_pre_n, axis=0, keepdims=True)
    r.d_part[...] = d_fine
    r.d_pre_n[...] = d_pre_n_bf
    d_agg = right_t(d_pre_n_bf, r.w_node[1]).astype(BF16)
    r.table_t[:, half_e:] = fold_t(right_t(r.w_edge[3], d_agg), half_c).astype(BF16)
    early = jnp.concatenate(
        [
            dot(hb_t, d_agg),
            dot(r.ext_t[:, :cells], d_pre_n_bf),
            dot(agg_t, d_pre_n_bf),
            dot(hid_t, d_fine_bf),
            g_v1,
            g_v2,
        ],
        axis=0,
    ).reshape(ng, a_own, W)
    spare = r.a_src.shape[1] - a_own
    if spare:
        early = jnp.concatenate([early, jnp.zeros((ng, spare, W), F32)], axis=1)
    r.a_src[...] = early.astype(BF16)
    a_stage.start()

    r.s_acc[...] = jnp.zeros_like(r.s_acc)
    r.r_acc[...] = jnp.zeros_like(r.r_acc)
    r.we_acc[...] = jnp.zeros_like(r.we_acc)

    def backward(t, c):
        above = high_r(t)
        got = pick_half(above, dot(r.table_t[:, half_e:], r.marks[t, half_e:, :]))
        d_pre = got * r.slopes[t]
        d_pre_bf = d_pre.astype(BF16)
        r.d_pre[t] = d_pre_bf
        r.s_acc[...] += right_t(r.marks[t, :half_e, :], halves(sender_row(t), half_e, d_pre_bf))
        r.r_acc[...] += right_t(r.marks[t, half_e:, :], halves(receiver_row(t), half_c, d_pre_bf))
        r.we_acc[...] += dot(d_pre_bf, r.feat[edge_rows(t), :])
        return c

    def edge_out(t, c):
        r.d_edges[edge_rows(t), :] = dot(r.w_edge[2], r.d_pre[t]).T.astype(BF16)
        return c

    leaving = []

    def leave(k, src, dst):
        leaving.append(pltpu.make_async_copy(src, dst, r.out_sem.at[k]))
        leaving[-1].start()

    half = tiles // 2
    for t in range(tiles):
        backward(t, 0)
    a_stage.to_column()

    s_bf = unfold(r.s_acc[...]).astype(BF16)
    r_sum = unfold(r.r_acc[...])
    r_bf = r_sum.astype(BF16)
    r.back_src[...] = right_t(s_bf[cells:, :], r.w_edge[0]).astype(BF16).reshape(4, W, W)
    back_out = halo_copies(r.back_src, r.back_got, r.back_sem)
    for copy in back_out:
        copy.start()
    r.bias_rows[share : share + 1, :] = jnp.sum(r_sum, axis=0, keepdims=True)
    r.b_flat[: 3 * W, :] = jnp.concatenate(
        [dot(r.ext_t[...], s_bf), dot(r.ext_t[:, :cells], r_bf), r.we_acc[...].T], axis=0
    )
    r.b_flat[3 * W :, :] = jnp.zeros((b_own, W), F32)
    inner = lax.broadcasted_iota(I32, (b_own, W), 0) < share
    for k in range(ng):
        part = r.b_flat[k * share : k * share + b_own, :]
        r.b_src[k] = jnp.where(inner, part, r.bias_rows[...]).astype(BF16)
    b_stage.start()
    r.d_part[...] = (
        r.d_part[...]
        + right_t(r.d_pre_n[...], r.w_node[0])
        + right_t(s_bf[:cells, :], r.w_edge[0])
        + right_t(r_bf, r.w_edge[1])
    )
    for copy in back_out:
        copy.wait_recv()
    returned = jnp.concatenate(
        [jnp.where(present[k], r.back_got[k].astype(F32), 0.0) for k in range(4)], axis=0
    ).astype(BF16)
    r.d_nodes[...] = (r.d_part[...] + dot(r.hot_list[...], returned)).astype(BF16)
    leave(0, r.d_nodes, r.d_nodes_out)
    b_stage.to_column()
    a_stage.to_layer()
    lax.fori_loop(0, half, edge_out, 0)
    first, second = pl.ds(0, half * tile), pl.ds(half * tile, (tiles - half) * tile)
    leave(1, r.d_edges.at[first], r.d_edges_out.at[first])
    row.arrive(r.coarse_all, r.coarse_sem)
    r.node_out[...] = (r.fine[...] + from_coarse(r.coarse_all[...])).astype(BF16)
    leave(2, r.node_out, r.node_out_out)
    b_stage.to_layer()
    lax.fori_loop(half, tiles, edge_out, 0)
    leave(3, r.d_edges.at[second], r.d_edges_out.at[second])
    r.bias_grads[...] = r.b_sum[share : share + 3, :]
    leave(4, r.bias_grads, r.bias_grads_out)
    a_stage.finish()
    r.grads[3 * W :, :] = r.a_all[...].astype(F32)[:, :a_own, :].reshape(6 * W, W)
    late, soon = pl.ds(0, 3 * W), pl.ds(3 * W, 6 * W)
    leave(5, r.grads.at[soon], r.grads_out.at[soon])
    row.sent(r.cot_got, r.cot_sem)
    row.sent(r.fine_got, r.fine_sem)
    row.sent(r.coarse_all, r.coarse_sem)
    row.sent(r.d_coarse_all, r.d_coarse_sem)
    for copy in halo_out + back_out:
        copy.wait_send()
    a_stage.sent()
    layer.sent(r.b_in, r.b_rs_sem)
    column.sent(r.b_z, r.b_z_sem)
    b_stage.finish()
    for k in range(ng):
        r.grads[k * share : (k + 1) * share, :] = r.b_all[k].astype(F32)[:share, :]
    leave(6, r.grads.at[late], r.grads_out.at[late])
    layer.sent(r.b_all, r.b_ag_sem)
    for copy in leaving:
        copy.wait()


def settle(cuts, *refs):
    count = len(cuts)
    held, sems = refs[2 * count : 3 * count], refs[3 * count]
    pieces = []
    for k, parts in enumerate(cuts):
        rows = refs[k].shape[0] // parts
        pieces += [(k, pl.ds(p * rows, rows)) for p in range(parts)]
    gets = [
        pltpu.make_async_copy(refs[k].at[here], held[k].at[here], sems.at[0, n])
        for n, (k, here) in enumerate(pieces)
    ]
    puts = [
        pltpu.make_async_copy(held[k].at[here], refs[count + k].at[here], sems.at[1, n])
        for n, (k, here) in enumerate(pieces)
    ]
    for get in gets:
        get.start()
    for get, put in zip(gets, puts):
        get.wait()
        put.start()
    for put in puts:
        put.wait()


def body(
    dims,
    nodes,
    edge_feat,
    senders,
    receivers,
    send_lists,
    owner,
    edge_live,
    cotangent,
    w_edge,
    w_node,
    w_coarse,
    biases,
):
    nx, ny, cells, edges, tile = dims
    nz = nx // 2
    ng = 2 * ny
    ext = cells + 4 * W
    owned = cells // ny
    a_rows = -(-(6 * W // ng) // 16) * 16
    b_rows = -(-(3 * W // ng + 3) // 16) * 16
    operands = dict(
        nodes=nodes,
        feat=edge_feat,
        snd=senders.reshape(edges // W, W),
        rcv=receivers.reshape(edges // W, W),
        slist=send_lists.reshape(4, W),
        owner=owner.reshape(cells // W, W),
        cot=cotangent,
        w_edge=w_edge,
        w_node=w_node,
        w_coarse=w_coarse,
        bias=biases,
    )
    shapes = (
        jax.ShapeDtypeStruct((cells, W), BF16),
        jax.ShapeDtypeStruct((cells, W), BF16),
        jax.ShapeDtypeStruct((edges, W), BF16),
        jax.ShapeDtypeStruct((9 * W, W), F32),
        jax.ShapeDtypeStruct((3, W), F32),
    )
    scratch = {name: pltpu.VMEM(operands[name].shape, operands[name].dtype) for name in INPUTS}
    scratch |= {name: pltpu.VMEM(s.shape, s.dtype) for name, s in zip(OUTPUTS, shapes)}
    scratch |= dict(
        iota=pltpu.VMEM((BLOCK, max(cells, tile)), BF16),
        ext_t=pltpu.VMEM((W, ext), BF16),
        table_t=pltpu.VMEM((2 * W, (ext + cells) // 2), BF16),
        marks=pltpu.VMEM((edges // tile, (ext + cells) // 2, tile), BF16),
        hot_list=pltpu.VMEM((cells, 4 * W), BF16),
        own_t=pltpu.VMEM((cells // 2, cells), BF16),
        own_n=pltpu.VMEM((cells, cells // 2), BF16),
        own_at=pltpu.VMEM((cells, W), F32),
        own_high=pltpu.VMEM((cells, W), F32),
        pick=pltpu.VMEM((4, W, W), BF16),
        halo=pltpu.VMEM((4, W, W), BF16),
        slopes=pltpu.VMEM((edges // tile, W, tile), F32),
        d_pre=pltpu.VMEM((edges // tile, W, tile), BF16),
        h_acc=pltpu.VMEM((cells // 2, 2 * W), F32),
        s_acc=pltpu.VMEM((ext // 2, 2 * W), F32),
        r_acc=pltpu.VMEM((cells // 2, 2 * W), F32),
        we_acc=pltpu.VMEM((W, W), F32),
        fine=pltpu.VMEM((cells, W), F32),
        node_slope=pltpu.VMEM((cells, W), F32),
        d_part=pltpu.VMEM((cells, W), F32),
        hb=pltpu.VMEM((cells, W), BF16),
        agg=pltpu.VMEM((cells, W), BF16),
        hid=pltpu.VMEM((cells, W), BF16),
        cot_src=pltpu.VMEM((ny, owned, W), BF16),
        cot_got=pltpu.VMEM((ny, owned, W), BF16),
        fine_src=pltpu.VMEM((ny, owned, W), BF16),
        fine_got=pltpu.VMEM((ny, owned, W), BF16),
        coarse_all=pltpu.VMEM((ny, owned, W), BF16),
        d_coarse_all=pltpu.VMEM((ny, owned, W), BF16),
        d_pre_n=pltpu.VMEM((cells, W), BF16),
        back_src=pltpu.VMEM((4, W, W), BF16),
        back_got=pltpu.VMEM((4, W, W), BF16),
        bias_rows=pltpu.VMEM((b_rows, W), F32),
        b_flat=pltpu.VMEM((3 * W + b_rows, W), F32),
        load_sem=pltpu.SemaphoreType.DMA((len(INPUTS),)),
        halo_sem=pltpu.SemaphoreType.DMA((2, 4)),
        back_sem=pltpu.SemaphoreType.DMA((2, 4)),
        cot_sem=pltpu.SemaphoreType.DMA((2,)),
        fine_sem=pltpu.SemaphoreType.DMA((2,)),
        coarse_sem=pltpu.SemaphoreType.DMA((2,)),
        d_coarse_sem=pltpu.SemaphoreType.DMA((2,)),
        out_sem=pltpu.SemaphoreType.DMA((7,)),
    )
    for name, rows in (("a", a_rows), ("b", b_rows)):
        scratch |= {
            name + "_src": pltpu.VMEM((ng, rows, W), BF16),
            name + "_in": pltpu.VMEM((ng, rows, W), BF16),
            name + "_z": pltpu.VMEM((nz, rows, W), BF16),
            name + "_all": pltpu.VMEM((ng, rows, W), BF16),
            name + "_sum": pltpu.VMEM((rows, W), F32),
            name + "_rs_sem": pltpu.SemaphoreType.DMA((2,)),
            name + "_z_sem": pltpu.SemaphoreType.DMA((2,)),
            name + "_ag_sem": pltpu.SemaphoreType.DMA((2,)),
        }
    names = tuple(name + "_in" for name in INPUTS) + ("live",)
    names += tuple(name + "_out" for name in OUTPUTS) + tuple(scratch)
    smem = pl.BlockSpec(memory_space=pltpu.SMEM)
    hbm = pl.BlockSpec(memory_space=pltpu.HBM)
    outs = pl.pallas_call(
        functools.partial(kernel, dims, names),
        out_shape=shapes,
        in_specs=[hbm] * len(INPUTS) + [smem],
        out_specs=(hbm,) * 5,
        scratch_shapes=list(scratch.values()),
        compiler_params=pltpu.CompilerParams(
            collective_id=0, has_side_effects=True, vmem_limit_bytes=61440 * 1024
        ),
        cost_estimate=pl.CostEstimate(
            flops=2 * edges * W * (2 * ext + 4 * cells + 4 * W),
            bytes_accessed=2 * W * (2 * edges + 4 * cells),
            transcendentals=edges * W,
        ),
        name="mesh_step",
    )(*[operands[name] for name in INPUTS], edge_live)
    cuts = (1, 1, 4, 2, 1)
    outs = pl.pallas_call(
        functools.partial(settle, cuts),
        out_shape=shapes,
        in_specs=[hbm] * 5,
        out_specs=(hbm,) * 5,
        scratch_shapes=[pltpu.VMEM(s.shape, s.dtype) for s in shapes]
        + [pltpu.SemaphoreType.DMA((2, sum(cuts)))],
        compiler_params=pltpu.CompilerParams(vmem_limit_bytes=60 * 1024 * 1024),
        name="settle",
    )(*outs)
    node_out, d_nodes, d_edges, grads, bias_grads = outs
    return node_out, d_nodes, d_edges, grads.reshape(9, W, W), bias_grads


def solution(mesh, cells=1024, edges=4096, tile=1024):
    both = ("gx", "gy")
    dims = (mesh.shape["gx"], mesh.shape["gy"], cells, edges, tile)
    in_specs = (
        P(both, None),
        P(both, None),
        P(both),
        P(both),
        P(both, None, None),
        P(both),
        P(both),
        P(both, None),
        P(),
        P(),
        P(),
        P(),
    )
    out_specs = (P(both, None), P(both, None), P(both, None), P(), P())
    return jax.shard_map(
        functools.partial(body, dims),
        mesh=mesh,
        in_specs=in_specs,
        out_specs=out_specs,
        check_vma=False,
    )
```
